32 devices in a mesh: case: 2 (over y), lon: 4 (over z), lat: 2 (over x), sub: 2 (over core).
Axes of the slice: x: 2, y: 2, z: 4, core: 2. Of those that a mesh axis runs over, the one named last changes fastest.
Arguments:
- traj_u: float32 [6, 128, 2048], P('case', ('lat', 'sub'), 'lon'), parts along dimension 0, may hold values from -4 to 4
- traj_v: float32 [6, 128, 2048], P('case', ('lat', 'sub'), 'lon'), parts along dimension 0, may hold values from -4 to 4
- adj_h: float32 [16, 128, 2048], P('case', ('lat', 'sub'), 'lon'), parts along dimension 0, may hold values from -6 to 6
- adj_u: float32 [16, 128, 2048], P('case', ('lat', 'sub'), 'lon'), parts along dimension 0, may hold values from -6 to 6
- adj_v: float32 [16, 128, 2048], P('case', ('lat', 'sub'), 'lon'), parts along dimension 0, may hold values from -6 to 6
- depth: float32 [128, 2048], P(('lat', 'sub'), 'lon'), may hold values from 0.25 to 1
- drag: float32 [128, 2048], P(('lat', 'sub'), 'lon'), may hold values from 0.1 to 1
- land: int32 [128, 2048], P(('lat', 'sub'), 'lon'), may hold values 0 or 1
- wet_u: int32 [6, 128, 2048], P('case', ('lat', 'sub'), 'lon'), parts along dimension 0, may hold values 0 or 1
- wet_v: int32 [6, 128, 2048], P('case', ('lat', 'sub'), 'lon'), parts along dimension 0, may hold values 0 or 1
Outputs:
- out_h: float32 [16, 128, 2048], P('case', ('lat', 'sub'), 'lon'), parts along dimension 0
- out_u: float32 [16, 128, 2048], P('case', ('lat', 'sub'), 'lon'), parts along dimension 0
- out_v: float32 [16, 128, 2048], P('case', ('lat', 'sub'), 'lon'), parts along dimension 0
- out_depth: float32 [16, 128, 2048], P('case', ('lat', 'sub'), 'lon'), parts along dimension 0
- out_drag: float32 [16, 128, 2048], P('case', ('lat', 'sub'), 'lon'), parts along dimension 0
The draws below stay inside these ranges and needn't reach their ends.
There are 2 independent parts, one for each index of `case`. The reference program is written for one: setup_inputs(seed, part) draws one part's arguments, and reference() takes and returns one part's arrays. A program takes and returns all parts, laid end to end along the dimension named above; an argument that names none is the same for every part. Nothing has to cross between parts.
All inputs are finite; a program needn't handle non-finite values. No bound on the sum of `land` or of `wet_u` or of `wet_v` on one device may be relied on, other than what follows from the above.
Results may differ from the reference program's by a relative error of at most 0.00002.
Values sent between devices are 32-bit elements; how exact they have to be, the bound alone decides.
No kernel may reach another device: no remote copies, remote signals or barrier semaphores. Data moves between devices by JAX's collectives and lax.ppermute only.
A program may use at most 64 MiB of HBM per device.

```python
import math
import jax
import jax.numpy as jnp
from jax import lax

NSENS = 8
STEPS = 3
NY = 128
NX = 2048


def set_ends(entries, key, smallest, largest):
    index_at = [jax.random.randint(jax.random.fold_in(key, axis), (), 0, length) for axis, length in enumerate(entries.shape)]
    widest = entries.shape.index(max(entries.shape))
    beside = index_at[:widest] + [(index_at[widest] + 1) % entries.shape[widest]] + index_at[widest + 1:]
    return entries.at[tuple(index_at)].set(smallest).at[tuple(beside)].set(largest)


def shard_levels(rng, dims, pieces, smallest, top_value):
    level, own = 1.0, jax.random.fold_in(rng, 6)
    for position, parts in pieces:
        draws = jnp.exp(jax.random.uniform(jax.random.fold_in(own, position), (parts,), jnp.float32, smallest / len(pieces), top_value / len(pieces)))
        level = level * jnp.repeat(draws, dims[position] // parts).reshape([-1 if axis == position else 1 for axis in range(len(dims))])
    return level


def scatter_about(key, dims, width, reach, split=(), kind=jnp.bfloat16):
    entries = jax.random.normal(key, dims, jnp.float32) * width
    if len(split) > 0:
        entries = shard_levels(key, dims, split, -0.22, 0.18) * entries
    return jnp.clip(entries, min=-reach, max=reach).astype(kind)


def setup_inputs(seed: int = 0, part: int = 0) -> dict:
    seeds = jax.random.split(jax.random.key(seed), 11)
    part_keys = jax.random.split(jax.random.fold_in(seeds[10], part), 11)
    traj_u = scatter_about(part_keys[0], (STEPS, NY, NX), 1.0, 4.0, ((1, 4), (2, 4)), jnp.float32)
    traj_v = scatter_about(part_keys[1], (STEPS, NY, NX), 1.0, 4.0, ((1, 4), (2, 4)), jnp.float32)
    adj_h = scatter_about(part_keys[2], (NSENS, NY, NX), 1.0, 6.0, ((1, 4), (2, 4)), jnp.float32)
    adj_u = scatter_about(part_keys[3], (NSENS, NY, NX), 1.0, 6.0, ((1, 4), (2, 4)), jnp.float32)
    adj_v = scatter_about(part_keys[4], (NSENS, NY, NX), 1.0, 6.0, ((1, 4), (2, 4)), jnp.float32)
    depth = jnp.clip(jnp.exp(math.log(1.0) - 1.3862944 * jax.random.uniform(seeds[5], (NY, NX), jnp.float32) ** shard_levels(seeds[5], (NY, NX), ((0, 4), (1, 4)), -0.2, 0.2)), 0.25, 1.0)
    drag = jnp.clip(jnp.exp(math.log(1.0) - 2.3025851 * jax.random.uniform(seeds[6], (NY, NX), jnp.float32) ** shard_levels(seeds[6], (NY, NX), ((0, 4), (1, 4)), -0.2, 0.2)), 0.1, 1.0)
    land = set_ends((jax.random.randint(seeds[7], (NY, NX), 0, 16) < 15).astype(jnp.int32), jax.random.fold_in(seeds[7], 1), 0, 1)
    wet_u = set_ends((jax.random.randint(part_keys[8], (STEPS, NY, NX), 0, 8) < 7).astype(jnp.int32), jax.random.fold_in(part_keys[8], 1), 0, 1)
    wet_v = set_ends((jax.random.randint(part_keys[9], (STEPS, NY, NX), 0, 8) < 7).astype(jnp.int32), jax.random.fold_in(part_keys[9], 1), 0, 1)
    return dict(traj_u=traj_u, traj_v=traj_v, adj_h=adj_h, adj_u=adj_u, adj_v=adj_v, depth=depth, drag=drag, land=land, wet_u=wet_u, wet_v=wet_v)


time_step = 0.5
gravity = 1.0
speed_floor = 0.01

def face_depths(depth):
    east_depth = jnp.roll(depth, -1, axis=1)
    north_depth = jnp.concatenate([depth[1:], depth[-1:, ::-1]], axis=0)
    return (0.5 * (depth + east_depth), 0.5 * (depth + north_depth))

def model_step(height, vel_u, vel_v, depth, drag, land_f, mask_u, mask_v):
    depth_u, depth_v = face_depths(depth)
    flux_u = depth_u * vel_u
    flux_v = depth_v * vel_v
    west_flux = jnp.roll(flux_u, 1, axis=1)
    south_flux = jnp.concatenate([jnp.zeros_like(flux_v[:1]), flux_v[:-1]], axis=0)
    fold_flux = jnp.concatenate([jnp.zeros_like(flux_v[:-1]), flux_v[-1:, ::-1]], axis=0)
    height_new = height - time_step * land_f * (flux_u - west_flux + flux_v - south_flux - fold_flux)
    east_height = jnp.roll(height_new, -1, axis=1)
    north_height = jnp.concatenate([height_new[1:], height_new[-1:, ::-1]], axis=0)
    drag_u = drag * vel_u * jnp.sqrt(vel_u * vel_u + speed_floor) / depth_u
    drag_v = drag * vel_v * jnp.sqrt(vel_v * vel_v + speed_floor) / depth_v
    u_new = mask_u * (vel_u - time_step * gravity * (east_height - height_new) - time_step * drag_u)
    v_new = mask_v * (vel_v - time_step * gravity * (north_height - height_new) - time_step * drag_v)
    return (height_new, u_new, v_new)

def reference(traj_u, traj_v, adj_h, adj_u, adj_v, depth, drag, land, wet_u, wet_v):
    land_f = land.astype(jnp.float32)

    def one_case(cotangents):
        bar_h, bar_u, bar_v = cotangents
        grad_depth = jnp.zeros_like(depth)
        grad_drag = jnp.zeros_like(drag)
        for step_index in range(STEPS - 1, -1, -1):
            mask_u = wet_u[step_index].astype(jnp.float32)
            mask_v = wet_v[step_index].astype(jnp.float32)

            def advance(height, vel_u, vel_v, depth_in, drag_in):
                return model_step(height, vel_u, vel_v, depth_in, drag_in, land_f, mask_u, mask_v)
            _, pullback = jax.vjp(advance, jnp.zeros_like(bar_h), traj_u[step_index], traj_v[step_index], depth, drag)
            bar_h, bar_u, bar_v, part_depth, part_drag = pullback((bar_h, bar_u, bar_v))
            grad_depth = grad_depth + part_depth
            grad_drag = grad_drag + part_drag
        return (bar_h, bar_u, bar_v, grad_depth, grad_drag)
    out_h, out_u, out_v, out_depth, out_drag = lax.map(one_case, (adj_h, adj_u, adj_v))
    return (out_h, out_u, out_v, out_depth, out_drag)
```

```python
import jax
import jax.numpy as jnp
from jax import lax
from jax.experimental import pallas as pl
from jax.experimental.pallas import tpu as pltpu
from jax.sharding import PartitionSpec as P

time_step = 0.5
gravity = 1.0
speed_floor = 0.01

ROWS = ("lat", "sub")
GRID = ("lon", "lat", "sub")
TILE = 8
LANES = 128
DEEP = 4
STATICS = 16
VMEM_LIMIT = 48 * 1024 * 1024


def iota(shape, axis):
    return lax.broadcasted_iota(jnp.int32, shape, axis)


def place():
    row = lax.axis_index("lat") * lax.axis_size("sub") + lax.axis_index("sub")
    last = lax.axis_size("lat") * lax.axis_size("sub") - 1
    return row % 2 == 0, row == last


def kind_of(field, count):
    if field < 3 * count:
        kind = field % 3
        return kind, kind > 0
    static = field - 3 * count
    if static < 12:
        return 1 + (static // 3) % 2, static < 6
    return (0, 1, 2, 0)[static - 12], False


def field_list(adj, rest):
    adj_h, adj_u, adj_v = adj
    traj_u, traj_v, wet_u, wet_v, depth, drag, land = rest
    loads = []
    for sens in range(adj_h.shape[0]):
        for ref in (adj_h, adj_u, adj_v):
            loads.append(lambda ref=ref, sens=sens: ref[sens])
    for ref in (traj_u, traj_v, wet_u, wet_v):
        for step in range(3):
            loads.append(lambda ref=ref, step=step: ref[step].astype(jnp.float32))
    for ref in (depth, drag, drag, land):
        loads.append(lambda ref=ref: ref[...].astype(jnp.float32))
    return loads


def lane_tiles(value):
    return [value[:, at : at + LANES] for at in range(0, value.shape[1], LANES)]


def pack_rows(*refs):
    bottom = field_list(refs[0:3], refs[3:10])
    top = field_list(refs[10:13], refs[13:20])
    one, two = refs[20:22]
    count = refs[0].shape[0]
    even, at_top = place()
    width = refs[0].shape[2]
    lower = iota((TILE, width), 0) < DEEP

    def pair(loads, index, shift_first):
        first, second = loads[index](), loads[index + 1]()
        if shift_first:
            return jnp.where(lower, pltpu.roll(first, DEEP, 0), second)
        return jnp.where(lower, first, pltpu.roll(second, DEEP, 0))

    for tile in range(one.shape[0]):
        from_bottom = pair(bottom, 2 * tile, False)
        from_top = pair(top, 2 * tile, True)
        one[tile] = jnp.where(even, from_top, from_bottom)
        two[tile] = jnp.where(even, from_bottom, from_top)

    @pl.when(at_top)
    def _():
        row = iota((TILE, LANES), 0)
        lane = LANES - 1 - iota((TILE, LANES), 1)
        backward = (2 * TILE - 1 - row) % TILE
        backward_v = (row < 3) * (6 - row) + (row == 3) * 7 + (row > 3) * row
        sign = jnp.where(row == 3, 1.0, -1.0)

        def mirrored(field):
            kind, turned = kind_of(field, count)
            value = top[field]()
            pieces = []
            for piece in lane_tiles(value)[::-1]:
                piece = jnp.take_along_axis(piece, lane, axis=1)
                piece = jnp.take_along_axis(piece, backward_v if kind == 2 else backward, axis=0)
                if turned:
                    piece = piece * sign
                pieces.append(piece)
            return jnp.concatenate(pieces, axis=1)

        for tile in range(one.shape[0]):
            first, second = mirrored(2 * tile), mirrored(2 * tile + 1)
            two[tile] = jnp.where(lower, first, pltpu.roll(second, DEEP, 0))


def group_lanes(field):
    return field // 32, DEEP * (field % 32)


def pack_columns_own(*refs):
    west = field_list(refs[0:3], refs[3:10])
    east = field_list(refs[10:13], refs[13:20])
    to_west, to_east = refs[20:22]
    rows = refs[0].shape[1]
    lane = iota((rows, LANES), 1)
    for loads, target, origin in ((west, to_west, 0), (east, to_east, LANES - DEEP)):
        packed = [None, None]
        for field, load in enumerate(loads):
            side, at = group_lanes(field)
            value = load()
            shift = (at - origin) % LANES
            if shift:
                value = pltpu.roll(value, shift, 1)
            packed[side] = value if packed[side] is None else jnp.where(lane >= at, value, packed[side])
        for side in range(2):
            target[:, side * LANES : (side + 1) * LANES] = packed[side]


def merge_rows(one, two, own_west, own_east, halo, halo_static, to_west, to_east):
    even, _ = place()
    width = one.shape[2]
    rows = own_west.shape[0]
    lower = iota((TILE, width), 0) < DEEP
    lane = iota((TILE, LANES), 1)
    to_west[:rows, :] = own_west[...]
    to_east[:rows, :] = own_east[...]
    packed = [[None, None], [None, None]]
    for tile in range(one.shape[0]):
        north = jnp.where(even, one[tile], two[tile])
        south = jnp.where(even, two[tile], one[tile])
        first = jnp.where(lower, north, pltpu.roll(south, DEEP, 0))
        second = jnp.where(lower, pltpu.roll(north, DEEP, 0), south)
        for field, value in ((2 * tile, first), (2 * tile + 1, second)):
            if field < halo.shape[0]:
                halo[field] = value
            else:
                halo_static[field - halo.shape[0]] = value
            side, at = group_lanes(field)
            pieces = lane_tiles(value)
            for way, piece, origin in ((0, pieces[0], 0), (1, pieces[-1], LANES - DEEP)):
                shift = (at - origin) % LANES
                if shift:
                    piece = pltpu.roll(piece, shift, 1)
                held = packed[way][side]
                packed[way][side] = piece if held is None else jnp.where(lane >= at, piece, held)
    for way, target in ((0, to_west), (1, to_east)):
        for side in range(2):
            target[rows:, side * LANES : (side + 1) * LANES] = packed[way][side]


def steps_kernel(
    adj_h, adj_u, adj_v, traj_u, traj_v, wet_u, wet_v, depth, drag, land,
    halo, halo_static, from_west, from_east,
    out_h, out_u, out_v, out_depth, out_drag,
    mask_u_s, mask_v_s, keep_u_s, keep_v_s, drag_u_s, drag_v_s, vel_u_s, vel_v_s,
    depth_u_s, depth_v_s, ratio_u_s, ratio_v_s, land_s,
):
    _, at_top = place()
    rows, width = adj_h.shape[1:]
    count = rows // TILE + 1
    last = count - 1
    wide = width + LANES
    row = iota((TILE, wide), 0)
    lane = iota((TILE, LANES), 1)
    sens = pl.program_id(0)

    def corner(field_side, at, tile):
        here = slice(tile * TILE, (tile + 1) * TILE)
        cols = slice(field_side * LANES, (field_side + 1) * LANES)
        east = pltpu.roll(from_east[here, cols], (LANES - at) % LANES, 1)
        west = pltpu.roll(from_west[here, cols], (2 * LANES - DEEP - at) % LANES, 1)
        return jnp.where(lane < LANES // 2, east, west)

    def extended(own, halo_rows, side, at, kind):
        out = []
        for tile in range(count):
            body = own(tile) if tile < last else halo_rows()
            value = jnp.concatenate([body, corner(side, at, tile)], axis=1)
            if tile == last and kind == 1:
                value = jnp.where(at_top & (row < DEEP), pltpu.roll(value, wide - 1, 1), value)
            out.append(value)
        return out

    def east_of(value):
        return pltpu.roll(value, wide - 1, 1)

    def west_of(value):
        return pltpu.roll(value, 1, 1)

    def south_of(values, tile):
        return jnp.where(row == 0, pltpu.roll(values[tile - 1], 1, 0), pltpu.roll(values[tile], 1, 0))

    def north_of(values, tile):
        return jnp.where(
            row == TILE - 1,
            pltpu.roll(values[(tile + 1) % count], TILE - 1, 0),
            pltpu.roll(values[tile], TILE - 1, 0),
        )

    def rows_of(tile):
        return slice(tile * TILE, (tile + 1) * TILE)

    @pl.when(sens == 0)
    def _():
        first_static = 3 * adj_count

        def static(index, ref):
            side, at = group_lanes(first_static + index)
            kind, _ = kind_of(first_static + index, adj_count)
            return extended(
                lambda tile: ref[rows_of(tile), :].astype(jnp.float32),
                lambda: halo_static[index],
                side,
                at,
                kind,
            )

        cells = [jnp.where(value > 0.0, value, 1.0) for value in static(12, depth)]
        drag_u = static(13, drag)
        drag_v = static(14, drag)
        sea = static(15, land)
        face_u = [0.5 * (value + east_of(value)) for value in cells]
        face_v = [0.5 * (cells[tile] + north_of(cells, tile)) for tile in range(count)]
        face_v[last] = jnp.where(row == 3, pltpu.roll(face_v[last - 1], DEEP, 0), face_v[last])
        for tile in range(count):
            here = rows_of(tile)
            land_s[here, :] = 0.5 * sea[tile]
            inverse_u = 1.0 / face_u[tile]
            inverse_v = 1.0 / face_v[tile]
            depth_u_s[here, :] = face_u[tile]
            depth_v_s[here, :] = face_v[tile]
            ratio_u_s[here, :] = -drag_u[tile] * inverse_u
            ratio_v_s[here, :] = -drag_v[tile] * inverse_v
        for step in range(3):
            for vel_index, wet_index, vel_ref, wet_ref, depth_s, ratio_s, mask_s, keep_s, drag_s, vel_s in (
                (step, 6 + step, traj_u, wet_u, depth_u_s, ratio_u_s, mask_u_s, keep_u_s, drag_u_s, vel_u_s),
                (3 + step, 9 + step, traj_v, wet_v, depth_v_s, ratio_v_s, mask_v_s, keep_v_s, drag_v_s, vel_v_s),
            ):
                vel = static(vel_index, vel_ref.at[step])
                wet = static(wet_index, wet_ref.at[step])
                for tile in range(count):
                    here = rows_of(tile)
                    square = vel[tile] * vel[tile]
                    speed = jnp.sqrt(square + speed_floor)
                    mask_s[step, here, :] = 0.5 * wet[tile]
                    keep_s[step, here, :] = 2.0 + ratio_s[here, :] * (speed + square / speed)
                    drag_s[step, here, :] = -vel[tile] * speed / depth_s[here, :]
                    vel_s[step, here, :] = vel[tile]

    def dynamic(kind, ref):
        return extended(
            lambda tile: ref[0, rows_of(tile), :],
            lambda: halo[kind],
            0,
            DEEP * (3 * sens + kind),
            kind,
        )

    bar_h, bar_u, bar_v = dynamic(0, adj_h), dynamic(1, adj_u), dynamic(2, adj_v)
    sum_xu, sum_xv, sum_u, sum_v = ([None] * count for _ in range(4))

    def add_to(sums, tile, value):
        sums[tile] = value if sums[tile] is None else sums[tile] + value

    for step in (2, 1, 0):
        flow_u, flow_v, flow_v_face, sea = [], [], [], []
        for tile in range(count):
            here = rows_of(tile)
            flow_u.append(mask_u_s[step, here, :] * bar_u[tile])
            flow_v.append(mask_v_s[step, here, :] * bar_v[tile])
        flow_v_face = list(flow_v)
        flow_v_face[last - 1] = flow_v[last - 1] - jnp.where(
            at_top & (row == TILE - 1), pltpu.roll(flow_v[last], DEEP, 0), 0.0
        )
        for tile in range(count):
            here = rows_of(tile)
            bar_h[tile] = (
                bar_h[tile]
                + (flow_u[tile] - west_of(flow_u[tile]))
                + (flow_v_face[tile] - south_of(flow_v_face, tile))
            )
            sea.append(land_s[here, :] * bar_h[tile])
        for tile in range(count):
            here = rows_of(tile)
            turn_u = east_of(sea[tile]) - sea[tile]
            turn_v = north_of(sea, tile) - sea[tile]
            if tile == last:
                turn_v = jnp.where(row == 3, -pltpu.roll(fold_turn, DEEP, 0), turn_v)
            fold_turn = turn_v
            bar_u[tile] = keep_u_s[step, here, :] * flow_u[tile] + depth_u_s[here, :] * turn_u
            bar_v[tile] = keep_v_s[step, here, :] * flow_v[tile] + depth_v_s[here, :] * turn_v
            add_to(sum_xu, tile, drag_u_s[step, here, :] * flow_u[tile])
            add_to(sum_xv, tile, drag_v_s[step, here, :] * flow_v[tile])
            add_to(sum_u, tile, vel_u_s[step, here, :] * turn_u)
            add_to(sum_v, tile, vel_v_s[step, here, :] * turn_v)

    face_v = [
        ratio_v_s[rows_of(tile), :] * sum_xv[tile] + sum_v[tile] for tile in range(count)
    ]
    for tile in range(last):
        here = rows_of(tile)
        face_u = ratio_u_s[here, :] * sum_xu[tile] + sum_u[tile]
        total = face_u + west_of(face_u) + face_v[tile] + south_of(face_v, tile)
        if tile == last - 1:
            total = total + jnp.where(
                at_top & (row == TILE - 1), pltpu.roll(face_v[last], DEEP, 0), 0.0
            )
        out_h[0, here, :] = bar_h[tile][:, :width]
        out_u[0, here, :] = bar_u[tile][:, :width]
        out_v[0, here, :] = bar_v[tile][:, :width]
        out_depth[0, here, :] = 0.5 * total[:, :width]
        out_drag[0, here, :] = (sum_xu[tile] + sum_xv[tile])[:, :width]


adj_count = 8


def on_device(traj_u, traj_v, adj_h, adj_u, adj_v, depth, drag, land, wet_u, wet_v):
    count, rows, width = adj_h.shape
    steps = traj_u.shape[0]
    fields = 3 * count + STATICS
    args = (adj_h, adj_u, adj_v, traj_u, traj_v, wet_u, wet_v, depth, drag, land)

    def blocks(shape, where):
        specs = []
        for arg in args:
            specs.append(pl.BlockSpec(arg.shape[:-2] + shape, (lambda n: lambda *_: (0,) * n + where)(arg.ndim - 2)))
        return specs

    params = pltpu.CompilerParams(vmem_limit_bytes=VMEM_LIMIT)
    row_pack = jax.ShapeDtypeStruct((fields // 2, TILE, width), jnp.float32)
    one, two = pl.pallas_call(
        pack_rows,
        grid=(1,),
        in_specs=blocks((TILE, width), (0, 0)) + blocks((TILE, width), (rows // TILE - 1, 0)),
        out_specs=[pl.BlockSpec(row_pack.shape, lambda *_: (0, 0, 0))] * 2,
        out_shape=[row_pack] * 2,
        compiler_params=params,
        name="pack_rows",
    )(*args, *args)

    lons, lats, subs = (lax.axis_size(axis) for axis in GRID)
    total_rows = lats * subs

    def device(lon, row):
        return lon * total_rows + row

    one = lax.ppermute(one, "sub", [(core, core ^ 1) for core in range(subs)])
    route = []
    for lon in range(lons):
        for row in range(1, total_rows - 1, 2):
            route += [(device(lon, row), device(lon, row + 1)), (device(lon, row + 1), device(lon, row))]
        route.append((device(lon, total_rows - 1), device(lons - 1 - lon, total_rows - 1)))
    two = lax.ppermute(two, GRID, route)

    own_pack = jax.ShapeDtypeStruct((rows, 2 * LANES), jnp.float32)
    own_west, own_east = pl.pallas_call(
        pack_columns_own,
        grid=(1,),
        in_specs=blocks((rows, LANES), (0, 0)) + blocks((rows, LANES), (0, width // LANES - 1)),
        out_specs=[pl.BlockSpec(own_pack.shape, lambda *_: (0, 0))] * 2,
        out_shape=[own_pack] * 2,
        compiler_params=params,
        name="pack_columns",
    )(*args, *args)

    full_pack = jax.ShapeDtypeStruct((rows + TILE, 2 * LANES), jnp.float32)
    halo, halo_static, to_west, to_east = pl.pallas_call(
        merge_rows,
        out_shape=[
            jax.ShapeDtypeStruct((3 * count, TILE, width), jnp.float32),
            jax.ShapeDtypeStruct((STATICS, TILE, width), jnp.float32),
            full_pack,
            full_pack,
        ],
        compiler_params=params,
        name="merge_rows",
    )(one, two, own_west, own_east)
    from_east = lax.ppermute(to_west, "lon", [(lon, (lon - 1) % lons) for lon in range(lons)])
    from_west = lax.ppermute(to_east, "lon", [(lon, (lon + 1) % lons) for lon in range(lons)])

    def whole(shape):
        return pl.BlockSpec(shape, lambda sens: (0,) * len(shape))

    block = pl.BlockSpec((1, rows, width), lambda sens: (sens, 0, 0))
    out = jax.ShapeDtypeStruct(adj_h.shape, jnp.float32)
    ext = (rows + TILE, width + LANES)
    return pl.pallas_call(
        steps_kernel,
        grid=(count,),
        in_specs=[block] * 3
        + [whole(arg.shape) for arg in args[3:]]
        + [
            pl.BlockSpec((3, TILE, width), lambda sens: (sens, 0, 0)),
            pl.BlockSpec((STATICS, TILE, width), lambda sens: (0, 0, 0)),
            whole(full_pack.shape),
            whole(full_pack.shape),
        ],
        out_specs=[block] * 5,
        out_shape=[out] * 5,
        scratch_shapes=[pltpu.VMEM((steps,) + ext, jnp.float32)] * 8 + [pltpu.VMEM(ext, jnp.float32)] * 5,
        compiler_params=params,
        name="reverse_steps",
    )(*args, halo, halo_static, from_west, from_east)


def solution(mesh):
    state = P("case", ROWS, "lon")
    fixed = P(ROWS, "lon")
    return jax.shard_map(
        on_device,
        mesh=mesh,
        in_specs=(state,) * 5 + (fixed,) * 3 + (state,) * 2,
        out_specs=(state,) * 5,
        check_vma=False,
    )
```

```python
import functools

import jax
import jax.numpy as jnp
from jax import lax
from jax.experimental import pallas as pl
from jax.experimental.pallas import tpu as pltpu
from jax.sharding import PartitionSpec as P

time_step = 0.5
gravity = 1.0
speed_floor = 0.01

ROWS = ("lat", "sub")
GRID = ("lon", "lat", "sub")
TILE = 8
LANES = 128
DEEP = 4
VMEM_LIMIT = 48 * 1024 * 1024


def iota(shape, axis):
    return lax.broadcasted_iota(jnp.int32, shape, axis)


def place():
    row = lax.axis_index("lat") * lax.axis_size("sub") + lax.axis_index("sub")
    last = lax.axis_size("lat") * lax.axis_size("sub") - 1
    return row % 2 == 0, row == last


STATE_SLOTS = (3, 3, 4)
SHARED = (
    (("traj_v", 2), 2, 3, True),
    (("traj_v", 1), 2, 2, True),
    (("traj_v", 0), 2, 1, True),
    (("traj_u", 2), 1, 2, True),
    (("traj_u", 1), 1, 1, True),
    (("wet_v", 1), 2, 3, False),
    (("wet_v", 0), 2, 2, False),
    (("wet_u", 1), 1, 2, False),
    (("wet_u", 0), 1, 1, False),
    (("depth", None), 0, 3, False),
    (("drag", None), 3, 3, False),
    (("land", None), 0, 3, False),
)
NAMES = ("adj_h", "adj_u", "adj_v", "traj_u", "traj_v", "wet_u", "wet_v", "depth", "drag", "land")
TILES = tuple(entry[0] for entry in SHARED[:10]) + (("drag", 1), ("drag", 2), ("land", None), ("traj_u", 0))


def load(refs, name, step):
    value = refs[name][...] if step is None or name == "drag" else refs[name][step]
    return value.astype(jnp.float32)


def message_rows(count):
    rows = sum(STATE_SLOTS) * count + sum(entry[2] for entry in SHARED)
    return -(-rows // TILE) * TILE


def row_plan(count):
    plan, at = [], 0
    for sens in range(count):
        for kind in range(3):
            plan.append(((NAMES[kind], sens), kind, kind > 0, at, STATE_SLOTS[kind]))
            at += STATE_SLOTS[kind]
    for key, kind, slots, turned in SHARED:
        plan.append((key, kind, turned, at, slots))
        at += slots
    return plan


def lane_tiles(value):
    return [value[:, at : at + LANES] for at in range(0, value.shape[1], LANES)]


def masked(refs, key):
    name, step = key
    value = load(refs, name, step)
    if name == "adj_u":
        value = value * load(refs, "wet_u", 2)
    if name == "adj_v":
        value = value * load(refs, "wet_v", 2)
    return value


def pack_rows(*refs):
    arrays = dict(zip(NAMES, refs[:10]))
    one, two = refs[10:12]
    bottom = dict(zip(NAMES, refs[12:22]))
    top = dict(zip(NAMES, refs[22:32]))
    sems = refs[32]
    count, rows, width = arrays["adj_h"].shape
    even, at_top = place()
    copies = {}
    order = ("wet_u", "wet_v", "adj_h", "adj_u", "adj_v", "traj_u", "traj_v", "depth", "drag", "land")
    for number, name in enumerate(order):
        array = arrays[name]
        lead = (slice(None),) * (array.ndim - 2)
        pair = []
        for side, (held, first) in enumerate(((bottom, 0), (top, rows - TILE))):
            pair.append(
                pltpu.make_async_copy(array.at[lead + (pl.ds(first, TILE),)], held[name], sems.at[number, side])
            )
        for copy in pair:
            copy.start()
        copies[name] = pair
    for name in order:
        for copy in copies[name]:
            copy.wait()

    plan = row_plan(count)
    for key, kind, turned, at, slots in plan:
        low = masked(bottom, key)[:slots]
        high = masked(top, key)[TILE - slots :]
        here = slice(at, at + slots)
        one[here, :] = jnp.where(even, high, low)
        two[here, :] = jnp.where(even, low, high)

    @pl.when(at_top)
    def _():
        row = iota((TILE, LANES), 0)
        lane = LANES - 1 - iota((TILE, LANES), 1)
        for key, kind, turned, at, slots in plan:
            value = masked(top, key)
            sources = [TILE - 1 - slot for slot in range(slots)]
            if kind == 2:
                sources = [TILE - 2 - slot for slot in range(slots - 1)] + [TILE - 1]
            order = jnp.zeros((TILE, LANES), jnp.int32)
            for slot, source in enumerate(sources):
                order = jnp.where(row == slot, source, order)
            pieces = []
            for piece in lane_tiles(value)[::-1]:
                piece = jnp.take_along_axis(piece, lane, axis=1)
                piece = jnp.take_along_axis(piece, order, axis=0)
                if turned:
                    piece = jnp.where(row == slots - 1, piece, -piece) if kind == 2 else -piece
                pieces.append(piece)
            two[at : at + slots, :] = jnp.concatenate(pieces, axis=1)[:slots]


def group_lanes(field):
    return field // 32, DEEP * (field % 32)


def column_fields(count):
    return [(NAMES[kind], sens) for sens in range(count) for kind in range(3)] + list(TILES)


def pack_columns_own(*refs):
    arrays = dict(zip(NAMES, refs[:10]))
    to_west, to_east = refs[10:12]
    west = dict(zip(NAMES, refs[12:22]))
    east = dict(zip(NAMES, refs[22:32]))
    sems = refs[32]
    count, rows, width = arrays["adj_h"].shape
    copies = []
    for number, name in enumerate(NAMES):
        array = arrays[name]
        lead = (slice(None),) * (array.ndim - 1)
        for side, (held, first) in enumerate(((west, 0), (east, width - LANES))):
            copies.append(
                pltpu.make_async_copy(array.at[lead + (pl.ds(first, LANES),)], held[name], sems.at[number, side])
            )
    for copy in copies:
        copy.start()
    for copy in copies:
        copy.wait()
    lane = iota((rows, LANES), 1)
    for held, target, origin in ((west, to_west, 0), (east, to_east, LANES - DEEP)):
        packed = [None, None]
        for field, key in enumerate(column_fields(count)):
            side, at = group_lanes(field)
            value = masked(held, key)
            shift = (at - origin) % LANES
            if shift:
                value = pltpu.roll(value, shift, 1)
            packed[side] = value if packed[side] is None else jnp.where(lane >= at, value, packed[side])
        for side in range(2):
            target[:, side * LANES : (side + 1) * LANES] = packed[side]


def merge_rows(one, two, own_west, own_east, halo, halo_static, to_west, to_east):
    even, at_top = place()
    width = one.shape[1]
    rows = own_west.shape[0]
    count = halo.shape[0] // 3
    lane = iota((TILE, LANES), 1)
    to_west[:rows, :] = own_west[...]
    to_east[:rows, :] = own_east[...]
    packed = [[None, None], [None, None]]
    field = 0
    for key, kind, turned, at, slots in row_plan(count):
        here = slice(at, at + slots)
        north = jnp.where(even, one[here, :], two[here, :])
        south = jnp.where(even, two[here, :], one[here, :])
        blank = jnp.zeros((DEEP - slots, width), jnp.float32)
        gap = [blank] if slots < DEEP else []
        plain = jnp.concatenate([north] + gap + gap + [south], axis=0)
        values = [plain]
        if kind >= 2 and slots < DEEP:
            fold = ([north[:-1]] if slots > 1 else []) + gap + [north[-1:]] + gap + [south]
            if kind == 3:
                fold = [north[1:], blank, north[:1]] + gap + [south]
                values.append(jnp.where(at_top, jnp.concatenate(fold, axis=0), plain))
            else:
                values = [jnp.where(at_top, jnp.concatenate(fold, axis=0), plain)]
        for value in values:
            if field < halo.shape[0]:
                halo[field] = value
            else:
                halo_static[field - halo.shape[0]] = value
            side, start = group_lanes(field)
            pieces = lane_tiles(value)
            for way, piece, origin in ((0, pieces[0], 0), (1, pieces[-1], LANES - DEEP)):
                shift = (start - origin) % LANES
                if shift:
                    piece = pltpu.roll(piece, shift, 1)
                held = packed[way][side]
                packed[way][side] = piece if held is None else jnp.where(lane >= start, piece, held)
            field += 1
    halo_static[field - halo.shape[0]] = jnp.zeros((TILE, width), jnp.float32)
    for way, target in ((0, to_west), (1, to_east)):
        for side in range(2):
            target[rows:, side * LANES : (side + 1) * LANES] = packed[way][side]


def steps_kernel(
    adj_count, adj_h, adj_u, adj_v, traj_u, traj_v, wet_u, wet_v, depth, drag, land,
    halo, halo_static, from_west, from_east,
    out_h, out_u, out_v, out_depth, out_drag,
    mask_u_s, mask_v_s, keep_u_s, keep_v_s, drag_u_s, drag_v_s, vel_u_s, vel_v_s,
    depth_u_s, depth_v_s, ratio_u_s, ratio_v_s, land_s,
):
    _, at_top = place()
    rows, width = adj_h.shape[1:]
    count = rows // TILE + 1
    last = count - 1
    wide = width + LANES
    row = iota((TILE, wide), 0)
    lane = iota((TILE, LANES), 1)
    sens = pl.program_id(0)
    halo_count = 3 * adj_count

    def corner(side, at, tile):
        here = slice(tile * TILE, (tile + 1) * TILE)
        cols = slice(side * LANES, (side + 1) * LANES)
        east = pltpu.roll(from_east[here, cols], (LANES - at) % LANES, 1)
        west = pltpu.roll(from_west[here, cols], (2 * LANES - DEEP - at) % LANES, 1)
        return jnp.where(lane < LANES // 2, east, west)

    def extended(own, halo_rows, corner_of, kind):
        out = []
        for tile in range(count):
            body = own(tile) if tile < last else halo_rows()
            value = jnp.concatenate([body, corner_of(tile)], axis=1)
            if tile == last and kind == 1:
                value = jnp.where(at_top & (row < DEEP), pltpu.roll(value, wide - 1, 1), value)
            out.append(value)
        return out

    def east_of(value):
        return pltpu.roll(value, wide - 1, 1)

    def west_of(value):
        return pltpu.roll(value, 1, 1)

    def south_of(values, tile):
        return jnp.where(row == 0, pltpu.roll(values[tile - 1], 1, 0), pltpu.roll(values[tile], 1, 0))

    def north_of(values, tile):
        return jnp.where(
            row == TILE - 1,
            pltpu.roll(values[(tile + 1) % count], TILE - 1, 0),
            pltpu.roll(values[tile], TILE - 1, 0),
        )

    def rows_of(tile):
        return slice(tile * TILE, (tile + 1) * TILE)

    @pl.when(sens == 0)
    def _():
        def static(key, ref, kind):
            own = lambda tile: ref[rows_of(tile), :].astype(jnp.float32)
            if key not in TILES:
                ones = lambda columns: jnp.ones((TILE, columns), jnp.float32)
                return extended(own, lambda: ones(width), lambda tile: ones(LANES), 0)
            index = TILES.index(key)
            side, at = group_lanes(halo_count + index)
            return extended(own, lambda: halo_static[index], lambda tile: corner(side, at, tile), kind)

        cells = [jnp.where(value > 0.0, value, 1.0) for value in static(("depth", None), depth, 0)]
        drag_u = static(("drag", 1), drag, 1)
        drag_v = static(("drag", 2), drag, 2)
        sea = static(("land", None), land, 0)
        face_u = [0.5 * (value + east_of(value)) for value in cells]
        face_v = [0.5 * (cells[tile] + north_of(cells, tile)) for tile in range(count)]
        face_v[last] = jnp.where(row == 3, pltpu.roll(face_v[last - 1], DEEP, 0), face_v[last])
        for tile in range(count):
            here = rows_of(tile)
            land_s[here, :] = 0.5 * sea[tile]
            inverse_u = 1.0 / face_u[tile]
            inverse_v = 1.0 / face_v[tile]
            depth_u_s[here, :] = face_u[tile]
            depth_v_s[here, :] = face_v[tile]
            ratio_u_s[here, :] = -drag_u[tile] * inverse_u
            ratio_v_s[here, :] = -drag_v[tile] * inverse_v
        for step in range(3):
            for kind, way, vel_ref, wet_ref, depth_s, ratio_s, mask_s, keep_s, drag_s, vel_s in (
                (1, "u", traj_u, wet_u, depth_u_s, ratio_u_s, mask_u_s, keep_u_s, drag_u_s, vel_u_s),
                (2, "v", traj_v, wet_v, depth_v_s, ratio_v_s, mask_v_s, keep_v_s, drag_v_s, vel_v_s),
            ):
                vel = static(("traj_" + way, step), vel_ref.at[step], kind)
                wet = static(("wet_" + way, step), wet_ref.at[step], kind)
                for tile in range(count):
                    here = rows_of(tile)
                    square = vel[tile] * vel[tile]
                    speed = jnp.sqrt(square + speed_floor)
                    mask_s[step, here, :] = 0.5 * wet[tile]
                    keep_s[step, here, :] = 2.0 + ratio_s[here, :] * (speed + square / speed)
                    drag_s[step, here, :] = -vel[tile] * speed / depth_s[here, :]
                    vel_s[step, here, :] = vel[tile]

    def dynamic(kind, ref):
        at = DEEP * (3 * sens + kind)
        return extended(
            lambda tile: ref[0, rows_of(tile), :],
            lambda: halo[kind],
            lambda tile: corner(0, at, tile),
            kind,
        )

    bar_h, bar_u, bar_v = dynamic(0, adj_h), dynamic(1, adj_u), dynamic(2, adj_v)
    sum_xu, sum_xv, sum_u, sum_v = ([None] * count for _ in range(4))

    def add_to(sums, tile, value):
        sums[tile] = value if sums[tile] is None else sums[tile] + value

    for step in (2, 1, 0):
        flow_u, flow_v, flow_v_face, sea = [], [], [], []
        for tile in range(count):
            here = rows_of(tile)
            flow_u.append(mask_u_s[step, here, :] * bar_u[tile])
            flow_v.append(mask_v_s[step, here, :] * bar_v[tile])
        flow_v_face = list(flow_v)
        flow_v_face[last - 1] = flow_v[last - 1] - jnp.where(
            at_top & (row == TILE - 1), pltpu.roll(flow_v[last], DEEP, 0), 0.0
        )
        for tile in range(count):
            here = rows_of(tile)
            bar_h[tile] = (
                bar_h[tile]
                + (flow_u[tile] - west_of(flow_u[tile]))
                + (flow_v_face[tile] - south_of(flow_v_face, tile))
            )
            sea.append(land_s[here, :] * bar_h[tile])
        for tile in range(count):
            here = rows_of(tile)
            turn_u = east_of(sea[tile]) - sea[tile]
            turn_v = north_of(sea, tile) - sea[tile]
            if tile == last:
                turn_v = jnp.where(row == 3, -pltpu.roll(fold_turn, DEEP, 0), turn_v)
            fold_turn = turn_v
            bar_u[tile] = keep_u_s[step, here, :] * flow_u[tile] + depth_u_s[here, :] * turn_u
            bar_v[tile] = keep_v_s[step, here, :] * flow_v[tile] + depth_v_s[here, :] * turn_v
            add_to(sum_xu, tile, drag_u_s[step, here, :] * flow_u[tile])
            add_to(sum_xv, tile, drag_v_s[step, here, :] * flow_v[tile])
            add_to(sum_u, tile, vel_u_s[step, here, :] * turn_u)
            add_to(sum_v, tile, vel_v_s[step, here, :] * turn_v)

    face_v = [
        ratio_v_s[rows_of(tile), :] * sum_xv[tile] + sum_v[tile] for tile in range(count)
    ]
    for tile in range(last):
        here = rows_of(tile)
        face_u = ratio_u_s[here, :] * sum_xu[tile] + sum_u[tile]
        total = face_u + west_of(face_u) + face_v[tile] + south_of(face_v, tile)
        if tile == last - 1:
            total = total + jnp.where(
                at_top & (row == TILE - 1), pltpu.roll(face_v[last], DEEP, 0), 0.0
            )
        out_h[0, here, :] = bar_h[tile][:, :width]
        out_u[0, here, :] = bar_u[tile][:, :width]
        out_v[0, here, :] = bar_v[tile][:, :width]
        out_depth[0, here, :] = 0.5 * total[:, :width]
        out_drag[0, here, :] = (sum_xu[tile] + sum_xv[tile])[:, :width]


def on_device(traj_u, traj_v, adj_h, adj_u, adj_v, depth, drag, land, wet_u, wet_v):
    count, rows, width = adj_h.shape
    steps = traj_u.shape[0]
    args = (adj_h, adj_u, adj_v, traj_u, traj_v, wet_u, wet_v, depth, drag, land)

    def pieces(shape):
        return [pltpu.VMEM(arg.shape[:-2] + shape, arg.dtype) for arg in args] * 2

    in_place = [pl.BlockSpec(memory_space=pl.ANY)] * len(args)
    params = pltpu.CompilerParams(vmem_limit_bytes=VMEM_LIMIT)
    row_pack = jax.ShapeDtypeStruct((message_rows(count), width), jnp.float32)
    one, two = pl.pallas_call(
        pack_rows,
        in_specs=in_place,
        out_shape=[row_pack] * 2,
        scratch_shapes=pieces((TILE, width)) + [pltpu.SemaphoreType.DMA((len(args), 2))],
        compiler_params=params,
        name="pack_rows",
    )(*args)

    lons, lats, subs = (lax.axis_size(axis) for axis in GRID)
    total_rows = lats * subs

    def device(lon, row):
        return lon * total_rows + row

    one = lax.ppermute(one, "sub", [(core, core ^ 1) for core in range(subs)])
    route = []
    for lon in range(lons):
        for row in range(1, total_rows - 1, 2):
            route += [(device(lon, row), device(lon, row + 1)), (device(lon, row + 1), device(lon, row))]
        route.append((device(lon, total_rows - 1), device(lons - 1 - lon, total_rows - 1)))
    two = lax.ppermute(two, GRID, route)

    own_pack = jax.ShapeDtypeStruct((rows, 2 * LANES), jnp.float32)
    own_west, own_east = pl.pallas_call(
        pack_columns_own,
        in_specs=in_place,
        out_shape=[own_pack] * 2,
        scratch_shapes=pieces((rows, LANES)) + [pltpu.SemaphoreType.DMA((len(args), 2))],
        compiler_params=params,
        name="pack_columns",
    )(*args)

    full_pack = jax.ShapeDtypeStruct((rows + TILE, 2 * LANES), jnp.float32)
    halo, halo_static, to_west, to_east = pl.pallas_call(
        merge_rows,
        out_shape=[
            jax.ShapeDtypeStruct((3 * count, TILE, width), jnp.float32),
            jax.ShapeDtypeStruct((len(TILES), TILE, width), jnp.float32),
            full_pack,
            full_pack,
        ],
        compiler_params=params,
        name="merge_rows",
    )(one, two, own_west, own_east)
    from_east = lax.ppermute(to_west, "lon", [(lon, (lon - 1) % lons) for lon in range(lons)])
    from_west = lax.ppermute(to_east, "lon", [(lon, (lon + 1) % lons) for lon in range(lons)])

    def whole(shape):
        return pl.BlockSpec(shape, lambda sens: (0,) * len(shape))

    block = pl.BlockSpec((1, rows, width), lambda sens: (sens, 0, 0))
    out = jax.ShapeDtypeStruct(adj_h.shape, jnp.float32)
    ext = (rows + TILE, width + LANES)
    return pl.pallas_call(
        functools.partial(steps_kernel, count),
        grid=(count,),
        in_specs=[block] * 3
        + [whole(arg.shape) for arg in args[3:]]
        + [
            pl.BlockSpec((3, TILE, width), lambda sens: (sens, 0, 0)),
            pl.BlockSpec((len(TILES), TILE, width), lambda sens: (0, 0, 0)),
            whole(full_pack.shape),
            whole(full_pack.shape),
        ],
        out_specs=[block] * 5,
        out_shape=[out] * 5,
        scratch_shapes=[pltpu.VMEM((steps,) + ext, jnp.float32)] * 8 + [pltpu.VMEM(ext, jnp.float32)] * 5,
        compiler_params=params,
        name="reverse_steps",
    )(*args, halo, halo_static, from_west, from_east)


def solution(mesh):
    state = P("case", ROWS, "lon")
    fixed = P(ROWS, "lon")
    return jax.shard_map(
        on_device,
        mesh=mesh,
        in_specs=(state,) * 5 + (fixed,) * 3 + (state,) * 2,
        out_specs=(state,) * 5,
        check_vma=False,
    )
```

```python
import functools

import jax
import jax.numpy as jnp
from jax import lax
from jax.experimental import pallas as pl
from jax.experimental.pallas import tpu as pltpu
from jax.sharding import PartitionSpec as P

time_step = 0.5
gravity = 1.0
speed_floor = 0.01

ROWS = ("lat", "sub")
GRID = ("lon", "lat", "sub")
TILE = 8
LANES = 128
DEEP = 4
VMEM_LIMIT = 48 * 1024 * 1024


def iota(shape, axis):
    return lax.broadcasted_iota(jnp.int32, shape, axis)


def place():
    row = lax.axis_index("lat") * lax.axis_size("sub") + lax.axis_index("sub")
    last = lax.axis_size("lat") * lax.axis_size("sub") - 1
    return row % 2 == 0, row == last


STATE_SLOTS = (3, 3, 4)
SHARED = (
    (("traj_v", 2), 2, 3, True),
    (("traj_v", 1), 2, 2, True),
    (("traj_v", 0), 2, 1, True),
    (("traj_u", 2), 1, 2, True),
    (("traj_u", 1), 1, 1, True),
    (("wet_v", 1), 2, 3, False),
    (("wet_v", 0), 2, 2, False),
    (("wet_u", 1), 1, 2, False),
    (("wet_u", 0), 1, 1, False),
    (("depth", None), 0, 3, False),
    (("drag", None), 3, 3, False),
    (("land", None), 0, 3, False),
)
NAMES = ("adj_h", "adj_u", "adj_v", "traj_u", "traj_v", "wet_u", "wet_v", "depth", "drag", "land")
TILES = tuple(entry[0] for entry in SHARED[:10]) + (("drag", 1), ("drag", 2), ("land", None), ("traj_u", 0))


def load(refs, name, step):
    value = refs[name][...] if step is None or name == "drag" else refs[name][step]
    return value.astype(jnp.float32)


def message_rows(count):
    rows = sum(STATE_SLOTS) * count + sum(entry[2] for entry in SHARED)
    return -(-rows // TILE) * TILE


def row_plan(count):
    plan, at = [], 0
    for sens in range(count):
        for kind in range(3):
            plan.append(((NAMES[kind], sens), kind, kind > 0, at, STATE_SLOTS[kind]))
            at += STATE_SLOTS[kind]
    for key, kind, slots, turned in SHARED:
        plan.append((key, kind, turned, at, slots))
        at += slots
    return plan


def lane_tiles(value):
    return [value[:, at : at + LANES] for at in range(0, value.shape[1], LANES)]


def masked(refs, key):
    name, step = key
    value = load(refs, name, step)
    if name == "adj_u":
        value = value * load(refs, "wet_u", 2)
    if name == "adj_v":
        value = value * load(refs, "wet_v", 2)
    return value


def pack_rows(*refs):
    arrays = dict(zip(NAMES, refs[:10]))
    one, two = refs[10:12]
    bottom = dict(zip(NAMES, refs[12:22]))
    top = dict(zip(NAMES, refs[22:32]))
    sems = refs[32]
    count, rows, width = arrays["adj_h"].shape
    even, at_top = place()
    copies = {}
    order = ("wet_u", "wet_v", "adj_h", "adj_u", "adj_v", "traj_u", "traj_v", "depth", "drag", "land")
    for number, name in enumerate(order):
        array = arrays[name]
        lead = (slice(None),) * (array.ndim - 2)
        pair = []
        for side, (held, first) in enumerate(((bottom, 0), (top, rows - TILE))):
            pair.append(
                pltpu.make_async_copy(array.at[lead + (pl.ds(first, TILE),)], held[name], sems.at[number, side])
            )
        for copy in pair:
            copy.start()
        copies[name] = pair
    for name in order:
        for copy in copies[name]:
            copy.wait()

    plan = row_plan(count)
    for key, kind, turned, at, slots in plan:
        low = masked(bottom, key)[:slots]
        high = masked(top, key)[TILE - slots :]
        here = slice(at, at + slots)
        one[here, :] = jnp.where(even, high, low)
        two[here, :] = jnp.where(even, low, high)

    @pl.when(at_top)
    def _():
        row = iota((TILE, LANES), 0)
        lane = LANES - 1 - iota((TILE, LANES), 1)
        for key, kind, turned, at, slots in plan:
            value = masked(top, key)
            sources = [TILE - 1 - slot for slot in range(slots)]
            if kind == 2:
                sources = [TILE - 2 - slot for slot in range(slots - 1)] + [TILE - 1]
            order = jnp.zeros((TILE, LANES), jnp.int32)
            for slot, source in enumerate(sources):
                order = jnp.where(row == slot, source, order)
            pieces = []
            for piece in lane_tiles(value)[::-1]:
                piece = jnp.take_along_axis(piece, lane, axis=1)
                piece = jnp.take_along_axis(piece, order, axis=0)
                if turned:
                    piece = jnp.where(row == slots - 1, piece, -piece) if kind == 2 else -piece
                pieces.append(piece)
            two[at : at + slots, :] = jnp.concatenate(pieces, axis=1)[:slots]


def group_lanes(field):
    return field // 32, DEEP * (field % 32)


def column_fields(count):
    return [(NAMES[kind], sens) for sens in range(count) for kind in range(3)] + list(TILES)


def pack_columns_own(*refs):
    arrays = dict(zip(NAMES, refs[:10]))
    to_west, to_east = refs[10:12]
    west = dict(zip(NAMES, refs[12:22]))
    east = dict(zip(NAMES, refs[22:32]))
    sems = refs[32]
    count, rows, width = arrays["adj_h"].shape
    copies = []
    for number, name in enumerate(NAMES):
        array = arrays[name]
        lead = (slice(None),) * (array.ndim - 1)
        for side, (held, first) in enumerate(((west, 0), (east, width - LANES))):
            copies.append(
                pltpu.make_async_copy(array.at[lead + (pl.ds(first, LANES),)], held[name], sems.at[number, side])
            )
    for copy in copies:
        copy.start()
    for copy in copies:
        copy.wait()
    lane = iota((rows, LANES), 1)
    for held, target, origin in ((west, to_west, 0), (east, to_east, LANES - DEEP)):
        packed = [None, None]
        for field, key in enumerate(column_fields(count)):
            side, at = group_lanes(field)
            value = masked(held, key)
            shift = (at - origin) % LANES
            if shift:
                value = pltpu.roll(value, shift, 1)
            packed[side] = value if packed[side] is None else jnp.where(lane >= at, value, packed[side])
        for side in range(2):
            target[:, side * LANES : (side + 1) * LANES] = packed[side]


def merge_rows(one, two, own_west, own_east, halo, halo_static, to_west, to_east):
    even, at_top = place()
    width = one.shape[1]
    rows = own_west.shape[0]
    count = halo.shape[0] // 3
    lane = iota((TILE, LANES), 1)
    to_west[:rows, :] = own_west[...]
    to_east[:rows, :] = own_east[...]
    packed = [[None, None], [None, None]]
    field = 0
    for key, kind, turned, at, slots in row_plan(count):
        here = slice(at, at + slots)
        north = jnp.where(even, one[here, :], two[here, :])
        south = jnp.where(even, two[here, :], one[here, :])
        blank = jnp.zeros((DEEP - slots, width), jnp.float32)
        gap = [blank] if slots < DEEP else []
        plain = jnp.concatenate([north] + gap + gap + [south], axis=0)
        values = [plain]
        if kind >= 2 and slots < DEEP:
            fold = ([north[:-1]] if slots > 1 else []) + gap + [north[-1:]] + gap + [south]
            if kind == 3:
                fold = [north[1:], blank, north[:1]] + gap + [south]
                values.append(jnp.where(at_top, jnp.concatenate(fold, axis=0), plain))
            else:
                values = [jnp.where(at_top, jnp.concatenate(fold, axis=0), plain)]
        for value in values:
            if field < halo.shape[0]:
                halo[field] = value
            else:
                halo_static[field - halo.shape[0]] = value
            side, start = group_lanes(field)
            pieces = lane_tiles(value)
            for way, piece, origin in ((0, pieces[0], 0), (1, pieces[-1], LANES - DEEP)):
                shift = (start - origin) % LANES
                if shift:
                    piece = pltpu.roll(piece, shift, 1)
                held = packed[way][side]
                packed[way][side] = piece if held is None else jnp.where(lane >= start, piece, held)
            field += 1
    halo_static[field - halo.shape[0]] = jnp.zeros((TILE, width), jnp.float32)
    for way, target in ((0, to_west), (1, to_east)):
        for side in range(2):
            target[rows:, side * LANES : (side + 1) * LANES] = packed[way][side]


def steps_kernel(
    adj_count, adj_h, adj_u, adj_v, traj_u, traj_v, wet_u, wet_v, depth, drag, land,
    halo, halo_static, from_west, from_east,
    out_h, out_u, out_v, out_depth, out_drag,
    mask_u_s, mask_v_s, keep_u_s, keep_v_s, drag_u_s, drag_v_s, vel_u_s, vel_v_s,
    depth_u_s, depth_v_s, ratio_u_s, ratio_v_s, land_s,
):
    _, at_top = place()
    rows, width = adj_h.shape[1:]
    count = rows // TILE + 1
    last = count - 1
    wide = width + LANES
    row = iota((TILE, wide), 0)
    lane = iota((TILE, LANES), 1)
    sens = pl.program_id(0)
    halo_count = 3 * adj_count

    def corner(side, at, tile):
        here = slice(tile * TILE, (tile + 1) * TILE)
        cols = slice(side * LANES, (side + 1) * LANES)
        east = pltpu.roll(from_east[here, cols], (LANES - at) % LANES, 1)
        west = pltpu.roll(from_west[here, cols], (2 * LANES - DEEP - at) % LANES, 1)
        return jnp.where(lane < LANES // 2, east, west)

    def extended(own, halo_rows, corner_of, kind):
        out = []
        for tile in range(count):
            body = own(tile) if tile < last else halo_rows()
            value = jnp.concatenate([body, corner_of(tile)], axis=1)
            if tile == last and kind == 1:
                value = jnp.where(at_top & (row < DEEP), pltpu.roll(value, wide - 1, 1), value)
            out.append(value)
        return out

    def east_of(value):
        return pltpu.roll(value, wide - 1, 1)

    def west_of(value):
        return pltpu.roll(value, 1, 1)

    def south_of(values, tile):
        return jnp.where(row == 0, pltpu.roll(values[tile - 1], 1, 0), pltpu.roll(values[tile], 1, 0))

    def north_of(values, tile):
        return jnp.where(
            row == TILE - 1,
            pltpu.roll(values[(tile + 1) % count], TILE - 1, 0),
            pltpu.roll(values[tile], TILE - 1, 0),
        )

    def rows_of(tile):
        return slice(tile * TILE, (tile + 1) * TILE)

    @pl.when(sens == 0)
    def _():
        def static(key, ref, kind):
            own = lambda tile: ref[rows_of(tile), :].astype(jnp.float32)
            if key not in TILES:
                ones = lambda columns: jnp.ones((TILE, columns), jnp.float32)
                return extended(own, lambda: ones(width), lambda tile: ones(LANES), 0)
            index = TILES.index(key)
            side, at = group_lanes(halo_count + index)
            return extended(own, lambda: halo_static[index], lambda tile: corner(side, at, tile), kind)

        cells = [jnp.where(value > 0.0, value, 1.0) for value in static(("depth", None), depth, 0)]
        drag_u = static(("drag", 1), drag, 1)
        drag_v = static(("drag", 2), drag, 2)
        sea = static(("land", None), land, 0)
        face_u = [0.5 * (value + east_of(value)) for value in cells]
        face_v = [0.5 * (cells[tile] + north_of(cells, tile)) for tile in range(count)]
        face_v[last] = jnp.where(row == 3, pltpu.roll(face_v[last - 1], DEEP, 0), face_v[last])
        for tile in range(count):
            here = rows_of(tile)
            land_s[here, :] = 0.5 * sea[tile]
            inverse_u = 1.0 / face_u[tile]
            inverse_v = 1.0 / face_v[tile]
            depth_u_s[here, :] = face_u[tile]
            depth_v_s[here, :] = face_v[tile]
            ratio_u_s[here, :] = -drag_u[tile] * inverse_u
            ratio_v_s[here, :] = -drag_v[tile] * inverse_v
        for step in range(3):
            for kind, way, vel_ref, wet_ref, depth_s, ratio_s, mask_s, keep_s, drag_s, vel_s in (
                (1, "u", traj_u, wet_u, depth_u_s, ratio_u_s, mask_u_s, keep_u_s, drag_u_s, vel_u_s),
                (2, "v", traj_v, wet_v, depth_v_s, ratio_v_s, mask_v_s, keep_v_s, drag_v_s, vel_v_s),
            ):
                vel = static(("traj_" + way, step), vel_ref.at[step], kind)
                wet = static(("wet_" + way, step), wet_ref.at[step], kind)
                for tile in range(count):
                    here = rows_of(tile)
                    square = vel[tile] * vel[tile]
                    speed = jnp.sqrt(square + speed_floor)
                    mask_s[step, here, :] = 0.5 * wet[tile]
                    keep_s[step, here, :] = 2.0 + ratio_s[here, :] * (speed + square / speed)
                    drag_s[step, here, :] = -vel[tile] * speed / depth_s[here, :]
                    vel_s[step, here, :] = vel[tile]

    def dynamic(kind, ref):
        at = DEEP * (3 * sens + kind)
        return extended(
            lambda tile: ref[0, rows_of(tile), :],
            lambda: halo[kind],
            lambda tile: corner(0, at, tile),
            kind,
        )

    bar_h, bar_u, bar_v = dynamic(0, adj_h), dynamic(1, adj_u), dynamic(2, adj_v)
    sum_xu, sum_xv, sum_u, sum_v = ([None] * count for _ in range(4))

    def add_to(sums, tile, value):
        sums[tile] = value if sums[tile] is None else sums[tile] + value

    for step in (2, 1, 0):
        flow_u, flow_v, flow_v_face, sea = [], [], [], []
        for tile in range(count):
            here = rows_of(tile)
            flow_u.append(mask_u_s[step, here, :] * bar_u[tile])
            flow_v.append(mask_v_s[step, here, :] * bar_v[tile])
        flow_v_face = list(flow_v)
        flow_v_face[last - 1] = flow_v[last - 1] - jnp.where(
            at_top & (row == TILE - 1), pltpu.roll(flow_v[last], DEEP, 0), 0.0
        )
        for tile in range(count):
            here = rows_of(tile)
            bar_h[tile] = (
                bar_h[tile]
                + (flow_u[tile] - west_of(flow_u[tile]))
                + (flow_v_face[tile] - south_of(flow_v_face, tile))
            )
            sea.append(land_s[here, :] * bar_h[tile])
        for tile in range(count):
            here = rows_of(tile)
            turn_u = east_of(sea[tile]) - sea[tile]
            turn_v = north_of(sea, tile) - sea[tile]
            if tile == last:
                turn_v = jnp.where(row == 3, -pltpu.roll(fold_turn, DEEP, 0), turn_v)
            fold_turn = turn_v
            bar_u[tile] = keep_u_s[step, here, :] * flow_u[tile] + depth_u_s[here, :] * turn_u
            bar_v[tile] = keep_v_s[step, here, :] * flow_v[tile] + depth_v_s[here, :] * turn_v
            add_to(sum_xu, tile, drag_u_s[step, here, :] * flow_u[tile])
            add_to(sum_xv, tile, drag_v_s[step, here, :] * flow_v[tile])
            add_to(sum_u, tile, vel_u_s[step, here, :] * turn_u)
            add_to(sum_v, tile, vel_v_s[step, here, :] * turn_v)

    face_v = [
        ratio_v_s[rows_of(tile), :] * sum_xv[tile] + sum_v[tile] for tile in range(count)
    ]
    for tile in range(last):
        here = rows_of(tile)
        face_u = ratio_u_s[here, :] * sum_xu[tile] + sum_u[tile]
        total = face_u + west_of(face_u) + face_v[tile] + south_of(face_v, tile)
        if tile == last - 1:
            total = total + jnp.where(
                at_top & (row == TILE - 1), pltpu.roll(face_v[last], DEEP, 0), 0.0
            )
        out_h[0, here, :] = bar_h[tile][:, :width]
        out_u[0, here, :] = bar_u[tile][:, :width]
        out_v[0, here, :] = bar_v[tile][:, :width]
        out_depth[0, here, :] = 0.5 * total[:, :width]
        out_drag[0, here, :] = (sum_xu[tile] + sum_xv[tile])[:, :width]


def on_device(traj_u, traj_v, adj_h, adj_u, adj_v, depth, drag, land, wet_u, wet_v):
    count, rows, width = adj_h.shape
    steps = traj_u.shape[0]
    args = (adj_h, adj_u, adj_v, traj_u, traj_v, wet_u, wet_v, depth, drag, land)
    args = tuple(pltpu.with_memory_space_constraint(arg, pltpu.HBM) for arg in args)

    def pieces(shape):
        return [pltpu.VMEM(arg.shape[:-2] + shape, arg.dtype) for arg in args] * 2

    in_place = [pl.BlockSpec(memory_space=pl.ANY)] * len(args)
    params = pltpu.CompilerParams(vmem_limit_bytes=VMEM_LIMIT)
    row_pack = jax.ShapeDtypeStruct((message_rows(count), width), jnp.float32)
    one, two = pl.pallas_call(
        pack_rows,
        in_specs=in_place,
        out_shape=[row_pack] * 2,
        scratch_shapes=pieces((TILE, width)) + [pltpu.SemaphoreType.DMA((len(args), 2))],
        compiler_params=params,
        name="pack_rows",
    )(*args)

    lons, lats, subs = (lax.axis_size(axis) for axis in GRID)
    total_rows = lats * subs

    def device(lon, row):
        return lon * total_rows + row

    one = lax.ppermute(one, "sub", [(core, core ^ 1) for core in range(subs)])
    route = []
    for lon in range(lons):
        for row in range(1, total_rows - 1, 2):
            route += [(device(lon, row), device(lon, row + 1)), (device(lon, row + 1), device(lon, row))]
        route.append((device(lon, total_rows - 1), device(lons - 1 - lon, total_rows - 1)))
    two = lax.ppermute(two, GRID, route)

    own_pack = jax.ShapeDtypeStruct((rows, 2 * LANES), jnp.float32)
    own_west, own_east = pl.pallas_call(
        pack_columns_own,
        in_specs=in_place,
        out_shape=[own_pack] * 2,
        scratch_shapes=pieces((rows, LANES)) + [pltpu.SemaphoreType.DMA((len(args), 2))],
        compiler_params=params,
        name="pack_columns",
    )(*args)

    full_pack = jax.ShapeDtypeStruct((rows + TILE, 2 * LANES), jnp.float32)
    halo, halo_static, to_west, to_east = pl.pallas_call(
        merge_rows,
        out_shape=[
            jax.ShapeDtypeStruct((3 * count, TILE, width), jnp.float32),
            jax.ShapeDtypeStruct((len(TILES), TILE, width), jnp.float32),
            full_pack,
            full_pack,
        ],
        compiler_params=params,
        name="merge_rows",
    )(one, two, own_west, own_east)
    from_east = lax.ppermute(to_west, "lon", [(lon, (lon - 1) % lons) for lon in range(lons)])
    from_west = lax.ppermute(to_east, "lon", [(lon, (lon + 1) % lons) for lon in range(lons)])

    def whole(shape):
        return pl.BlockSpec(shape, lambda sens: (0,) * len(shape))

    block = pl.BlockSpec((1, rows, width), lambda sens: (sens, 0, 0))
    out = jax.ShapeDtypeStruct(adj_h.shape, jnp.float32)
    ext = (rows + TILE, width + LANES)
    return pl.pallas_call(
        functools.partial(steps_kernel, count),
        grid=(count,),
        in_specs=[block] * 3
        + [whole(arg.shape) for arg in args[3:]]
        + [
            pl.BlockSpec((3, TILE, width), lambda sens: (sens, 0, 0)),
            pl.BlockSpec((len(TILES), TILE, width), lambda sens: (0, 0, 0)),
            whole(full_pack.shape),
            whole(full_pack.shape),
        ],
        out_specs=[block] * 5,
        out_shape=[out] * 5,
        scratch_shapes=[pltpu.VMEM((steps,) + ext, jnp.float32)] * 8 + [pltpu.VMEM(ext, jnp.float32)] * 5,
        compiler_params=params,
        name="reverse_steps",
    )(*args, halo, halo_static, from_west, from_east)


def solution(mesh):
    state = P("case", ROWS, "lon")
    fixed = P(ROWS, "lon")
    return jax.shard_map(
        on_device,
        mesh=mesh,
        in_specs=(state,) * 5 + (fixed,) * 3 + (state,) * 2,
        out_specs=(state,) * 5,
        check_vma=False,
    )
```

```python
import functools

import jax
import jax.numpy as jnp
from jax import lax
from jax.experimental import pallas as pl
from jax.experimental.pallas import tpu as pltpu
from jax.sharding import PartitionSpec as P

time_step = 0.5
gravity = 1.0
speed_floor = 0.01

ROWS = ("lat", "sub")
GRID = ("lon", "lat", "sub")
TILE = 8
LANES = 128
DEEP = 4
VMEM_LIMIT = 48 * 1024 * 1024


def iota(shape, axis):
    return lax.broadcasted_iota(jnp.int32, shape, axis)


def place():
    row = lax.axis_index("lat") * lax.axis_size("sub") + lax.axis_index("sub")
    last = lax.axis_size("lat") * lax.axis_size("sub") - 1
    return row % 2 == 0, row == last, row == 0


STATE_SLOTS = (3, 3, 4)
SHARED = (
    (("traj_v", 2), 2, 3, True),
    (("traj_v", 1), 2, 2, True),
    (("traj_v", 0), 2, 1, True),
    (("traj_u", 2), 1, 2, True),
    (("traj_u", 1), 1, 1, True),
    (("wet_v", 1), 2, 3, False),
    (("wet_v", 0), 2, 2, False),
    (("wet_u", 1), 1, 2, False),
    (("wet_u", 0), 1, 1, False),
    (("depth", None), 0, 3, False),
    (("drag", None), 3, 3, False),
    (("land", None), 0, 3, False),
)
NAMES = ("adj_h", "adj_u", "adj_v", "traj_u", "traj_v", "wet_u", "wet_v", "depth", "drag", "land")
TILES = tuple(entry[0] for entry in SHARED[:10]) + (("drag", 1), ("drag", 2), ("land", None), ("traj_u", 0))


def load(refs, name, step):
    value = refs[name][...] if step is None or name == "drag" else refs[name][step]
    return value.astype(jnp.float32)


def message_rows(count):
    rows = sum(STATE_SLOTS) * count + sum(entry[2] for entry in SHARED)
    return -(-rows // TILE) * TILE


def row_plan(count):
    plan, at = [], 0
    for sens in range(count):
        for kind in range(3):
            plan.append(((NAMES[kind], sens), kind, kind > 0, at, STATE_SLOTS[kind]))
            at += STATE_SLOTS[kind]
    for key, kind, slots, turned in SHARED:
        plan.append((key, kind, turned, at, slots))
        at += slots
    return plan


def lane_tiles(value):
    return [value[:, at : at + LANES] for at in range(0, value.shape[1], LANES)]


def masked(refs, key):
    name, step = key
    value = load(refs, name, step)
    if name == "adj_u":
        value = value * load(refs, "wet_u", 2)
    if name == "adj_v":
        value = value * load(refs, "wet_v", 2)
    return value


def start_copies(arrays, held, sems, window, names=NAMES):
    copies = {}
    for number, name in enumerate(NAMES):
        array = arrays[name]
        if name in names:
            lead = (slice(None),) * (array.ndim - 2)
            source = array.at[lead + window(*array.shape[-2:])]
            copies[name] = pltpu.make_async_copy(source, held[name], sems.at[number])
            copies[name].start()
    return copies


def row_window(at_bottom_edge):
    def window(rows, width):
        first = pl.multiple_of(jnp.where(at_bottom_edge, 0, rows - TILE), TILE)
        return pl.ds(first, TILE), slice(None)

    return window


def pack_edge(held, target, from_bottom, count):
    for key, kind, turned, at, slots in row_plan(count):
        value = masked(held, key)
        target[at : at + slots, :] = jnp.where(from_bottom, value[:slots], value[TILE - slots :])


def pack_far(*refs):
    arrays = dict(zip(NAMES, refs[:10]))
    target = refs[10]
    held = dict(zip(NAMES, refs[11:21]))
    even, at_top, _ = place()
    count = arrays["adj_h"].shape[0]
    for copy in start_copies(arrays, held, refs[21], row_window(even)).values():
        copy.wait()

    @pl.when(jnp.logical_not(at_top))
    def _():
        pack_edge(held, target, even, count)

    @pl.when(at_top)
    def _():
        row = iota((TILE, LANES), 0)
        lane = LANES - 1 - iota((TILE, LANES), 1)
        for key, kind, turned, at, slots in row_plan(count):
            value = masked(held, key)
            sources = [TILE - 1 - slot for slot in range(slots)]
            if kind == 2:
                sources = [TILE - 2 - slot for slot in range(slots - 1)] + [TILE - 1]
            order = jnp.zeros((TILE, LANES), jnp.int32)
            for slot, source in enumerate(sources):
                order = jnp.where(row == slot, source, order)
            pieces = []
            for piece in lane_tiles(value)[::-1]:
                piece = jnp.take_along_axis(piece, lane, axis=1)
                piece = jnp.take_along_axis(piece, order, axis=0)
                if turned:
                    piece = jnp.where(row == slots - 1, piece, -piece) if kind == 2 else -piece
                pieces.append(piece)
            target[at : at + slots, :] = jnp.concatenate(pieces, axis=1)[:slots]


def group_lanes(field):
    return field // 32, DEEP * (field % 32)


def column_fields(count):
    return [(NAMES[kind], sens) for sens in range(count) for kind in range(3)] + list(TILES)


def pack_near(*refs):
    arrays = dict(zip(NAMES, refs[:10]))
    target, to_west, to_east = refs[10:13]
    held = dict(zip(NAMES, refs[13:23]))
    west = dict(zip(NAMES, refs[23:33]))
    east = dict(zip(NAMES, refs[33:43]))
    sems = refs[43]
    even, _, _ = place()
    count, rows, width = arrays["adj_h"].shape
    near = start_copies(arrays, held, sems.at[0], row_window(jnp.logical_not(even)))
    sides = []
    for number, (side, first) in enumerate(((west, 0), (east, width - LANES))):
        window = lambda rows, width, first=first: (slice(None), pl.ds(first, LANES))
        sides.append(start_copies(arrays, side, sems.at[1 + number], window))
    for copy in near.values():
        copy.wait()
    pack_edge(held, target, jnp.logical_not(even), count)
    lane = iota((rows, LANES), 1)
    for copies, side_held, packs, origin in (
        (sides[0], west, to_west, 0),
        (sides[1], east, to_east, LANES - DEEP),
    ):
        for copy in copies.values():
            copy.wait()
        packed = [None, None]
        for field, key in enumerate(column_fields(count)):
            side, at = group_lanes(field)
            value = masked(side_held, key)
            shift = (at - origin) % LANES
            if shift:
                value = pltpu.roll(value, shift, 1)
            packed[side] = value if packed[side] is None else jnp.where(lane >= at, value, packed[side])
        for side in range(2):
            packs[:, side * LANES : (side + 1) * LANES] = packed[side]


def merge_rows(one, two, own_west, own_east, halo, halo_static, to_west, to_east):
    even, at_top, at_bottom = place()
    width = one.shape[1]
    rows = own_west.shape[0]
    count = halo.shape[0] // 3
    lane = iota((TILE, LANES), 1)
    to_west[:rows, :] = own_west[...]
    to_east[:rows, :] = own_east[...]
    packed = [[None, None], [None, None]]
    field = 0
    for key, kind, turned, at, slots in row_plan(count):
        here = slice(at, at + slots)
        north = jnp.where(even, one[here, :], two[here, :])
        south = jnp.where(even, two[here, :], one[here, :])
        south = jnp.where(at_bottom, 0.0, south)
        blank = jnp.zeros((DEEP - slots, width), jnp.float32)
        gap = [blank] if slots < DEEP else []
        plain = jnp.concatenate([north] + gap + gap + [south], axis=0)
        values = [plain]
        if kind >= 2 and slots < DEEP:
            fold = ([north[:-1]] if slots > 1 else []) + gap + [north[-1:]] + gap + [south]
            if kind == 3:
                fold = [north[1:], blank, north[:1]] + gap + [south]
                values.append(jnp.where(at_top, jnp.concatenate(fold, axis=0), plain))
            else:
                values = [jnp.where(at_top, jnp.concatenate(fold, axis=0), plain)]
        for value in values:
            if field < halo.shape[0]:
                halo[field] = value
            else:
                halo_static[field - halo.shape[0]] = value
            side, start = group_lanes(field)
            pieces = lane_tiles(value)
            for way, piece, origin in ((0, pieces[0], 0), (1, pieces[-1], LANES - DEEP)):
                shift = (start - origin) % LANES
                if shift:
                    piece = pltpu.roll(piece, shift, 1)
                held = packed[way][side]
                packed[way][side] = piece if held is None else jnp.where(lane >= start, piece, held)
            field += 1
    halo_static[field - halo.shape[0]] = jnp.zeros((TILE, width), jnp.float32)
    for way, target in ((0, to_west), (1, to_east)):
        for side in range(2):
            target[rows:, side * LANES : (side + 1) * LANES] = packed[way][side]


def steps_kernel(
    adj_count, adj_h, adj_u, adj_v, traj_u, traj_v, wet_u, wet_v, depth, drag, land,
    halo, halo_static, from_west, from_east,
    out_h, out_u, out_v, out_depth, out_drag,
    mask_u_s, mask_v_s, keep_u_s, keep_v_s, drag_u_s, drag_v_s, vel_u_s, vel_v_s,
    depth_u_s, depth_v_s, ratio_u_s, ratio_v_s, land_s,
):
    _, at_top, _ = place()
    rows, width = adj_h.shape[1:]
    count = rows // TILE + 1
    last = count - 1
    wide = width + LANES
    row = iota((TILE, wide), 0)
    lane = iota((TILE, LANES), 1)
    sens = pl.program_id(0)
    halo_count = 3 * adj_count

    def corner(side, at, tile):
        here = slice(tile * TILE, (tile + 1) * TILE)
        cols = slice(side * LANES, (side + 1) * LANES)
        east = pltpu.roll(from_east[here, cols], (LANES - at) % LANES, 1)
        west = pltpu.roll(from_west[here, cols], (2 * LANES - DEEP - at) % LANES, 1)
        return jnp.where(lane < LANES // 2, east, west)

    def extended(own, halo_rows, corner_of, kind):
        out = []
        for tile in range(count):
            body = own(tile) if tile < last else halo_rows()
            value = jnp.concatenate([body, corner_of(tile)], axis=1)
            if tile == last and kind == 1:
                value = jnp.where(at_top & (row < DEEP), pltpu.roll(value, wide - 1, 1), value)
            out.append(value)
        return out

    def east_of(value):
        return pltpu.roll(value, wide - 1, 1)

    def west_of(value):
        return pltpu.roll(value, 1, 1)

    def south_of(values, tile):
        return jnp.where(row == 0, pltpu.roll(values[tile - 1], 1, 0), pltpu.roll(values[tile], 1, 0))

    def north_of(values, tile):
        return jnp.where(
            row == TILE - 1,
            pltpu.roll(values[(tile + 1) % count], TILE - 1, 0),
            pltpu.roll(values[tile], TILE - 1, 0),
        )

    def rows_of(tile):
        return slice(tile * TILE, (tile + 1) * TILE)

    @pl.when(sens == 0)
    def _():
        def static(key, ref, kind):
            own = lambda tile: ref[rows_of(tile), :].astype(jnp.float32)
            if key not in TILES:
                ones = lambda columns: jnp.ones((TILE, columns), jnp.float32)
                return extended(own, lambda: ones(width), lambda tile: ones(LANES), 0)
            index = TILES.index(key)
            side, at = group_lanes(halo_count + index)
            return extended(own, lambda: halo_static[index], lambda tile: corner(side, at, tile), kind)

        cells = [jnp.where(value > 0.0, value, 1.0) for value in static(("depth", None), depth, 0)]
        drag_u = static(("drag", 1), drag, 1)
        drag_v = static(("drag", 2), drag, 2)
        sea = static(("land", None), land, 0)
        face_u = [0.5 * (value + east_of(value)) for value in cells]
        face_v = [0.5 * (cells[tile] + north_of(cells, tile)) for tile in range(count)]
        face_v[last] = jnp.where(row == 3, pltpu.roll(face_v[last - 1], DEEP, 0), face_v[last])
        for tile in range(count):
            here = rows_of(tile)
            land_s[here, :] = 0.5 * sea[tile]
            inverse_u = 1.0 / face_u[tile]
            inverse_v = 1.0 / face_v[tile]
            depth_u_s[here, :] = face_u[tile]
            depth_v_s[here, :] = face_v[tile]
            ratio_u_s[here, :] = -drag_u[tile] * inverse_u
            ratio_v_s[here, :] = -drag_v[tile] * inverse_v
        for step in range(3):
            for kind, way, vel_ref, wet_ref, depth_s, ratio_s, mask_s, keep_s, drag_s, vel_s in (
                (1, "u", traj_u, wet_u, depth_u_s, ratio_u_s, mask_u_s, keep_u_s, drag_u_s, vel_u_s),
                (2, "v", traj_v, wet_v, depth_v_s, ratio_v_s, mask_v_s, keep_v_s, drag_v_s, vel_v_s),
            ):
                vel = static(("traj_" + way, step), vel_ref.at[step], kind)
                wet = static(("wet_" + way, step), wet_ref.at[step], kind)
                for tile in range(count):
                    here = rows_of(tile)
                    square = vel[tile] * vel[tile]
                    speed = jnp.sqrt(square + speed_floor)
                    mask_s[step, here, :] = 0.5 * wet[tile]
                    keep_s[step, here, :] = 2.0 + ratio_s[here, :] * (speed + square / speed)
                    drag_s[step, here, :] = -vel[tile] * speed / depth_s[here, :]
                    vel_s[step, here, :] = vel[tile]

    def dynamic(kind, ref):
        at = DEEP * (3 * sens + kind)
        return extended(
            lambda tile: ref[0, rows_of(tile), :],
            lambda: halo[kind],
            lambda tile: corner(0, at, tile),
            kind,
        )

    bar_h, bar_u, bar_v = dynamic(0, adj_h), dynamic(1, adj_u), dynamic(2, adj_v)
    sum_xu, sum_xv, sum_u, sum_v = ([None] * count for _ in range(4))

    def add_to(sums, tile, value):
        sums[tile] = value if sums[tile] is None else sums[tile] + value

    for step in (2, 1, 0):
        flow_u, flow_v, flow_v_face, sea = [], [], [], []
        for tile in range(count):
            here = rows_of(tile)
            flow_u.append(mask_u_s[step, here, :] * bar_u[tile])
            flow_v.append(mask_v_s[step, here, :] * bar_v[tile])
        flow_v_face = list(flow_v)
        flow_v_face[last - 1] = flow_v[last - 1] - jnp.where(
            at_top & (row == TILE - 1), pltpu.roll(flow_v[last], DEEP, 0), 0.0
        )
        for tile in range(count):
            here = rows_of(tile)
            bar_h[tile] = (
                bar_h[tile]
                + (flow_u[tile] - west_of(flow_u[tile]))
                + (flow_v_face[tile] - south_of(flow_v_face, tile))
            )
            sea.append(land_s[here, :] * bar_h[tile])
        for tile in range(count):
            here = rows_of(tile)
            turn_u = east_of(sea[tile]) - sea[tile]
            turn_v = north_of(sea, tile) - sea[tile]
            if tile == last:
                turn_v = jnp.where(row == 3, -pltpu.roll(fold_turn, DEEP, 0), turn_v)
            fold_turn = turn_v
            bar_u[tile] = keep_u_s[step, here, :] * flow_u[tile] + depth_u_s[here, :] * turn_u
            bar_v[tile] = keep_v_s[step, here, :] * flow_v[tile] + depth_v_s[here, :] * turn_v
            add_to(sum_xu, tile, drag_u_s[step, here, :] * flow_u[tile])
            add_to(sum_xv, tile, drag_v_s[step, here, :] * flow_v[tile])
            add_to(sum_u, tile, vel_u_s[step, here, :] * turn_u)
            add_to(sum_v, tile, vel_v_s[step, here, :] * turn_v)

    face_v = [
        ratio_v_s[rows_of(tile), :] * sum_xv[tile] + sum_v[tile] for tile in range(count)
    ]
    for tile in range(last):
        here = rows_of(tile)
        face_u = ratio_u_s[here, :] * sum_xu[tile] + sum_u[tile]
        total = face_u + west_of(face_u) + face_v[tile] + south_of(face_v, tile)
        if tile == last - 1:
            total = total + jnp.where(
                at_top & (row == TILE - 1), pltpu.roll(face_v[last], DEEP, 0), 0.0
            )
        out_h[0, here, :] = bar_h[tile][:, :width]
        out_u[0, here, :] = bar_u[tile][:, :width]
        out_v[0, here, :] = bar_v[tile][:, :width]
        out_depth[0, here, :] = 0.5 * total[:, :width]
        out_drag[0, here, :] = (sum_xu[tile] + sum_xv[tile])[:, :width]


def on_device(traj_u, traj_v, adj_h, adj_u, adj_v, depth, drag, land, wet_u, wet_v):
    count, rows, width = adj_h.shape
    steps = traj_u.shape[0]
    args = (adj_h, adj_u, adj_v, traj_u, traj_v, wet_u, wet_v, depth, drag, land)
    args = tuple(pltpu.with_memory_space_constraint(arg, pltpu.HBM) for arg in args)

    def pieces(shape):
        return [pltpu.VMEM(arg.shape[:-2] + shape, arg.dtype) for arg in args]

    in_place = [pl.BlockSpec(memory_space=pl.ANY)] * len(args)
    params = pltpu.CompilerParams(vmem_limit_bytes=VMEM_LIMIT)
    row_pack = jax.ShapeDtypeStruct((message_rows(count), width), jnp.float32)
    two = pl.pallas_call(
        pack_far,
        in_specs=in_place,
        out_shape=row_pack,
        scratch_shapes=pieces((TILE, width)) + [pltpu.SemaphoreType.DMA((len(args),))],
        compiler_params=params,
        name="pack_far",
    )(*args)

    lons, lats, subs = (lax.axis_size(axis) for axis in GRID)
    total_rows = lats * subs

    def device(lon, row):
        return lon * total_rows + row

    route = [(device(lon, 0), device(lon ^ 1, 0)) for lon in range(lons)]
    for lon in range(lons):
        for row in range(1, total_rows - 1, 2):
            route += [(device(lon, row), device(lon, row + 1)), (device(lon, row + 1), device(lon, row))]
        route.append((device(lon, total_rows - 1), device(lons - 1 - lon, total_rows - 1)))
    two = lax.ppermute(two, GRID, route)

    own_pack = jax.ShapeDtypeStruct((rows, 2 * LANES), jnp.float32)
    one, own_west, own_east = pl.pallas_call(
        pack_near,
        in_specs=in_place,
        out_shape=[row_pack, own_pack, own_pack],
        scratch_shapes=pieces((TILE, width))
        + pieces((rows, LANES)) * 2
        + [pltpu.SemaphoreType.DMA((3, len(args)))],
        compiler_params=params,
        name="pack_near",
    )(*args)
    one = lax.ppermute(one, "sub", [(core, core ^ 1) for core in range(subs)])

    full_pack = jax.ShapeDtypeStruct((rows + TILE, 2 * LANES), jnp.float32)
    halo, halo_static, to_west, to_east = pl.pallas_call(
        merge_rows,
        out_shape=[
            jax.ShapeDtypeStruct((3 * count, TILE, width), jnp.float32),
            jax.ShapeDtypeStruct((len(TILES), TILE, width), jnp.float32),
            full_pack,
            full_pack,
        ],
        compiler_params=params,
        name="merge_rows",
    )(one, two, own_west, own_east)
    from_east = lax.ppermute(to_west, "lon", [(lon, (lon - 1) % lons) for lon in range(lons)])
    from_west = lax.ppermute(to_east, "lon", [(lon, (lon + 1) % lons) for lon in range(lons)])

    def whole(shape):
        return pl.BlockSpec(shape, lambda sens: (0,) * len(shape))

    block = pl.BlockSpec((1, rows, width), lambda sens: (sens, 0, 0))
    out = jax.ShapeDtypeStruct(adj_h.shape, jnp.float32)
    ext = (rows + TILE, width + LANES)
    return pl.pallas_call(
        functools.partial(steps_kernel, count),
        grid=(count,),
        in_specs=[block] * 3
        + [whole(arg.shape) for arg in args[3:]]
        + [
            pl.BlockSpec((3, TILE, width), lambda sens: (sens, 0, 0)),
            pl.BlockSpec((len(TILES), TILE, width), lambda sens: (0, 0, 0)),
            whole(full_pack.shape),
            whole(full_pack.shape),
        ],
        out_specs=[block] * 5,
        out_shape=[out] * 5,
        scratch_shapes=[pltpu.VMEM((steps,) + ext, jnp.float32)] * 8 + [pltpu.VMEM(ext, jnp.float32)] * 5,
        compiler_params=params,
        name="reverse_steps",
    )(*args, halo, halo_static, from_west, from_east)


def solution(mesh):
    state = P("case", ROWS, "lon")
    fixed = P(ROWS, "lon")
    return jax.shard_map(
        on_device,
        mesh=mesh,
        in_specs=(state,) * 5 + (fixed,) * 3 + (state,) * 2,
        out_specs=(state,) * 5,
        check_vma=False,
    )
```

```python
import functools

import jax
import jax.numpy as jnp
from jax import lax
from jax.experimental import pallas as pl
from jax.experimental.pallas import tpu as pltpu
from jax.sharding import PartitionSpec as P

time_step = 0.5
gravity = 1.0
speed_floor = 0.01

ROWS = ("lat", "sub")
GRID = ("lon", "lat", "sub")
TILE = 8
LANES = 128
DEEP = 4
GROUP = 16
PAIR = 4
VMEM_LIMIT = 48 * 1024 * 1024


def iota(shape, axis):
    return lax.broadcasted_iota(jnp.int32, shape, axis)


def place():
    row = lax.axis_index("lat") * lax.axis_size("sub") + lax.axis_index("sub")
    last = lax.axis_size("lat") * lax.axis_size("sub") - 1
    return row % 2 == 0, row == last, row == 0


STATE_SLOTS = (3, 3, 4)
SHARED = (
    (("traj_v", 2), 2, 3, True),
    (("traj_v", 1), 2, 2, True),
    (("traj_v", 0), 2, 1, True),
    (("traj_u", 2), 1, 2, True),
    (("traj_u", 1), 1, 1, True),
    (("wet_v", 1), 2, 3, False),
    (("wet_v", 0), 2, 2, False),
    (("wet_u", 1), 1, 2, False),
    (("wet_u", 0), 1, 1, False),
    (("depth", None), 0, 3, False),
    (("drag", None), 3, 3, False),
    (("land", None), 0, 3, False),
)
NAMES = ("adj_h", "adj_u", "adj_v", "traj_u", "traj_v", "wet_u", "wet_v", "depth", "drag", "land")
TILES = tuple(entry[0] for entry in SHARED[:10]) + (("drag", 1), ("drag", 2), ("land", None), ("traj_u", 0))


def load(refs, name, step):
    value = refs[name][...] if step is None or name == "drag" else refs[name][step]
    return value.astype(jnp.float32)


def message_rows(count):
    rows = sum(STATE_SLOTS) * count + sum(entry[2] for entry in SHARED)
    return -(-rows // TILE) * TILE


def row_plan(count):
    plan, at = [], 0
    for sens in range(count):
        for kind in range(3):
            plan.append(((NAMES[kind], sens), kind, kind > 0, at, STATE_SLOTS[kind]))
            at += STATE_SLOTS[kind]
    for key, kind, slots, turned in SHARED:
        plan.append((key, kind, turned, at, slots))
        at += slots
    return plan


def lane_tiles(value):
    return [value[:, at : at + LANES] for at in range(0, value.shape[1], LANES)]


def masked(refs, key):
    name, step = key
    value = load(refs, name, step)
    if name == "adj_u":
        value = value * load(refs, "wet_u", 2)
    if name == "adj_v":
        value = value * load(refs, "wet_v", 2)
    return value


def start_copies(arrays, held, sems, window, names=NAMES):
    copies = {}
    for number, name in enumerate(NAMES):
        array = arrays[name]
        if name in names:
            lead = (slice(None),) * (array.ndim - 2)
            source = array.at[lead + window(*array.shape[-2:])]
            copies[name] = pltpu.make_async_copy(source, held[name], sems.at[number])
            copies[name].start()
    return copies


def edge(held, rows):
    return {name: ref.at[(slice(None),) * (ref.ndim - 2) + (rows,)] for name, ref in held.items()}


def pack_edges(*refs):
    arrays = dict(zip(NAMES, refs[:10]))
    held = dict(zip(NAMES, refs[10:20]))
    near, target, sems = refs[20:23]
    even, at_top, _ = place()
    count, rows, width = arrays["adj_h"].shape
    for copy in start_copies(arrays, held, sems, lambda rows, width: (slice(None), slice(None))).values():
        copy.wait()
    low, held = edge(held, pl.ds(0, TILE)), edge(held, pl.ds(rows - TILE, TILE))
    for key, kind, turned, at, slots in row_plan(count):
        here = slice(at, at + slots)
        south, north = masked(low, key)[:slots], masked(held, key)[TILE - slots :]
        near[here, :] = jnp.where(even, north, south)
        target[here, :] = jnp.where(even, south, north)

    @pl.when(at_top)
    def _():
        row = iota((TILE, LANES), 0)
        lane = LANES - 1 - iota((TILE, LANES), 1)
        for key, kind, turned, at, slots in row_plan(count):
            value = masked(held, key)
            sources = [TILE - 1 - slot for slot in range(slots)]
            if kind == 2:
                sources = [TILE - 2 - slot for slot in range(slots - 1)] + [TILE - 1]
            order = jnp.zeros((TILE, LANES), jnp.int32)
            for slot, source in enumerate(sources):
                order = jnp.where(row == slot, source, order)
            pieces = []
            for piece in lane_tiles(value)[::-1]:
                piece = jnp.take_along_axis(piece, lane, axis=1)
                piece = jnp.take_along_axis(piece, order, axis=0)
                if turned:
                    piece = jnp.where(row == slots - 1, piece, -piece) if kind == 2 else -piece
                pieces.append(piece)
            target[at : at + slots, :] = jnp.concatenate(pieces, axis=1)[:slots]


def group_lanes(field, count):
    if field < 3 * count:
        return 0, GROUP * (field // 3) + DEEP * (field % 3)
    static = field - 3 * count
    return static // count, GROUP * (static % count) + 3 * DEEP


def column_fields(count):
    keys = [(NAMES[kind], sens) for sens in range(count) for kind in range(3)] + list(TILES)
    fields = [(key,) + group_lanes(field, count) + (field,) for field, key in enumerate(keys)]
    return sorted(fields, key=lambda entry: entry[1:])


def pack_columns(held, to_west, to_east):
    count, rows, width = held["adj_h"].shape
    lane = iota((rows, LANES), 1)
    for target, first, origin in ((to_west, 0, 0), (to_east, width - LANES, LANES - DEEP)):
        side_held = {name: ref.at[(slice(None),) * (ref.ndim - 1) + (pl.ds(first, LANES),)] for name, ref in held.items()}
        packed = [None, None]
        for key, side, at, _ in column_fields(count):
            value = masked(side_held, key)
            shift = (at - origin) % LANES
            if shift:
                value = pltpu.roll(value, shift, 1)
            packed[side] = value if packed[side] is None else jnp.where(lane >= at, value, packed[side])
        for side in range(2):
            target[:, side * LANES : (side + 1) * LANES] = packed[side]


def merge_rows(one, two, own_west, own_east, halo, halo_static, inner, outer):
    even, at_top, at_bottom = place()
    width = one.shape[1]
    rows = own_west.shape[0]
    count = halo.shape[0] // 3
    lane = iota((TILE, LANES), 1)
    west_inner = lax.axis_index("lon") % 2 == 1
    inner[:rows, :] = jnp.where(west_inner, own_west[...], own_east[...])
    outer[:rows, :] = jnp.where(west_inner, own_east[...], own_west[...])
    field = 0
    tiles = []
    for key, kind, turned, at, slots in row_plan(count):
        here = slice(at, at + slots)
        north = jnp.where(even, one[here, :], two[here, :])
        south = jnp.where(even, two[here, :], one[here, :])
        south = jnp.where(at_bottom, 0.0, south)
        blank = jnp.zeros((DEEP - slots, width), jnp.float32)
        gap = [blank] if slots < DEEP else []
        plain = jnp.concatenate([north] + gap + gap + [south], axis=0)
        values = [plain]
        if kind >= 2 and slots < DEEP:
            fold = ([north[:-1]] if slots > 1 else []) + gap + [north[-1:]] + gap + [south]
            if kind == 3:
                fold = [north[1:], blank, north[:1]] + gap + [south]
                values.append(jnp.where(at_top, jnp.concatenate(fold, axis=0), plain))
            else:
                values = [jnp.where(at_top, jnp.concatenate(fold, axis=0), plain)]
        tiles += values
    tiles.append(jnp.zeros((TILE, width), jnp.float32))
    for field, value in enumerate(tiles):
        if field < halo.shape[0]:
            halo[field] = value
        else:
            halo_static[field - halo.shape[0]] = value
    packed = [[None, None], [None, None]]
    for key, side, start, field in column_fields(count):
        pieces = lane_tiles(tiles[field])
        for way, piece, origin in ((0, pieces[0], 0), (1, pieces[-1], LANES - DEEP)):
            shift = (start - origin) % LANES
            if shift:
                piece = pltpu.roll(piece, shift, 1)
            held = packed[way][side]
            packed[way][side] = piece if held is None else jnp.where(lane >= start, piece, held)
    for side in range(2):
        cols = slice(side * LANES, (side + 1) * LANES)
        west, east = packed[0][side], packed[1][side]
        inner[rows:, cols] = jnp.where(west_inner, west, east)
        outer[rows:, cols] = jnp.where(west_inner, east, west)


def rows_of(tile):
    return slice(tile * TILE, (tile + 1) * TILE)


KEEP, DEPTH, DRAG, VEL = 0, 2, 4, 6
FIRST, LAND, RATIO = 0, 2, 3


def coefficients(field, halo, moving, fixed):
    cells = field(("depth", None), 0)
    cells = jnp.where(cells > 0.0, cells, 1.0)
    height, wide = cells.shape
    row = iota((height, wide), 0)
    stores = [(fixed, (LAND,), 0.5 * field(("land", None), 0))]
    for side, way in enumerate("uv"):
        kind = side + 1
        if side == 0:
            face = 0.5 * (cells + pltpu.roll(cells, wide - 1, 1))
        else:
            face = 0.5 * (cells + pltpu.roll(cells, height - 1, 0))
            if halo is not None:
                face = jnp.where(row == halo * TILE + 3, pltpu.roll(face, DEEP, 0), face)
        inverse = 1.0 / face
        ratio = -field(("drag", kind), kind) * inverse
        wet = [field(("wet_" + way, step), kind) for step in range(3)]
        stores += [(fixed, (RATIO + side,), ratio), (fixed, (FIRST + side,), 0.5 * wet[2])]
        for step in range(3):
            now = field(("traj_" + way, step), kind)
            square = now * now
            speed = jnp.sqrt(square + speed_floor)
            keep = 2.0 + ratio * (speed + square / speed)
            deep = face
            if step > 0:
                mask = 0.5 * wet[step - 1]
                keep, deep = keep * mask, deep * mask
            stores += [
                (moving, (KEEP + side, step), keep),
                (moving, (DEPTH + side, step), deep),
                (moving, (DRAG + side, step), -now * speed * inverse),
                (moving, (VEL + side, step), now),
            ]
    for ref, index, value in stores:
        ref[index] = value


def south_of(values, tile):
    row = iota(values[tile].shape, 0)
    return jnp.where(row == 0, pltpu.roll(values[tile - 1], 1, 0), pltpu.roll(values[tile], 1, 0))


def north_of(values, tile):
    row = iota(values[tile].shape, 0)
    after = values[(tile + 1) % len(values)]
    return jnp.where(row == TILE - 1, pltpu.roll(after, TILE - 1, 0), pltpu.roll(values[tile], TILE - 1, 0))


def march(states, moving, fixed, halo, at_top):
    count = len(states[0][0])
    wide = states[0][0][0].shape[1]
    row = iota((TILE, wide), 0)
    group = range(len(states))

    def east_of(value):
        return pltpu.roll(value, wide - 1, 1)

    def west_of(value):
        return pltpu.roll(value, 1, 1)

    def fold_row(value):
        return jnp.where(at_top & (row == TILE - 1), pltpu.roll(value, DEEP, 0), 0.0)

    high = [list(state[0]) for state in states]
    flow_u, flow_v = [[] for _ in group], [[] for _ in group]
    for tile in range(count):
        here = rows_of(tile)
        first_u, first_v = fixed[FIRST, here, :], fixed[FIRST + 1, here, :]
        for one in group:
            flow_u[one].append(first_u * states[one][1][tile])
            flow_v[one].append(first_v * states[one][2][tile])
    history = []
    for step in (2, 1, 0):
        sea, turns_u, turns_v, next_u, next_v = ([[] for _ in group] for _ in range(5))
        face = [list(flows) for flows in flow_v]
        if halo is not None:
            for one in group:
                face[one][halo - 1] = flow_v[one][halo - 1] - fold_row(flow_v[one][halo])
        for tile in range(count):
            land = fixed[LAND, rows_of(tile), :]
            for one in group:
                high[one][tile] = (
                    high[one][tile]
                    + (flow_u[one][tile] - west_of(flow_u[one][tile]))
                    + (face[one][tile] - south_of(face[one], tile))
                )
                sea[one].append(land * high[one][tile])
        for tile in range(count):
            here = rows_of(tile)
            keep_u, keep_v = moving[KEEP, step, here, :], moving[KEEP + 1, step, here, :]
            deep_u, deep_v = moving[DEPTH, step, here, :], moving[DEPTH + 1, step, here, :]
            for one in group:
                turn_u = east_of(sea[one][tile]) - sea[one][tile]
                turn_v = north_of(sea[one], tile) - sea[one][tile]
                if tile == halo:
                    turn_v = jnp.where(row == 3, -pltpu.roll(turns_v[one][tile - 1], DEEP, 0), turn_v)
                turns_u[one].append(turn_u)
                turns_v[one].append(turn_v)
                next_u[one].append(keep_u * flow_u[one][tile] + deep_u * turn_u)
                next_v[one].append(keep_v * flow_v[one][tile] + deep_v * turn_v)
        history.append((step, flow_u, flow_v, turns_u, turns_v))
        flow_u, flow_v = next_u, next_v

    face_u, face_v, drags = ([[] for _ in group] for _ in range(3))
    for tile in range(count):
        here = rows_of(tile)
        sums = [[0.0] * 4 for _ in group]
        for step, steps_u, steps_v, turns_u, turns_v in history:
            for number, (index, values) in enumerate(
                ((DRAG, steps_u), (DRAG + 1, steps_v), (VEL, turns_u), (VEL + 1, turns_v))
            ):
                factor = moving[index, step, here, :]
                for one in group:
                    sums[one][number] += factor * values[one][tile]
        ratio_u, ratio_v = fixed[RATIO, here, :], fixed[RATIO + 1, here, :]
        for one in group:
            face_u[one].append(ratio_u * sums[one][0] + sums[one][2])
            face_v[one].append(ratio_v * sums[one][1] + sums[one][3])
            drags[one].append(sums[one][0] + sums[one][1])
    outs = []
    for one in group:
        totals = []
        for tile in range(count):
            total = face_u[one][tile] + west_of(face_u[one][tile]) + face_v[one][tile] + south_of(face_v[one], tile)
            if halo is not None and tile == halo - 1:
                total = total + fold_row(face_v[one][halo])
            totals.append(0.5 * total)
        outs.append((high[one], flow_u[one], flow_v[one], totals, drags[one]))
    return outs


STRIP_KEYS = tuple(
    (name, step) for name in ("traj_u", "traj_v", "wet_u", "wet_v") for step in range(3)
) + (("depth", None), ("drag", None), ("land", None))


def spread(packed):
    lane = iota(packed.shape, 1)
    arrays = [packed]
    for shift in (4 * GROUP, 2 * GROUP, GROUP):
        upper = (lane & shift) != 0
        halves = []
        for value in arrays:
            other = pltpu.roll(value, shift, 1)
            halves += [jnp.where(upper, other, value), jnp.where(upper, value, other)]
        arrays = halves
    return arrays


def shared_strips(values):
    strips = []
    for first in range(0, len(values), LANES // GROUP):
        some = values[first : first + LANES // GROUP]
        sides = [spread(packed) for packed in state_strips(some)]
        strips += [jnp.concatenate([sides[0][number], sides[1][number]], axis=1) for number in range(len(some))]
    return strips


def state_strips(values):
    lane = iota(values[0][0].shape, 1)
    sides = []
    for end in (-1, 0):
        strip = None
        for sens, pieces in enumerate(values):
            piece = pltpu.roll(pieces[end], GROUP * sens + GROUP // 2, 1)
            strip = piece if strip is None else jnp.where(lane >= GROUP * sens, piece, strip)
        sides.append(strip)
    return sides


def interior(*refs):
    held = dict(zip(NAMES, refs[:10]))
    results = refs[10:15]
    strips, strips_static, to_west, to_east = refs[15:19]
    moving, fixed = refs[19:21]
    sens_count, rows, width = held["adj_h"].shape
    count = rows // TILE

    def field(key, kind):
        name, step = key
        return (held[name][...] if held[name].ndim == 2 else held[name][step]).astype(jnp.float32)

    coefficients(field, None, moving, fixed)
    for number, strip in enumerate(shared_strips([lane_tiles(field(key, 0)) for key in STRIP_KEYS])):
        strips_static[number] = strip
    pack_columns(held, to_west, to_east)

    def each(turn, carry):
        first = turn * PAIR
        states = [
            tuple([held[name][first + one, rows_of(tile), :] for tile in range(count)] for name in NAMES[:3])
            for one in range(PAIR)
        ]
        for one, values in enumerate(march(states, moving, fixed, None, False)):
            for ref, tiles in zip(results, values):
                for tile in range(count):
                    ref[first + one, rows_of(tile), :] = tiles[tile]
        return carry

    lax.fori_loop(0, sens_count // PAIR, each, 0)
    for kind in range(3):
        values = [lane_tiles(held[NAMES[kind]][sens]) for sens in range(sens_count)]
        strips[kind] = jnp.concatenate(state_strips(values), axis=1)


def row_edges(*refs):
    held = dict(zip(NAMES, refs[:10]))
    halo, halo_static = refs[10:12]
    results = refs[17:22]
    outs = refs[22:27]
    strips, strips_static = refs[27:29]
    moving, fixed, sems = refs[29:32]
    _, at_top, _ = place()
    sens_count, rows, width = held["adj_h"].shape
    row = iota((TILE, width), 0)
    top, bottom = rows // TILE - 1, 0

    def shifted_halo(value, kind):
        if kind == 1:
            return jnp.where(at_top & (row < DEEP), pltpu.roll(value, width - 1, 1), value)
        return value

    def field(key, kind):
        name, step = key
        ref = held[name] if held[name].ndim == 2 else held[name].at[step]
        if key in TILES:
            between = shifted_halo(halo_static[TILES.index(key)], kind)
        else:
            between = jnp.ones((TILE, width), jnp.float32)
        parts = [ref[rows_of(top), :].astype(jnp.float32), between, ref[rows_of(bottom), :].astype(jnp.float32)]
        return jnp.concatenate(parts, axis=0)

    coefficients(field, 1, moving, fixed)

    def each(turn, carry):
        first = turn * PAIR
        states = []
        for one in range(PAIR):
            state = []
            for kind in range(3):
                ref = held[NAMES[kind]]
                between = shifted_halo(halo[3 * (first + one) + kind], kind)
                state.append([ref[first + one, rows_of(top), :], between, ref[first + one, rows_of(bottom), :]])
            states.append(tuple(state))
        for one, values in enumerate(march(states, moving, fixed, 1, at_top)):
            for ref, tiles in zip(results, values):
                ref[first + one, rows - DEEP :, :] = tiles[0][DEEP:]
                ref[first + one, :DEEP, :] = tiles[2][:DEEP]
        for one in range(PAIR):
            for number in range(5):
                middle = (first + one, slice(None), pl.ds(LANES, width - 2 * LANES))
                pltpu.make_async_copy(
                    results[number].at[middle], outs[number].at[middle], sems.at[number]
                ).start()
        return carry

    lax.fori_loop(0, sens_count // PAIR, each, 0)
    state = [
        state_strips([lane_tiles(halo[3 * sens + kind]) for sens in range(sens_count)]) for kind in range(3)
    ]
    static = shared_strips([lane_tiles(halo_static[index]) for index in range(len(TILES))])
    for kind in range(3):
        strips[kind] = jnp.concatenate(state[kind], axis=1)
    for index in range(len(TILES)):
        strips_static[index] = static[index]
    for number in range(5):
        middle = (slice(None), slice(None), pl.ds(LANES, width - 2 * LANES))
        pltpu.make_async_copy(results[number].at[middle], outs[number].at[middle], sems.at[number]).wait()


def column_edges(*refs):
    results = refs[:5]
    strips, strips_static, halo_strips, halo_strips_static, inner, outer = refs[5:11]
    outs = refs[16:21]
    ends, moving, fixed, sems = refs[21:25]
    _, at_top, _ = place()
    sens_count, rows, width = results[0].shape
    count = rows // TILE + 1
    last = count - 1
    half = GROUP // 2
    height = rows + TILE
    lane = iota((height, LANES), 1)
    within = lane & (GROUP - 1)
    row = iota((height, 2 * LANES), 0)

    west_inner = lax.axis_index("lon") % 2 == 1
    from_west = jnp.where(west_inner, inner[...], outer[...])
    from_east = jnp.where(west_inner, outer[...], inner[...])
    beyond = []
    for side in range(2):
        cols = slice(side * LANES, (side + 1) * LANES)
        easts = spread(pltpu.roll(from_east[:, cols], LANES + half - 3 * DEEP, 1))
        wests = spread(pltpu.roll(from_west[:, cols], LANES + DEEP - 3 * DEEP, 1))
        beyond += zip(easts, wests)

    def joined(own, halo_own, east, west, kind):
        own = jnp.concatenate([own, halo_own], axis=0)
        east = jnp.where(within < half, own[:, :LANES], east)
        west = jnp.where(within >= half, own[:, LANES:], west)
        value = jnp.concatenate([east, west], axis=1)
        if kind == 1:
            turned = pltpu.roll(value, 2 * LANES - 1, 1)
            value = jnp.where(at_top & (row >= rows) & (row < rows + DEEP), turned, value)
        return value

    def field(key, kind):
        name, step = key
        own = strips_static[STRIP_KEYS.index((name, None) if name == "drag" else key)]
        if key not in TILES:
            east = west = jnp.ones((height, LANES), jnp.float32)
            return joined(own, jnp.ones((TILE, 2 * LANES), jnp.float32), east, west, kind)
        index = TILES.index(key)
        east, west = beyond[index]
        return joined(own, halo_strips_static[index], east, west, kind)

    coefficients(field, last, moving, fixed)
    state = []
    for kind in range(3):
        east = pltpu.roll(from_east[:, :LANES], (half - DEEP * kind) % LANES, 1)
        west = pltpu.roll(from_west[:, :LANES], (DEEP - DEEP * kind) % LANES, 1)
        value = joined(strips[kind], halo_strips[kind], east, west, kind)
        state.append([value[rows_of(tile), :] for tile in range(count)])
    (values,) = march([tuple(state)], moving, fixed, last, at_top)
    copies = []
    lane = iota((rows, LANES), 1)
    for number in range(5):
        strip = jnp.concatenate(values[number][:last], axis=0)
        for side, first in ((0, width - LANES), (1, 0)):
            inside = lane >= LANES - DEEP if side == 0 else lane < DEEP
            part = strip[:, side * LANES : (side + 1) * LANES]
            merged = []
            for sens in range(sens_count):
                shift = (LANES - half - GROUP * sens) % LANES
                piece = pltpu.roll(part, shift, 1) if shift else part
                merged.append(jnp.where(inside, piece, results[number][sens, :, first : first + LANES]))
            for sens in range(sens_count):
                ends[side, number, sens] = merged[sens]
            copies.append(
                pltpu.make_async_copy(
                    ends.at[side, number], outs[number].at[:, :, pl.ds(first, LANES)], sems.at[side, number]
                )
            )
            copies[-1].start()
    for copy in copies:
        copy.wait()


def on_device(traj_u, traj_v, adj_h, adj_u, adj_v, depth, drag, land, wet_u, wet_v):
    count, rows, width = adj_h.shape
    steps = traj_u.shape[0]
    args = (adj_h, adj_u, adj_v, traj_u, traj_v, wet_u, wet_v, depth, drag, land)
    args = tuple(pltpu.with_memory_space_constraint(arg, pltpu.HBM) for arg in args)

    in_vmem = pl.BlockSpec(memory_space=pltpu.VMEM)
    in_hbm = pl.BlockSpec(memory_space=pl.ANY)
    params = pltpu.CompilerParams(vmem_limit_bytes=VMEM_LIMIT)
    row_pack = jax.ShapeDtypeStruct((message_rows(count), width), jnp.float32)
    *held, one, two = pl.pallas_call(
        pack_edges,
        in_specs=[in_hbm] * len(args),
        out_specs=[in_vmem] * (len(args) + 2),
        out_shape=[jax.ShapeDtypeStruct(arg.shape, arg.dtype) for arg in args] + [row_pack] * 2,
        scratch_shapes=[pltpu.SemaphoreType.DMA((len(args),))],
        compiler_params=params,
        name="pack_edges",
    )(*args)

    lons, lats, subs = (lax.axis_size(axis) for axis in GRID)
    total_rows = lats * subs

    def device(lon, row):
        return lon * total_rows + row

    route = [(device(lon, 0), device(lon ^ 1, 0)) for lon in range(lons)]
    for lon in range(lons):
        for row in range(1, total_rows - 1, 2):
            route += [(device(lon, row), device(lon, row + 1)), (device(lon, row + 1), device(lon, row))]
        route.append((device(lon, total_rows - 1), device(lons - 1 - lon, total_rows - 1)))
    two = lax.ppermute(two, GRID, route)

    one = lax.ppermute(one, "sub", [(core, core ^ 1) for core in range(subs)])

    def shape(*dims):
        return jax.ShapeDtypeStruct(dims, jnp.float32)

    def scratch(tiles, wide):
        return [
            pltpu.VMEM((8, steps, tiles * TILE, wide), jnp.float32),
            pltpu.VMEM((5, tiles * TILE, wide), jnp.float32),
        ]

    state = shape(*adj_h.shape)
    first = pl.pallas_call(
        interior,
        in_specs=[in_vmem] * 10,
        out_specs=[in_vmem] * 9,
        out_shape=[state] * 5
        + [shape(3, rows, 2 * LANES), shape(len(STRIP_KEYS), rows, 2 * LANES)]
        + [shape(rows, 2 * LANES)] * 2,
        scratch_shapes=scratch(rows // TILE, width),
        compiler_params=params,
        name="interior",
    )(*held)
    results, strips, own_columns = first[:5], first[5:7], first[7:]

    full_pack = jax.ShapeDtypeStruct((rows + TILE, 2 * LANES), jnp.float32)
    halo, halo_static, inner, outer = pl.pallas_call(
        merge_rows,
        out_shape=[
            shape(3 * count, TILE, width),
            shape(len(TILES), TILE, width),
            full_pack,
            full_pack,
        ],
        compiler_params=params,
        name="merge_rows",
    )(one, two, *own_columns)
    outer = lax.ppermute(outer, "lon", [(lon, (lon - 1 + 2 * (lon % 2)) % lons) for lon in range(lons)])
    inner = lax.ppermute(inner, "lon", [(lon, lon ^ 1) for lon in range(lons)])

    second = pl.pallas_call(
        row_edges,
        in_specs=[in_vmem] * 17,
        out_specs=[in_vmem] * 5 + [in_hbm] * 5 + [in_vmem] * 2,
        out_shape=[state] * 10 + [shape(3, TILE, 2 * LANES), shape(len(TILES), TILE, 2 * LANES)],
        input_output_aliases={12 + number: number for number in range(5)},
        scratch_shapes=scratch(3, width) + [pltpu.SemaphoreType.DMA((5,))],
        compiler_params=params,
        name="row_edges",
    )(*held, halo, halo_static, *results)
    results, outs, halo_strips = second[:5], second[5:10], second[10:]

    return pl.pallas_call(
        column_edges,
        in_specs=[in_vmem] * 11 + [in_hbm] * 5,
        out_specs=[in_hbm] * 5,
        out_shape=[state] * 5,
        input_output_aliases={11 + number: number for number in range(5)},
        scratch_shapes=[pltpu.VMEM((2, 5, count, rows, LANES), jnp.float32)]
        + scratch(rows // TILE + 1, 2 * LANES)
        + [pltpu.SemaphoreType.DMA((2, 5))],
        compiler_params=params,
        name="column_edges",
    )(*results, *strips, *halo_strips, inner, outer, *outs)


def solution(mesh):
    state = P("case", ROWS, "lon")
    fixed = P(ROWS, "lon")
    return jax.shard_map(
        on_device,
        mesh=mesh,
        in_specs=(state,) * 5 + (fixed,) * 3 + (state,) * 2,
        out_specs=(state,) * 5,
        check_vma=False,
    )
```

```python
import functools

import jax
import jax.numpy as jnp
from jax import lax
from jax.experimental import pallas as pl
from jax.experimental.pallas import tpu as pltpu
from jax.sharding import PartitionSpec as P

time_step = 0.5
gravity = 1.0
speed_floor = 0.01

ROWS = ("lat", "sub")
GRID = ("lon", "lat", "sub")
TILE = 8
LANES = 128
DEEP = 4
GROUP = 16
PAIR = 4
VMEM_LIMIT = 48 * 1024 * 1024


def iota(shape, axis):
    return lax.broadcasted_iota(jnp.int32, shape, axis)


def place():
    row = lax.axis_index("lat") * lax.axis_size("sub") + lax.axis_index("sub")
    last = lax.axis_size("lat") * lax.axis_size("sub") - 1
    return row % 2 == 0, row == last, row == 0


STATE_SLOTS = (3, 3, 4)
SHARED = (
    (("traj_v", 2), 2, 3, True),
    (("traj_v", 1), 2, 2, True),
    (("traj_v", 0), 2, 1, True),
    (("traj_u", 2), 1, 2, True),
    (("traj_u", 1), 1, 1, True),
    (("wet_v", 1), 2, 3, False),
    (("wet_v", 0), 2, 2, False),
    (("wet_u", 1), 1, 2, False),
    (("wet_u", 0), 1, 1, False),
    (("depth", None), 0, 3, False),
    (("drag", None), 3, 3, False),
    (("land", None), 0, 3, False),
)
NAMES = ("adj_h", "adj_u", "adj_v", "traj_u", "traj_v", "wet_u", "wet_v", "depth", "drag", "land")
TILES = tuple(entry[0] for entry in SHARED[:10]) + (("drag", 1), ("drag", 2), ("land", None), ("traj_u", 0))


def load(refs, name, step):
    value = refs[name][...] if step is None or name == "drag" else refs[name][step]
    return value.astype(jnp.float32)


def message_size(count):
    return sum(STATE_SLOTS) * count + sum(entry[2] for entry in SHARED)


def message_rows(count):
    return -(-message_size(count) // TILE) * TILE


def row_plan(count):
    plan, at = [], 0
    for sens in range(count):
        for kind in range(3):
            plan.append(((NAMES[kind], sens), kind, kind > 0, at, STATE_SLOTS[kind]))
            at += STATE_SLOTS[kind]
    for key, kind, slots, turned in SHARED:
        plan.append((key, kind, turned, at, slots))
        at += slots
    return plan


def lane_tiles(value):
    return [value[:, at : at + LANES] for at in range(0, value.shape[1], LANES)]


def masked(refs, key):
    name, step = key
    value = load(refs, name, step)
    if name == "adj_u":
        value = value * load(refs, "wet_u", 2)
    if name == "adj_v":
        value = value * load(refs, "wet_v", 2)
    return value


def start_copies(arrays, held, sems, window, names=NAMES):
    copies = {}
    for number, name in enumerate(NAMES):
        array = arrays[name]
        if name in names:
            lead = (slice(None),) * (array.ndim - 2)
            source = array.at[lead + window(*array.shape[-2:])]
            copies[name] = pltpu.make_async_copy(source, held[name], sems.at[number])
            copies[name].start()
    return copies


def row_window(at_bottom_edge):
    def window(rows, width):
        first = pl.multiple_of(jnp.where(at_bottom_edge, 0, rows - TILE), TILE)
        return pl.ds(first, TILE), slice(None)

    return window


def pack_edge(held, target, from_bottom, count):
    for key, kind, turned, at, slots in row_plan(count):
        value = masked(held, key)
        target[at : at + slots, :] = jnp.where(from_bottom, value[:slots], value[TILE - slots :])


def pack_far(*refs):
    arrays = dict(zip(NAMES, refs[:10]))
    target = refs[10]
    held = dict(zip(NAMES, refs[11:21]))
    even, at_top, _ = place()
    count = arrays["adj_h"].shape[0]
    for copy in start_copies(arrays, held, refs[21], row_window(even)).values():
        copy.wait()

    @pl.when(jnp.logical_not(at_top))
    def _():
        pack_edge(held, target, even, count)

    @pl.when(at_top)
    def _():
        row = iota((TILE, LANES), 0)
        lane = LANES - 1 - iota((TILE, LANES), 1)
        for key, kind, turned, at, slots in row_plan(count):
            value = masked(held, key)
            sources = [TILE - 1 - slot for slot in range(slots)]
            if kind == 2:
                sources = [TILE - 2 - slot for slot in range(slots - 1)] + [TILE - 1]
            order = jnp.zeros((TILE, LANES), jnp.int32)
            for slot, source in enumerate(sources):
                order = jnp.where(row == slot, source, order)
            pieces = []
            for piece in lane_tiles(value)[::-1]:
                piece = jnp.take_along_axis(piece, lane, axis=1)
                piece = jnp.take_along_axis(piece, order, axis=0)
                if turned:
                    piece = jnp.where(row == slots - 1, piece, -piece) if kind == 2 else -piece
                pieces.append(piece)
            target[at : at + slots, :] = jnp.concatenate(pieces, axis=1)[:slots]


def pack_near(*refs):
    args = dict(zip(NAMES, refs[:10]))
    near = refs[11]
    even, _, _ = place()
    count, rows, width = args["adj_h"].shape
    low, high = (
        {name: ref.at[(slice(None),) * (ref.ndim - 2) + (pl.ds(first, TILE),)] for name, ref in args.items()}
        for first in (0, rows - TILE)
    )
    for key, kind, turned, at, slots in row_plan(count):
        near[at : at + slots, :] = jnp.where(even, masked(high, key)[TILE - slots :], masked(low, key)[:slots])


def group_lanes(field, count):
    if field < 3 * count:
        return 0, GROUP * (field // 3) + DEEP * (field % 3)
    static = field - 3 * count
    return static // count, GROUP * (static % count) + 3 * DEEP


def column_fields(count):
    keys = [(NAMES[kind], sens) for sens in range(count) for kind in range(3)] + list(TILES)
    fields = [(key,) + group_lanes(field, count) + (field,) for field, key in enumerate(keys)]
    return sorted(fields, key=lambda entry: entry[1:])


def pack_columns(held, to_west, to_east):
    count, rows, width = held["adj_h"].shape
    lane = iota((rows, LANES), 1)
    for target, first, origin in ((to_west, 0, 0), (to_east, width - LANES, LANES - DEEP)):
        side_held = {name: ref.at[(slice(None),) * (ref.ndim - 1) + (pl.ds(first, LANES),)] for name, ref in held.items()}
        packed = [None, None]
        for key, side, at, _ in column_fields(count):
            value = masked(side_held, key)
            shift = (at - origin) % LANES
            if shift:
                value = pltpu.roll(value, shift, 1)
            packed[side] = value if packed[side] is None else jnp.where(lane >= at, value, packed[side])
        for side in range(2):
            target[:, side * LANES : (side + 1) * LANES] = packed[side]


def merge_rows(one, two, own_west, own_east, halo, halo_static, inner, outer):
    even, at_top, at_bottom = place()
    width = one.shape[1]
    rows = own_west.shape[0]
    count = halo.shape[0] // 3
    lane = iota((TILE, LANES), 1)
    west_inner = lax.axis_index("lon") % 2 == 1
    inner[:rows, :] = jnp.where(west_inner, own_west[...], own_east[...])
    outer[:rows, :] = jnp.where(west_inner, own_east[...], own_west[...])
    field = 0
    tiles = []
    for key, kind, turned, at, slots in row_plan(count):
        here = slice(at, at + slots)
        north = jnp.where(even, one[here, :], two[here, :])
        south = jnp.where(even, two[here, :], one[here, :])
        south = jnp.where(at_bottom, 0.0, south)
        blank = jnp.zeros((DEEP - slots, width), jnp.float32)
        gap = [blank] if slots < DEEP else []
        plain = jnp.concatenate([north] + gap + gap + [south], axis=0)
        values = [plain]
        if kind >= 2 and slots < DEEP:
            fold = ([north[:-1]] if slots > 1 else []) + gap + [north[-1:]] + gap + [south]
            if kind == 3:
                fold = [north[1:], blank, north[:1]] + gap + [south]
                values.append(jnp.where(at_top, jnp.concatenate(fold, axis=0), plain))
            else:
                values = [jnp.where(at_top, jnp.concatenate(fold, axis=0), plain)]
        tiles += values
    tiles.append(jnp.zeros((TILE, width), jnp.float32))
    for field, value in enumerate(tiles):
        if field < halo.shape[0]:
            halo[field] = value
        else:
            halo_static[field - halo.shape[0]] = value
    packed = [[None, None], [None, None]]
    for key, side, start, field in column_fields(count):
        pieces = lane_tiles(tiles[field])
        for way, piece, origin in ((0, pieces[0], 0), (1, pieces[-1], LANES - DEEP)):
            shift = (start - origin) % LANES
            if shift:
                piece = pltpu.roll(piece, shift, 1)
            held = packed[way][side]
            packed[way][side] = piece if held is None else jnp.where(lane >= start, piece, held)
    for side in range(2):
        cols = slice(side * LANES, (side + 1) * LANES)
        west, east = packed[0][side], packed[1][side]
        inner[rows:, cols] = jnp.where(west_inner, west, east)
        outer[rows:, cols] = jnp.where(west_inner, east, west)


def rows_of(tile):
    return slice(tile * TILE, (tile + 1) * TILE)


KEEP, DEPTH, DRAG, VEL = 0, 2, 4, 6
FIRST, LAND, RATIO = 0, 2, 3


def coefficients(field, halo, moving, fixed):
    cells = field(("depth", None), 0)
    cells = jnp.where(cells > 0.0, cells, 1.0)
    height, wide = cells.shape
    row = iota((height, wide), 0)
    stores = [(fixed, (LAND,), 0.5 * field(("land", None), 0))]
    for side, way in enumerate("uv"):
        kind = side + 1
        if side == 0:
            face = 0.5 * (cells + pltpu.roll(cells, wide - 1, 1))
        else:
            face = 0.5 * (cells + pltpu.roll(cells, height - 1, 0))
            if halo is not None:
                face = jnp.where(row == halo * TILE + 3, pltpu.roll(face, DEEP, 0), face)
        inverse = 1.0 / face
        ratio = -field(("drag", kind), kind) * inverse
        wet = [field(("wet_" + way, step), kind) for step in range(3)]
        stores += [(fixed, (RATIO + side,), ratio), (fixed, (FIRST + side,), 0.5 * wet[2])]
        for step in range(3):
            now = field(("traj_" + way, step), kind)
            square = now * now
            speed = jnp.sqrt(square + speed_floor)
            keep = 2.0 + ratio * (speed + square / speed)
            deep = face
            if step > 0:
                mask = 0.5 * wet[step - 1]
                keep, deep = keep * mask, deep * mask
            stores += [
                (moving, (KEEP + side, step), keep),
                (moving, (DEPTH + side, step), deep),
                (moving, (DRAG + side, step), -now * speed * inverse),
                (moving, (VEL + side, step), now),
            ]
    for ref, index, value in stores:
        ref[index] = value


def south_of(values, tile):
    row = iota(values[tile].shape, 0)
    return jnp.where(row == 0, pltpu.roll(values[tile - 1], 1, 0), pltpu.roll(values[tile], 1, 0))


def north_of(values, tile):
    row = iota(values[tile].shape, 0)
    after = values[(tile + 1) % len(values)]
    return jnp.where(row == TILE - 1, pltpu.roll(after, TILE - 1, 0), pltpu.roll(values[tile], TILE - 1, 0))


def march(states, moving, fixed, halo, at_top):
    count = len(states[0][0])
    wide = states[0][0][0].shape[1]
    row = iota((TILE, wide), 0)
    group = range(len(states))

    def east_of(value):
        return pltpu.roll(value, wide - 1, 1)

    def west_of(value):
        return pltpu.roll(value, 1, 1)

    def fold_row(value):
        return jnp.where(at_top & (row == TILE - 1), pltpu.roll(value, DEEP, 0), 0.0)

    high = [list(state[0]) for state in states]
    flow_u, flow_v = [[] for _ in group], [[] for _ in group]
    for tile in range(count):
        here = rows_of(tile)
        first_u, first_v = fixed[FIRST, here, :], fixed[FIRST + 1, here, :]
        for one in group:
            flow_u[one].append(first_u * states[one][1][tile])
            flow_v[one].append(first_v * states[one][2][tile])
    history = []
    for step in (2, 1, 0):
        sea, turns_u, turns_v, next_u, next_v = ([[] for _ in group] for _ in range(5))
        face = [list(flows) for flows in flow_v]
        if halo is not None:
            for one in group:
                face[one][halo - 1] = flow_v[one][halo - 1] - fold_row(flow_v[one][halo])
        for tile in range(count):
            land = fixed[LAND, rows_of(tile), :]
            for one in group:
                high[one][tile] = (
                    high[one][tile]
                    + (flow_u[one][tile] - west_of(flow_u[one][tile]))
                    + (face[one][tile] - south_of(face[one], tile))
                )
                sea[one].append(land * high[one][tile])
        for tile in range(count):
            here = rows_of(tile)
            keep_u, keep_v = moving[KEEP, step, here, :], moving[KEEP + 1, step, here, :]
            deep_u, deep_v = moving[DEPTH, step, here, :], moving[DEPTH + 1, step, here, :]
            for one in group:
                turn_u = east_of(sea[one][tile]) - sea[one][tile]
                turn_v = north_of(sea[one], tile) - sea[one][tile]
                if tile == halo:
                    turn_v = jnp.where(row == 3, -pltpu.roll(turns_v[one][tile - 1], DEEP, 0), turn_v)
                turns_u[one].append(turn_u)
                turns_v[one].append(turn_v)
                next_u[one].append(keep_u * flow_u[one][tile] + deep_u * turn_u)
                next_v[one].append(keep_v * flow_v[one][tile] + deep_v * turn_v)
        history.append((step, flow_u, flow_v, turns_u, turns_v))
        flow_u, flow_v = next_u, next_v

    face_u, face_v, drags = ([[] for _ in group] for _ in range(3))
    for tile in range(count):
        here = rows_of(tile)
        sums = [[0.0] * 4 for _ in group]
        for step, steps_u, steps_v, turns_u, turns_v in history:
            for number, (index, values) in enumerate(
                ((DRAG, steps_u), (DRAG + 1, steps_v), (VEL, turns_u), (VEL + 1, turns_v))
            ):
                factor = moving[index, step, here, :]
                for one in group:
                    sums[one][number] += factor * values[one][tile]
        ratio_u, ratio_v = fixed[RATIO, here, :], fixed[RATIO + 1, here, :]
        for one in group:
            face_u[one].append(ratio_u * sums[one][0] + sums[one][2])
            face_v[one].append(ratio_v * sums[one][1] + sums[one][3])
            drags[one].append(sums[one][0] + sums[one][1])
    outs = []
    for one in group:
        totals = []
        for tile in range(count):
            total = face_u[one][tile] + west_of(face_u[one][tile]) + face_v[one][tile] + south_of(face_v[one], tile)
            if halo is not None and tile == halo - 1:
                total = total + fold_row(face_v[one][halo])
            totals.append(0.5 * total)
        outs.append((high[one], flow_u[one], flow_v[one], totals, drags[one]))
    return outs


STRIP_KEYS = tuple(
    (name, step) for name in ("traj_u", "traj_v", "wet_u", "wet_v") for step in range(3)
) + (("depth", None), ("drag", None), ("land", None))


def spread(packed):
    lane = iota(packed.shape, 1)
    arrays = [packed]
    for shift in (4 * GROUP, 2 * GROUP, GROUP):
        upper = (lane & shift) != 0
        halves = []
        for value in arrays:
            other = pltpu.roll(value, shift, 1)
            halves += [jnp.where(upper, other, value), jnp.where(upper, value, other)]
        arrays = halves
    return arrays


def shared_strips(values):
    strips = []
    for first in range(0, len(values), LANES // GROUP):
        some = values[first : first + LANES // GROUP]
        sides = [spread(packed) for packed in state_strips(some)]
        strips += [jnp.concatenate([sides[0][number], sides[1][number]], axis=1) for number in range(len(some))]
    return strips


def state_strips(values):
    lane = iota(values[0][0].shape, 1)
    sides = []
    for end in (-1, 0):
        strip = None
        for sens, pieces in enumerate(values):
            piece = pltpu.roll(pieces[end], GROUP * sens + GROUP // 2, 1)
            strip = piece if strip is None else jnp.where(lane >= GROUP * sens, piece, strip)
        sides.append(strip)
    return sides


def interior(*refs):
    held = dict(zip(NAMES, refs[:10]))
    results = refs[10:15]
    strips, strips_static, to_west, to_east = refs[15:19]
    moving, fixed = refs[19:21]
    sens_count, rows, width = held["adj_h"].shape
    count = rows // TILE

    def field(key, kind):
        name, step = key
        return (held[name][...] if held[name].ndim == 2 else held[name][step]).astype(jnp.float32)

    coefficients(field, None, moving, fixed)
    for number, strip in enumerate(shared_strips([lane_tiles(field(key, 0)) for key in STRIP_KEYS])):
        strips_static[number] = strip
    pack_columns(held, to_west, to_east)

    def each(turn, carry):
        first = turn * PAIR
        states = [
            tuple([held[name][first + one, rows_of(tile), :] for tile in range(count)] for name in NAMES[:3])
            for one in range(PAIR)
        ]
        for one, values in enumerate(march(states, moving, fixed, None, False)):
            for ref, tiles in zip(results, values):
                for tile in range(count):
                    ref[first + one, rows_of(tile), :] = tiles[tile]
        return carry

    lax.fori_loop(0, sens_count // PAIR, each, 0)
    for kind in range(3):
        values = [lane_tiles(held[NAMES[kind]][sens]) for sens in range(sens_count)]
        strips[kind] = jnp.concatenate(state_strips(values), axis=1)


def row_edges(*refs):
    held = dict(zip(NAMES, refs[:10]))
    halo, halo_static = refs[10:12]
    results = refs[17:22]
    outs = refs[22:27]
    strips, strips_static = refs[27:29]
    moving, fixed, sems = refs[29:32]
    _, at_top, _ = place()
    sens_count, rows, width = held["adj_h"].shape
    row = iota((TILE, width), 0)
    top, bottom = rows // TILE - 1, 0

    def shifted_halo(value, kind):
        if kind == 1:
            return jnp.where(at_top & (row < DEEP), pltpu.roll(value, width - 1, 1), value)
        return value

    def field(key, kind):
        name, step = key
        ref = held[name] if held[name].ndim == 2 else held[name].at[step]
        if key in TILES:
            between = shifted_halo(halo_static[TILES.index(key)], kind)
        else:
            between = jnp.ones((TILE, width), jnp.float32)
        parts = [ref[rows_of(top), :].astype(jnp.float32), between, ref[rows_of(bottom), :].astype(jnp.float32)]
        return jnp.concatenate(parts, axis=0)

    coefficients(field, 1, moving, fixed)

    def each(turn, carry):
        first = turn * PAIR
        states = []
        for one in range(PAIR):
            state = []
            for kind in range(3):
                ref = held[NAMES[kind]]
                between = shifted_halo(halo[3 * (first + one) + kind], kind)
                state.append([ref[first + one, rows_of(top), :], between, ref[first + one, rows_of(bottom), :]])
            states.append(tuple(state))
        for one, values in enumerate(march(states, moving, fixed, 1, at_top)):
            for ref, tiles in zip(results, values):
                ref[first + one, rows - DEEP :, :] = tiles[0][DEEP:]
                ref[first + one, :DEEP, :] = tiles[2][:DEEP]
        for one in range(PAIR):
            for number in range(5):
                middle = (first + one, slice(None), pl.ds(LANES, width - 2 * LANES))
                pltpu.make_async_copy(
                    results[number].at[middle], outs[number].at[middle], sems.at[number]
                ).start()
        return carry

    lax.fori_loop(0, sens_count // PAIR, each, 0)
    state = [
        state_strips([lane_tiles(halo[3 * sens + kind]) for sens in range(sens_count)]) for kind in range(3)
    ]
    static = shared_strips([lane_tiles(halo_static[index]) for index in range(len(TILES))])
    for kind in range(3):
        strips[kind] = jnp.concatenate(state[kind], axis=1)
    for index in range(len(TILES)):
        strips_static[index] = static[index]
    for number in range(5):
        middle = (slice(None), slice(None), pl.ds(LANES, width - 2 * LANES))
        pltpu.make_async_copy(results[number].at[middle], outs[number].at[middle], sems.at[number]).wait()


def column_edges(*refs):
    results = refs[:5]
    strips, strips_static, halo_strips, halo_strips_static, inner, outer = refs[5:11]
    outs = refs[16:21]
    ends, moving, fixed, sems = refs[21:25]
    _, at_top, _ = place()
    sens_count, rows, width = results[0].shape
    count = rows // TILE + 1
    last = count - 1
    half = GROUP // 2
    height = rows + TILE
    lane = iota((height, LANES), 1)
    within = lane & (GROUP - 1)
    row = iota((height, 2 * LANES), 0)

    west_inner = lax.axis_index("lon") % 2 == 1
    from_west = jnp.where(west_inner, inner[...], outer[...])
    from_east = jnp.where(west_inner, outer[...], inner[...])
    beyond = []
    for side in range(2):
        cols = slice(side * LANES, (side + 1) * LANES)
        easts = spread(pltpu.roll(from_east[:, cols], LANES + half - 3 * DEEP, 1))
        wests = spread(pltpu.roll(from_west[:, cols], LANES + DEEP - 3 * DEEP, 1))
        beyond += zip(easts, wests)

    def joined(own, halo_own, east, west, kind):
        own = jnp.concatenate([own, halo_own], axis=0)
        east = jnp.where(within < half, own[:, :LANES], east)
        west = jnp.where(within >= half, own[:, LANES:], west)
        value = jnp.concatenate([east, west], axis=1)
        if kind == 1:
            turned = pltpu.roll(value, 2 * LANES - 1, 1)
            value = jnp.where(at_top & (row >= rows) & (row < rows + DEEP), turned, value)
        return value

    def field(key, kind):
        name, step = key
        own = strips_static[STRIP_KEYS.index((name, None) if name == "drag" else key)]
        if key not in TILES:
            east = west = jnp.ones((height, LANES), jnp.float32)
            return joined(own, jnp.ones((TILE, 2 * LANES), jnp.float32), east, west, kind)
        index = TILES.index(key)
        east, west = beyond[index]
        return joined(own, halo_strips_static[index], east, west, kind)

    coefficients(field, last, moving, fixed)
    state = []
    for kind in range(3):
        east = pltpu.roll(from_east[:, :LANES], (half - DEEP * kind) % LANES, 1)
        west = pltpu.roll(from_west[:, :LANES], (DEEP - DEEP * kind) % LANES, 1)
        value = joined(strips[kind], halo_strips[kind], east, west, kind)
        state.append([value[rows_of(tile), :] for tile in range(count)])
    (values,) = march([tuple(state)], moving, fixed, last, at_top)
    copies = []
    lane = iota((rows, LANES), 1)
    for number in range(5):
        strip = jnp.concatenate(values[number][:last], axis=0)
        for side, first in ((0, width - LANES), (1, 0)):
            inside = lane >= LANES - DEEP if side == 0 else lane < DEEP
            part = strip[:, side * LANES : (side + 1) * LANES]
            merged = []
            for sens in range(sens_count):
                shift = (LANES - half - GROUP * sens) % LANES
                piece = pltpu.roll(part, shift, 1) if shift else part
                merged.append(jnp.where(inside, piece, results[number][sens, :, first : first + LANES]))
            for sens in range(sens_count):
                ends[side, number, sens] = merged[sens]
            copies.append(
                pltpu.make_async_copy(
                    ends.at[side, number], outs[number].at[:, :, pl.ds(first, LANES)], sems.at[side, number]
                )
            )
            copies[-1].start()
    for copy in copies:
        copy.wait()


def on_device(traj_u, traj_v, adj_h, adj_u, adj_v, depth, drag, land, wet_u, wet_v):
    count, rows, width = adj_h.shape
    steps = traj_u.shape[0]
    args = (adj_h, adj_u, adj_v, traj_u, traj_v, wet_u, wet_v, depth, drag, land)
    in_hbm_args = tuple(pltpu.with_memory_space_constraint(arg, pltpu.HBM) for arg in args)

    in_vmem = pl.BlockSpec(memory_space=pltpu.VMEM)
    in_hbm = pl.BlockSpec(memory_space=pl.ANY)
    params = pltpu.CompilerParams(vmem_limit_bytes=VMEM_LIMIT)
    row_pack = jax.ShapeDtypeStruct((message_rows(count), width), jnp.float32)
    packed = pl.pallas_call(
        pack_far,
        in_specs=[in_hbm] * len(args),
        out_specs=in_vmem,
        out_shape=row_pack,
        scratch_shapes=[pltpu.VMEM(arg.shape[:-2] + (TILE, width), arg.dtype) for arg in args]
        + [pltpu.SemaphoreType.DMA((len(args),))],
        compiler_params=params,
        name="pack_far",
    )(*in_hbm_args)

    lons, lats, subs = (lax.axis_size(axis) for axis in GRID)
    total_rows = lats * subs

    def device(lon, row):
        return lon * total_rows + row

    route = [(device(lon, 0), device(lon ^ 1, 0)) for lon in range(lons)]
    for lon in range(lons):
        for row in range(1, total_rows - 1, 2):
            route += [(device(lon, row), device(lon, row + 1)), (device(lon, row + 1), device(lon, row))]
        route.append((device(lon, total_rows - 1), device(lons - 1 - lon, total_rows - 1)))
    two = lax.ppermute(packed, GRID, route)
    one = pl.pallas_call(
        pack_near,
        in_specs=[in_vmem] * len(args) + [in_hbm],
        out_specs=in_vmem,
        out_shape=jax.ShapeDtypeStruct((message_size(count), width), jnp.float32),
        compiler_params=params,
        name="pack_near",
    )(*args, packed)
    one = lax.ppermute(one, "sub", [(core, core ^ 1) for core in range(subs)])


    def shape(*dims):
        return jax.ShapeDtypeStruct(dims, jnp.float32)

    def scratch(tiles, wide):
        return [
            pltpu.VMEM((8, steps, tiles * TILE, wide), jnp.float32),
            pltpu.VMEM((5, tiles * TILE, wide), jnp.float32),
        ]

    state = shape(*adj_h.shape)
    first = pl.pallas_call(
        interior,
        in_specs=[in_vmem] * 10,
        out_specs=[in_vmem] * 9,
        out_shape=[state] * 5
        + [shape(3, rows, 2 * LANES), shape(len(STRIP_KEYS), rows, 2 * LANES)]
        + [shape(rows, 2 * LANES)] * 2,
        scratch_shapes=scratch(rows // TILE, width),
        compiler_params=params,
        name="interior",
    )(*args)
    results, strips, own_columns = first[:5], first[5:7], first[7:]

    full_pack = jax.ShapeDtypeStruct((rows + TILE, 2 * LANES), jnp.float32)
    halo, halo_static, inner, outer = pl.pallas_call(
        merge_rows,
        out_shape=[
            shape(3 * count, TILE, width),
            shape(len(TILES), TILE, width),
            full_pack,
            full_pack,
        ],
        compiler_params=params,
        name="merge_rows",
    )(one, two, *own_columns)
    outer = lax.ppermute(outer, "lon", [(lon, (lon - 1 + 2 * (lon % 2)) % lons) for lon in range(lons)])
    inner = lax.ppermute(inner, "lon", [(lon, lon ^ 1) for lon in range(lons)])

    second = pl.pallas_call(
        row_edges,
        in_specs=[in_vmem] * 17,
        out_specs=[in_vmem] * 5 + [in_hbm] * 5 + [in_vmem] * 2,
        out_shape=[state] * 10 + [shape(3, TILE, 2 * LANES), shape(len(TILES), TILE, 2 * LANES)],
        input_output_aliases={12 + number: number for number in range(5)},
        scratch_shapes=scratch(3, width) + [pltpu.SemaphoreType.DMA((5,))],
        compiler_params=params,
        name="row_edges",
    )(*args, halo, halo_static, *results)
    results, outs, halo_strips = second[:5], second[5:10], second[10:]

    return pl.pallas_call(
        column_edges,
        in_specs=[in_vmem] * 11 + [in_hbm] * 5,
        out_specs=[in_hbm] * 5,
        out_shape=[state] * 5,
        input_output_aliases={11 + number: number for number in range(5)},
        scratch_shapes=[pltpu.VMEM((2, 5, count, rows, LANES), jnp.float32)]
        + scratch(rows // TILE + 1, 2 * LANES)
        + [pltpu.SemaphoreType.DMA((2, 5))],
        compiler_params=params,
        name="column_edges",
    )(*results, *strips, *halo_strips, inner, outer, *outs)


def solution(mesh):
    state = P("case", ROWS, "lon")
    fixed = P(ROWS, "lon")
    return jax.shard_map(
        on_device,
        mesh=mesh,
        in_specs=(state,) * 5 + (fixed,) * 3 + (state,) * 2,
        out_specs=(state,) * 5,
        check_vma=False,
    )
```

```python
import functools

import jax
import jax.numpy as jnp
from jax import lax
from jax.experimental import pallas as pl
from jax.experimental.pallas import tpu as pltpu
from jax.sharding import PartitionSpec as P

time_step = 0.5
gravity = 1.0
speed_floor = 0.01

ROWS = ("lat", "sub")
GRID = ("lon", "lat", "sub")
TILE = 8
LANES = 128
DEEP = 4
GROUP = 16
PAIR = 8
VMEM_LIMIT = 48 * 1024 * 1024


def iota(shape, axis):
    return lax.broadcasted_iota(jnp.int32, shape, axis)


def place():
    row = lax.axis_index("lat") * lax.axis_size("sub") + lax.axis_index("sub")
    last = lax.axis_size("lat") * lax.axis_size("sub") - 1
    return row % 2 == 0, row == last, row == 0


STATE_SLOTS = (3, 3, 4)
SHARED = (
    (("traj_v", 2), 2, 3, True),
    (("traj_v", 1), 2, 2, True),
    (("traj_v", 0), 2, 1, True),
    (("traj_u", 2), 1, 2, True),
    (("traj_u", 1), 1, 1, True),
    (("wet_v", 1), 2, 3, False),
    (("wet_v", 0), 2, 2, False),
    (("wet_u", 1), 1, 2, False),
    (("wet_u", 0), 1, 1, False),
    (("depth", None), 0, 3, False),
    (("drag", None), 3, 3, False),
    (("land", None), 0, 3, False),
)
NAMES = ("adj_h", "adj_u", "adj_v", "traj_u", "traj_v", "wet_u", "wet_v", "depth", "drag", "land")
TILES = tuple(entry[0] for entry in SHARED[:10]) + (("drag", 1), ("drag", 2), ("land", None), ("traj_u", 0))


def load(refs, name, step):
    value = refs[name][...] if step is None or name == "drag" else refs[name][step]
    return value.astype(jnp.float32)


def message_size(count):
    return sum(STATE_SLOTS) * count + sum(entry[2] for entry in SHARED)


def message_rows(count):
    return -(-message_size(count) // TILE) * TILE


def row_plan(count):
    plan, at = [], 0
    for sens in range(count):
        for kind in range(3):
            plan.append(((NAMES[kind], sens), kind, kind > 0, at, STATE_SLOTS[kind]))
            at += STATE_SLOTS[kind]
    for key, kind, slots, turned in SHARED:
        plan.append((key, kind, turned, at, slots))
        at += slots
    return plan


def lane_tiles(value):
    return [value[:, at : at + LANES] for at in range(0, value.shape[1], LANES)]


def masked(refs, key):
    name, step = key
    value = load(refs, name, step)
    if name == "adj_u":
        value = value * load(refs, "wet_u", 2)
    if name == "adj_v":
        value = value * load(refs, "wet_v", 2)
    return value


def start_copies(arrays, held, sems, window, names=NAMES):
    copies = {}
    for number, name in enumerate(NAMES):
        array = arrays[name]
        if name in names:
            lead = (slice(None),) * (array.ndim - 2)
            source = array.at[lead + window(*array.shape[-2:])]
            copies[name] = pltpu.make_async_copy(source, held[name], sems.at[number])
            copies[name].start()
    return copies


def row_window(at_bottom_edge):
    def window(rows, width):
        first = pl.multiple_of(jnp.where(at_bottom_edge, 0, rows - TILE), TILE)
        return pl.ds(first, TILE), slice(None)

    return window


def pack_edge(held, target, from_bottom, count):
    for key, kind, turned, at, slots in row_plan(count):
        value = masked(held, key)
        target[at : at + slots, :] = jnp.where(from_bottom, value[:slots], value[TILE - slots :])


def pack_far(*refs):
    arrays = dict(zip(NAMES, refs[:10]))
    target = refs[10]
    held = dict(zip(NAMES, refs[11:21]))
    even, at_top, _ = place()
    count = arrays["adj_h"].shape[0]
    for copy in start_copies(arrays, held, refs[21], row_window(even)).values():
        copy.wait()

    @pl.when(jnp.logical_not(at_top))
    def _():
        pack_edge(held, target, even, count)

    @pl.when(at_top)
    def _():
        row = iota((TILE, LANES), 0)
        lane = LANES - 1 - iota((TILE, LANES), 1)
        for key, kind, turned, at, slots in row_plan(count):
            value = masked(held, key)
            sources = [TILE - 1 - slot for slot in range(slots)]
            if kind == 2:
                sources = [TILE - 2 - slot for slot in range(slots - 1)] + [TILE - 1]
            order = jnp.zeros((TILE, LANES), jnp.int32)
            for slot, source in enumerate(sources):
                order = jnp.where(row == slot, source, order)
            pieces = []
            for piece in lane_tiles(value)[::-1]:
                piece = jnp.take_along_axis(piece, lane, axis=1)
                piece = jnp.take_along_axis(piece, order, axis=0)
                if turned:
                    piece = jnp.where(row == slots - 1, piece, -piece) if kind == 2 else -piece
                pieces.append(piece)
            target[at : at + slots, :] = jnp.concatenate(pieces, axis=1)[:slots]


def pack_near(*refs):
    args = dict(zip(NAMES, refs[:10]))
    near = refs[11]
    even, _, _ = place()
    count, rows, width = args["adj_h"].shape
    low, high = (
        {name: ref.at[(slice(None),) * (ref.ndim - 2) + (pl.ds(first, TILE),)] for name, ref in args.items()}
        for first in (0, rows - TILE)
    )
    for key, kind, turned, at, slots in row_plan(count):
        near[at : at + slots, :] = jnp.where(even, masked(high, key)[TILE - slots :], masked(low, key)[:slots])


def group_lanes(field, count):
    if field < 3 * count:
        return 0, GROUP * (field // 3) + DEEP * (field % 3)
    static = field - 3 * count
    return static // count, GROUP * (static % count) + 3 * DEEP


def column_fields(count):
    keys = [(NAMES[kind], sens) for sens in range(count) for kind in range(3)] + list(TILES)
    fields = [(key,) + group_lanes(field, count) + (field,) for field, key in enumerate(keys)]
    return sorted(fields, key=lambda entry: entry[1:])


def pack_columns(held, to_west, to_east):
    count, rows, width = held["adj_h"].shape
    lane = iota((rows, LANES), 1)
    for target, first, origin in ((to_west, 0, 0), (to_east, width - LANES, LANES - DEEP)):
        side_held = {name: ref.at[(slice(None),) * (ref.ndim - 1) + (pl.ds(first, LANES),)] for name, ref in held.items()}
        packed = [None, None]
        for key, side, at, _ in column_fields(count):
            value = masked(side_held, key)
            shift = (at - origin) % LANES
            if shift:
                value = pltpu.roll(value, shift, 1)
            packed[side] = value if packed[side] is None else jnp.where(lane >= at, value, packed[side])
        for side in range(2):
            target[:, side * LANES : (side + 1) * LANES] = packed[side]


def merge_rows(one, two, own_west, own_east, halo, halo_static, to_west, to_east):
    even, at_top, at_bottom = place()
    width = one.shape[1]
    rows = own_west.shape[0]
    count = halo.shape[0] // 3
    lane = iota((TILE, LANES), 1)
    to_west[:rows, :] = own_west[...]
    to_east[:rows, :] = own_east[...]
    field = 0
    tiles = []
    for key, kind, turned, at, slots in row_plan(count):
        here = slice(at, at + slots)
        north = jnp.where(even, one[here, :], two[here, :])
        south = jnp.where(even, two[here, :], one[here, :])
        south = jnp.where(at_bottom, 0.0, south)
        blank = jnp.zeros((DEEP - slots, width), jnp.float32)
        gap = [blank] if slots < DEEP else []
        plain = jnp.concatenate([north] + gap + gap + [south], axis=0)
        values = [plain]
        if kind >= 2 and slots < DEEP:
            fold = ([north[:-1]] if slots > 1 else []) + gap + [north[-1:]] + gap + [south]
            if kind == 3:
                fold = [north[1:], blank, north[:1]] + gap + [south]
                values.append(jnp.where(at_top, jnp.concatenate(fold, axis=0), plain))
            else:
                values = [jnp.where(at_top, jnp.concatenate(fold, axis=0), plain)]
        tiles += values
    tiles.append(jnp.zeros((TILE, width), jnp.float32))
    for field, value in enumerate(tiles):
        if field < halo.shape[0]:
            halo[field] = value
        else:
            halo_static[field - halo.shape[0]] = value
    packed = [[None, None], [None, None]]
    for key, side, start, field in column_fields(count):
        pieces = lane_tiles(tiles[field])
        for way, piece, origin in ((0, pieces[0], 0), (1, pieces[-1], LANES - DEEP)):
            shift = (start - origin) % LANES
            if shift:
                piece = pltpu.roll(piece, shift, 1)
            held = packed[way][side]
            packed[way][side] = piece if held is None else jnp.where(lane >= start, piece, held)
    for side in range(2):
        cols = slice(side * LANES, (side + 1) * LANES)
        to_west[rows:, cols] = packed[0][side]
        to_east[rows:, cols] = packed[1][side]


def rows_of(tile):
    return slice(tile * TILE, (tile + 1) * TILE)


KEEP, DEPTH, DRAG, VEL = 0, 2, 4, 6
FIRST, LAND, RATIO = 0, 2, 3


def coefficients(field, halo, moving, fixed):
    cells = field(("depth", None), 0)
    cells = jnp.where(cells > 0.0, cells, 1.0)
    height, wide = cells.shape
    row = iota((height, wide), 0)
    stores = [(fixed, (LAND,), 0.5 * field(("land", None), 0))]
    for side, way in enumerate("uv"):
        kind = side + 1
        if side == 0:
            face = 0.5 * (cells + pltpu.roll(cells, wide - 1, 1))
        else:
            face = 0.5 * (cells + pltpu.roll(cells, height - 1, 0))
            if halo is not None:
                face = jnp.where(row == halo * TILE + 3, pltpu.roll(face, DEEP, 0), face)
        inverse = 1.0 / face
        ratio = -field(("drag", kind), kind) * inverse
        wet = [field(("wet_" + way, step), kind) for step in range(3)]
        stores += [(fixed, (RATIO + side,), ratio), (fixed, (FIRST + side,), 0.5 * wet[2])]
        for step in range(3):
            now = field(("traj_" + way, step), kind)
            square = now * now
            speed = jnp.sqrt(square + speed_floor)
            keep = 2.0 + ratio * (speed + square / speed)
            deep = face
            if step > 0:
                mask = 0.5 * wet[step - 1]
                keep, deep = keep * mask, deep * mask
            stores += [
                (moving, (KEEP + side, step), keep),
                (moving, (DEPTH + side, step), deep),
                (moving, (DRAG + side, step), -now * speed * inverse),
                (moving, (VEL + side, step), now),
            ]
    for ref, index, value in stores:
        ref[index] = value


def south_of(values, tile):
    row = iota(values[tile].shape, 0)
    return jnp.where(row == 0, pltpu.roll(values[tile - 1], 1, 0), pltpu.roll(values[tile], 1, 0))


def north_of(values, tile):
    row = iota(values[tile].shape, 0)
    after = values[(tile + 1) % len(values)]
    return jnp.where(row == TILE - 1, pltpu.roll(after, TILE - 1, 0), pltpu.roll(values[tile], TILE - 1, 0))


def march(states, moving, fixed, halo, at_top):
    count = len(states[0][0])
    wide = states[0][0][0].shape[1]
    row = iota((TILE, wide), 0)
    group = range(len(states))

    def east_of(value):
        return pltpu.roll(value, wide - 1, 1)

    def west_of(value):
        return pltpu.roll(value, 1, 1)

    def fold_row(value):
        return jnp.where(at_top & (row == TILE - 1), pltpu.roll(value, DEEP, 0), 0.0)

    high = [list(state[0]) for state in states]
    flow_u, flow_v = [[] for _ in group], [[] for _ in group]
    for tile in range(count):
        here = rows_of(tile)
        first_u, first_v = fixed[FIRST, here, :], fixed[FIRST + 1, here, :]
        for one in group:
            flow_u[one].append(first_u * states[one][1][tile])
            flow_v[one].append(first_v * states[one][2][tile])
    history = []
    for step in (2, 1, 0):
        sea, turns_u, turns_v, next_u, next_v = ([[] for _ in group] for _ in range(5))
        face = [list(flows) for flows in flow_v]
        if halo is not None:
            for one in group:
                face[one][halo - 1] = flow_v[one][halo - 1] - fold_row(flow_v[one][halo])
        for tile in range(count):
            land = fixed[LAND, rows_of(tile), :]
            for one in group:
                high[one][tile] = (
                    high[one][tile]
                    + (flow_u[one][tile] - west_of(flow_u[one][tile]))
                    + (face[one][tile] - south_of(face[one], tile))
                )
                sea[one].append(land * high[one][tile])
        for tile in range(count):
            here = rows_of(tile)
            keep_u, keep_v = moving[KEEP, step, here, :], moving[KEEP + 1, step, here, :]
            deep_u, deep_v = moving[DEPTH, step, here, :], moving[DEPTH + 1, step, here, :]
            for one in group:
                turn_u = east_of(sea[one][tile]) - sea[one][tile]
                turn_v = north_of(sea[one], tile) - sea[one][tile]
                if tile == halo:
                    turn_v = jnp.where(row == 3, -pltpu.roll(turns_v[one][tile - 1], DEEP, 0), turn_v)
                turns_u[one].append(turn_u)
                turns_v[one].append(turn_v)
                next_u[one].append(keep_u * flow_u[one][tile] + deep_u * turn_u)
                next_v[one].append(keep_v * flow_v[one][tile] + deep_v * turn_v)
        history.append((step, flow_u, flow_v, turns_u, turns_v))
        flow_u, flow_v = next_u, next_v

    face_u, face_v, drags = ([[] for _ in group] for _ in range(3))
    for tile in range(count):
        here = rows_of(tile)
        sums = [[0.0] * 4 for _ in group]
        for step, steps_u, steps_v, turns_u, turns_v in history:
            for number, (index, values) in enumerate(
                ((DRAG, steps_u), (DRAG + 1, steps_v), (VEL, turns_u), (VEL + 1, turns_v))
            ):
                factor = moving[index, step, here, :]
                for one in group:
                    sums[one][number] += factor * values[one][tile]
        ratio_u, ratio_v = fixed[RATIO, here, :], fixed[RATIO + 1, here, :]
        for one in group:
            face_u[one].append(ratio_u * sums[one][0] + sums[one][2])
            face_v[one].append(ratio_v * sums[one][1] + sums[one][3])
            drags[one].append(sums[one][0] + sums[one][1])
    outs = []
    for one in group:
        totals = []
        for tile in range(count):
            total = face_u[one][tile] + west_of(face_u[one][tile]) + face_v[one][tile] + south_of(face_v[one], tile)
            if halo is not None and tile == halo - 1:
                total = total + fold_row(face_v[one][halo])
            totals.append(0.5 * total)
        outs.append((high[one], flow_u[one], flow_v[one], totals, drags[one]))
    return outs


STRIP_KEYS = tuple(
    (name, step) for name in ("traj_u", "traj_v", "wet_u", "wet_v") for step in range(3)
) + (("depth", None), ("drag", None), ("land", None))


def spread(packed):
    lane = iota(packed.shape, 1)
    arrays = [packed]
    for shift in (4 * GROUP, 2 * GROUP, GROUP):
        upper = (lane & shift) != 0
        halves = []
        for value in arrays:
            other = pltpu.roll(value, shift, 1)
            halves += [jnp.where(upper, other, value), jnp.where(upper, value, other)]
        arrays = halves
    return arrays


def shared_strips(values):
    strips = []
    for first in range(0, len(values), LANES // GROUP):
        some = values[first : first + LANES // GROUP]
        sides = [spread(packed) for packed in state_strips(some)]
        strips += [jnp.concatenate([sides[0][number], sides[1][number]], axis=1) for number in range(len(some))]
    return strips


def state_strips(values):
    lane = iota(values[0][0].shape, 1)
    sides = []
    for end in (-1, 0):
        strip = None
        for sens, pieces in enumerate(values):
            piece = pltpu.roll(pieces[end], GROUP * sens + GROUP // 2, 1)
            strip = piece if strip is None else jnp.where(lane >= GROUP * sens, piece, strip)
        sides.append(strip)
    return sides


def interior(*refs):
    held = dict(zip(NAMES, refs[:10]))
    results = refs[10:15]
    strips, strips_static, to_west, to_east = refs[15:19]
    moving, fixed = refs[19:21]
    sens_count, rows, width = held["adj_h"].shape
    count = rows // TILE

    def field(key, kind):
        name, step = key
        return (held[name][...] if held[name].ndim == 2 else held[name][step]).astype(jnp.float32)

    coefficients(field, None, moving, fixed)
    for number, strip in enumerate(shared_strips([lane_tiles(field(key, 0)) for key in STRIP_KEYS])):
        strips_static[number] = strip
    pack_columns(held, to_west, to_east)

    def each(turn, carry):
        first = turn * PAIR
        states = [
            tuple([held[name][first + one, rows_of(tile), :] for tile in range(count)] for name in NAMES[:3])
            for one in range(PAIR)
        ]
        for one, values in enumerate(march(states, moving, fixed, None, False)):
            for ref, tiles in zip(results, values):
                for tile in range(count):
                    ref[first + one, rows_of(tile), :] = tiles[tile]
        return carry

    lax.fori_loop(0, sens_count // PAIR, each, 0)
    for kind in range(3):
        values = [lane_tiles(held[NAMES[kind]][sens]) for sens in range(sens_count)]
        strips[kind] = jnp.concatenate(state_strips(values), axis=1)


def row_edges(*refs):
    held = dict(zip(NAMES, refs[:10]))
    halo, halo_static = refs[10:12]
    results = refs[17:22]
    outs = refs[22:27]
    strips, strips_static = refs[27:29]
    moving, fixed, sems = refs[29:32]
    _, at_top, _ = place()
    sens_count, rows, width = held["adj_h"].shape
    row = iota((TILE, width), 0)
    top, bottom = rows // TILE - 1, 0
    inside = (slice(None), pl.ds(TILE, rows - 2 * TILE), pl.ds(LANES, width - 2 * LANES))
    copies = [
        pltpu.make_async_copy(results[number].at[inside], outs[number].at[inside], sems.at[number])
        for number in range(5)
    ]
    for copy in copies:
        copy.start()

    def shifted_halo(value, kind):
        if kind == 1:
            return jnp.where(at_top & (row < DEEP), pltpu.roll(value, width - 1, 1), value)
        return value

    def field(key, kind):
        name, step = key
        ref = held[name] if held[name].ndim == 2 else held[name].at[step]
        if key in TILES:
            between = shifted_halo(halo_static[TILES.index(key)], kind)
        else:
            between = jnp.ones((TILE, width), jnp.float32)
        parts = [ref[rows_of(top), :].astype(jnp.float32), between, ref[rows_of(bottom), :].astype(jnp.float32)]
        return jnp.concatenate(parts, axis=0)

    coefficients(field, 1, moving, fixed)

    def each(turn, carry):
        first = turn * PAIR
        states = []
        for one in range(PAIR):
            state = []
            for kind in range(3):
                ref = held[NAMES[kind]]
                between = shifted_halo(halo[3 * (first + one) + kind], kind)
                state.append([ref[first + one, rows_of(top), :], between, ref[first + one, rows_of(bottom), :]])
            states.append(tuple(state))
        for one, values in enumerate(march(states, moving, fixed, 1, at_top)):
            for ref, tiles in zip(results, values):
                ref[first + one, rows - DEEP :, :] = tiles[0][DEEP:]
                ref[first + one, :DEEP, :] = tiles[2][:DEEP]
        return carry

    lax.fori_loop(0, sens_count // PAIR, each, 0)
    state = [
        state_strips([lane_tiles(halo[3 * sens + kind]) for sens in range(sens_count)]) for kind in range(3)
    ]
    static = shared_strips([lane_tiles(halo_static[index]) for index in range(len(TILES))])
    for kind in range(3):
        strips[kind] = jnp.concatenate(state[kind], axis=1)
    for index in range(len(TILES)):
        strips_static[index] = static[index]
    for copy in copies:
        copy.wait()


def column_edges(*refs):
    results = refs[:5]
    strips, strips_static, halo_strips, halo_strips_static, from_west_ref, from_east_ref = refs[5:11]
    outs = refs[16:21]
    ends, moving, fixed, sems = refs[21:25]
    _, at_top, _ = place()
    sens_count, rows, width = results[0].shape
    count = rows // TILE + 1
    last = count - 1
    half = GROUP // 2
    height = rows + TILE
    lane = iota((height, LANES), 1)
    within = lane & (GROUP - 1)
    row = iota((height, 2 * LANES), 0)

    copies = []
    for number in range(5):
        for side, first in enumerate((0, rows - TILE)):
            middle = (slice(None), pl.ds(first, TILE), pl.ds(LANES, width - 2 * LANES))
            copies.append(
                pltpu.make_async_copy(results[number].at[middle], outs[number].at[middle], sems.at[2 + side, number])
            )
            copies[-1].start()
    from_west, from_east = from_west_ref[...], from_east_ref[...]
    beyond = []
    for side in range(2):
        cols = slice(side * LANES, (side + 1) * LANES)
        easts = spread(pltpu.roll(from_east[:, cols], LANES + half - 3 * DEEP, 1))
        wests = spread(pltpu.roll(from_west[:, cols], LANES + DEEP - 3 * DEEP, 1))
        beyond += zip(easts, wests)

    def joined(own, halo_own, east, west, kind):
        own = jnp.concatenate([own, halo_own], axis=0)
        east = jnp.where(within < half, own[:, :LANES], east)
        west = jnp.where(within >= half, own[:, LANES:], west)
        value = jnp.concatenate([east, west], axis=1)
        if kind == 1:
            turned = pltpu.roll(value, 2 * LANES - 1, 1)
            value = jnp.where(at_top & (row >= rows) & (row < rows + DEEP), turned, value)
        return value

    def field(key, kind):
        name, step = key
        own = strips_static[STRIP_KEYS.index((name, None) if name == "drag" else key)]
        if key not in TILES:
            east = west = jnp.ones((height, LANES), jnp.float32)
            return joined(own, jnp.ones((TILE, 2 * LANES), jnp.float32), east, west, kind)
        index = TILES.index(key)
        east, west = beyond[index]
        return joined(own, halo_strips_static[index], east, west, kind)

    coefficients(field, last, moving, fixed)
    state = []
    for kind in range(3):
        east = pltpu.roll(from_east[:, :LANES], (half - DEEP * kind) % LANES, 1)
        west = pltpu.roll(from_west[:, :LANES], (DEEP - DEEP * kind) % LANES, 1)
        value = joined(strips[kind], halo_strips[kind], east, west, kind)
        state.append([value[rows_of(tile), :] for tile in range(count)])
    (values,) = march([tuple(state)], moving, fixed, last, at_top)
    lane = iota((rows, LANES), 1)
    for number in range(5):
        strip = jnp.concatenate(values[number][:last], axis=0)
        for side, first in ((0, width - LANES), (1, 0)):
            inside = lane >= LANES - DEEP if side == 0 else lane < DEEP
            part = strip[:, side * LANES : (side + 1) * LANES]
            merged = []
            for sens in range(sens_count):
                shift = (LANES - half - GROUP * sens) % LANES
                piece = pltpu.roll(part, shift, 1) if shift else part
                merged.append(jnp.where(inside, piece, results[number][sens, :, first : first + LANES]))
            for sens in range(sens_count):
                ends[side, number, sens] = merged[sens]
            copies.append(
                pltpu.make_async_copy(
                    ends.at[side, number], outs[number].at[:, :, pl.ds(first, LANES)], sems.at[side, number]
                )
            )
            copies[-1].start()
    for copy in copies:
        copy.wait()


def on_device(traj_u, traj_v, adj_h, adj_u, adj_v, depth, drag, land, wet_u, wet_v):
    count, rows, width = adj_h.shape
    steps = traj_u.shape[0]
    args = (adj_h, adj_u, adj_v, traj_u, traj_v, wet_u, wet_v, depth, drag, land)
    in_hbm_args = tuple(pltpu.with_memory_space_constraint(arg, pltpu.HBM) for arg in args)

    in_vmem = pl.BlockSpec(memory_space=pltpu.VMEM)
    in_hbm = pl.BlockSpec(memory_space=pl.ANY)
    params = pltpu.CompilerParams(vmem_limit_bytes=VMEM_LIMIT)
    row_pack = jax.ShapeDtypeStruct((message_rows(count), width), jnp.float32)
    packed = pl.pallas_call(
        pack_far,
        in_specs=[in_hbm] * len(args),
        out_specs=in_vmem,
        out_shape=row_pack,
        scratch_shapes=[pltpu.VMEM(arg.shape[:-2] + (TILE, width), arg.dtype) for arg in args]
        + [pltpu.SemaphoreType.DMA((len(args),))],
        compiler_params=params,
        name="pack_far",
    )(*in_hbm_args)

    lons, lats, subs = (lax.axis_size(axis) for axis in GRID)
    total_rows = lats * subs

    def device(lon, row):
        return lon * total_rows + row

    route = [(device(lon, 0), device(lon ^ 1, 0)) for lon in range(lons)]
    for lon in range(lons):
        for row in range(1, total_rows - 1, 2):
            route += [(device(lon, row), device(lon, row + 1)), (device(lon, row + 1), device(lon, row))]
        route.append((device(lon, total_rows - 1), device(lons - 1 - lon, total_rows - 1)))
    two = lax.ppermute(packed, GRID, route)
    one = pl.pallas_call(
        pack_near,
        in_specs=[in_vmem] * len(args) + [in_hbm],
        out_specs=in_vmem,
        out_shape=jax.ShapeDtypeStruct((message_size(count), width), jnp.float32),
        compiler_params=params,
        name="pack_near",
    )(*args, packed)
    one = lax.ppermute(one, "sub", [(core, core ^ 1) for core in range(subs)])


    def shape(*dims):
        return jax.ShapeDtypeStruct(dims, jnp.float32)

    def scratch(tiles, wide):
        return [
            pltpu.VMEM((8, steps, tiles * TILE, wide), jnp.float32),
            pltpu.VMEM((5, tiles * TILE, wide), jnp.float32),
        ]

    state = shape(*adj_h.shape)
    first = pl.pallas_call(
        interior,
        in_specs=[in_vmem] * 10,
        out_specs=[in_vmem] * 9,
        out_shape=[state] * 5
        + [shape(3, rows, 2 * LANES), shape(len(STRIP_KEYS), rows, 2 * LANES)]
        + [shape(rows, 2 * LANES)] * 2,
        scratch_shapes=scratch(rows // TILE, width),
        compiler_params=params,
        name="interior",
    )(*args)
    results, strips, own_columns = first[:5], first[5:7], first[7:]

    full_pack = jax.ShapeDtypeStruct((rows + TILE, 2 * LANES), jnp.float32)
    halo, halo_static, to_west, to_east = pl.pallas_call(
        merge_rows,
        out_shape=[
            shape(3 * count, TILE, width),
            shape(len(TILES), TILE, width),
            full_pack,
            full_pack,
        ],
        compiler_params=params,
        name="merge_rows",
    )(one, two, *own_columns)
    from_west = lax.ppermute(to_east, "lon", [(lon, (lon + 1) % lons) for lon in range(lons)])
    from_east = lax.ppermute(to_west, "lon", [(lon, (lon - 1) % lons) for lon in range(lons)])

    second = pl.pallas_call(
        row_edges,
        in_specs=[in_vmem] * 17,
        out_specs=[in_vmem] * 5 + [in_hbm] * 5 + [in_vmem] * 2,
        out_shape=[state] * 10 + [shape(3, TILE, 2 * LANES), shape(len(TILES), TILE, 2 * LANES)],
        input_output_aliases={12 + number: number for number in range(5)},
        scratch_shapes=scratch(3, width) + [pltpu.SemaphoreType.DMA((5,))],
        compiler_params=params,
        name="row_edges",
    )(*args, halo, halo_static, *results)
    results, outs, halo_strips = second[:5], second[5:10], second[10:]

    return pl.pallas_call(
        column_edges,
        in_specs=[in_vmem] * 11 + [in_hbm] * 5,
        out_specs=[in_hbm] * 5,
        out_shape=[state] * 5,
        input_output_aliases={11 + number: number for number in range(5)},
        scratch_shapes=[pltpu.VMEM((2, 5, count, rows, LANES), jnp.float32)]
        + scratch(rows // TILE + 1, 2 * LANES)
        + [pltpu.SemaphoreType.DMA((4, 5))],
        compiler_params=params,
        name="column_edges",
    )(*results, *strips, *halo_strips, from_west, from_east, *outs)


def solution(mesh):
    state = P("case", ROWS, "lon")
    fixed = P(ROWS, "lon")
    return jax.shard_map(
        on_device,
        mesh=mesh,
        in_specs=(state,) * 5 + (fixed,) * 3 + (state,) * 2,
        out_specs=(state,) * 5,
        check_vma=False,
    )
```

```python
import functools

import jax
import jax.numpy as jnp
from jax import lax
from jax.experimental import pallas as pl
from jax.experimental.pallas import tpu as pltpu
from jax.sharding import PartitionSpec as P

time_step = 0.5
gravity = 1.0
speed_floor = 0.01

ROWS = ("lat", "sub")
GRID = ("lon", "lat", "sub")
TILE = 8
LANES = 128
DEEP = 4
GROUP = 16
PAIR = 8
VMEM_LIMIT = 48 * 1024 * 1024


def iota(shape, axis):
    return lax.broadcasted_iota(jnp.int32, shape, axis)


def place():
    row = lax.axis_index("lat") * lax.axis_size("sub") + lax.axis_index("sub")
    last = lax.axis_size("lat") * lax.axis_size("sub") - 1
    return row % 2 == 0, row == last, row == 0


STATE_ROWS = 8
SHARED = (
    (("traj_v", 2), 2, 3, True),
    (("traj_v", 1), 2, 2, True),
    (("traj_v", 0), 2, 1, True),
    (("traj_u", 2), 1, 2, True),
    (("traj_u", 1), 1, 1, True),
    (("wet_v", 1), 2, 3, False),
    (("wet_v", 0), 2, 2, False),
    (("wet_u", 1), 1, 2, False),
    (("wet_u", 0), 1, 1, False),
    (("depth", None), 0, 3, False),
    (("drag", None), 3, 3, False),
    (("land", None), 0, 3, False),
)
NAMES = ("adj_h", "adj_u", "adj_v", "traj_u", "traj_v", "wet_u", "wet_v", "depth", "drag", "land")
TILES = tuple(entry[0] for entry in SHARED[:10]) + (("drag", 1), ("drag", 2), ("land", None), ("traj_u", 0))


def load(refs, name, step):
    value = refs[name][...] if step is None or name == "drag" else refs[name][step]
    return value.astype(jnp.float32)


def message_size(count, width):
    return STATE_ROWS * count + sum(entry[2] for entry in SHARED) + -(-count // (width // LANES))


def message_rows(count, width):
    return -(-message_size(count, width) // TILE) * TILE


def shared_plan(count):
    plan, at = [], STATE_ROWS * count
    for key, kind, slots, turned in SHARED:
        plan.append((key, kind, turned, at, slots))
        at += slots
    return plan, at


def lane_tiles(value):
    return [value[:, at : at + LANES] for at in range(0, value.shape[1], LANES)]


def masked(refs, key):
    name, step = key
    value = load(refs, name, step)
    if name == "adj_u":
        value = value * load(refs, "wet_u", 2)
    if name == "adj_v":
        value = value * load(refs, "wet_v", 2)
    return value


def start_copies(arrays, held, sems, window, names=NAMES):
    copies = {}
    for number, name in enumerate(NAMES):
        array = arrays[name]
        if name in names:
            lead = (slice(None),) * (array.ndim - 2)
            source = array.at[lead + window(*array.shape[-2:])]
            copies[name] = pltpu.make_async_copy(source, held[name], sems.at[number])
            copies[name].start()
    return copies


def row_window(at_bottom_edge):
    def window(rows, width):
        first = pl.multiple_of(jnp.where(at_bottom_edge, 0, rows - TILE), TILE)
        return pl.ds(first, TILE), slice(None)

    return window


LOW, HIGH, FOLD = range(3)


def edge_rows(value, slots, mode, kind=0, turned=False):
    if mode == LOW:
        return [value[:slots]]
    if mode == HIGH:
        return [value[TILE - slots :]]
    if kind == 2:
        order = [TILE - 2 - slot for slot in range(slots - 1)] + [TILE - 1]
    else:
        order = [TILE - 1 - slot for slot in range(slots)]
    picked = [value[source : source + 1] for source in order]
    if turned:
        picked = [-row for row in picked[: slots - 1]] + picked[slots - 1 :] if kind == 2 else [-row for row in picked]
    return picked


def pack_edge(held, target, mode):
    count, _, width = held["adj_h"].shape
    lane = iota((TILE, width), 1)
    across = LANES - 1 - iota((TILE, LANES), 1)
    third = 2 if mode == LOW else TILE - 3

    def mirrored(value):
        if mode != FOLD:
            return value
        rows = []
        for first in range(0, value.shape[0], TILE):
            pieces = lane_tiles(value[first : first + TILE])[::-1]
            rows.append(jnp.concatenate([jnp.take_along_axis(piece, across, axis=1) for piece in pieces], axis=1))
        return jnp.concatenate(rows, axis=0)

    ends = []
    for sens in range(count):
        high, flow_u, flow_v = (masked(held, (name, sens)) for name in NAMES[:3])
        west = jnp.where(lane == 0, 0.0, pltpu.roll(flow_u, 1, 1))
        ahead = high + 0.5 * (flow_u - west + flow_v - pltpu.roll(flow_v, 1, 0))
        rows = edge_rows(high, 2, mode)
        rows += edge_rows(flow_u, 2, mode, 1, True)
        rows += edge_rows(flow_v, 3, mode, 2, True)
        rows.append(ahead[third : third + 1])
        here = slice(STATE_ROWS * sens, STATE_ROWS * (sens + 1))
        target[here, :] = mirrored(jnp.concatenate(rows, axis=0))
        end = flow_u[third : third + 1, width - LANES :]
        ends.append(-end if mode == FOLD else end)
    rows = []
    plan, _ = shared_plan(count)
    for key, kind, turned, at, slots in plan:
        rows += edge_rows(masked(held, key), slots, mode, kind, turned)
    each = width // LANES
    for first in range(0, count, each):
        some = ends[first : first + each]
        blank = [jnp.zeros((1, LANES), jnp.float32)] * (each - len(some))
        rows.append(jnp.concatenate(some + blank, axis=1))
    rows.append(jnp.zeros((message_rows(count, width) - message_size(count, width), width), jnp.float32))
    shared = mirrored(jnp.concatenate([row for row in rows if row.shape[0]], axis=0))
    size = target.shape[0] - STATE_ROWS * count
    target[STATE_ROWS * count :, :] = shared[:size]


def pack_far(*refs):
    arrays = dict(zip(NAMES, refs[:10]))
    target = refs[10]
    held = dict(zip(NAMES, refs[11:21]))
    even, at_top, _ = place()
    for copy in start_copies(arrays, held, refs[21], row_window(even)).values():
        copy.wait()

    @pl.when(even)
    def _():
        pack_edge(held, target, LOW)

    @pl.when(jnp.logical_not(even) & jnp.logical_not(at_top))
    def _():
        pack_edge(held, target, HIGH)

    @pl.when(at_top)
    def _():
        pack_edge(held, target, FOLD)


def pack_near(*refs):
    args = dict(zip(NAMES, refs[:10]))
    near = refs[11]
    even, _, _ = place()
    count, rows, width = args["adj_h"].shape
    low, high = (
        {name: ref.at[(slice(None),) * (ref.ndim - 2) + (pl.ds(first, TILE),)] for name, ref in args.items()}
        for first in (0, rows - TILE)
    )

    @pl.when(even)
    def _():
        pack_edge(high, near, HIGH)

    @pl.when(jnp.logical_not(even))
    def _():
        pack_edge(low, near, LOW)


COLUMN_SLOTS = {
    ("traj_u", 2): (0, 0, 3),
    ("traj_u", 0): (0, 3, 1),
    ("wet_u", 1): (1, 0, 3),
    ("depth", None): (2, 0, 3),
    ("drag", 1): (3, 0, 3),
    ("land", None): (4, 0, 3),
    ("traj_u", 1): (5, 0, 2),
    ("wet_u", 0): (5, 2, 2),
    ("traj_v", 2): (6, 0, 2),
    ("wet_v", 1): (6, 2, 2),
    ("drag", 2): (7, 0, 2),
    ("traj_v", 1): (7, 2, 1),
    ("wet_v", 0): (7, 3, 1),
}


def column_fields(count):
    fields = []
    for sens in range(count):
        for kind in range(3):
            fields.append(((NAMES[kind], sens), GROUP * sens + DEEP * kind, DEEP, 3 * sens + kind))
    for key, (slot, offset, columns) in COLUMN_SLOTS.items():
        fields.append((key, GROUP * slot + 3 * DEEP + offset, columns, 3 * count + TILES.index(key)))
    return sorted(fields, key=lambda entry: entry[1])


def pack_columns(held, to_west, to_east):
    count, rows, width = held["adj_h"].shape
    lane = iota((rows, LANES), 1)
    for target, first, east in ((to_west, 0, False), (to_east, width - LANES, True)):
        side_held = {name: ref.at[(slice(None),) * (ref.ndim - 1) + (pl.ds(first, LANES),)] for name, ref in held.items()}
        packed = None
        for key, start, columns, _ in column_fields(count):
            value = masked(side_held, key)
            shift = (start + columns) % LANES if east else start
            if shift:
                value = pltpu.roll(value, shift, 1)
            packed = value if packed is None else jnp.where(lane >= start, value, packed)
        target[...] = packed


def merge_rows(one, two, own_west, own_east, halo, halo_static, to_west, to_east):
    even, at_top, at_bottom = place()
    width = one.shape[1]
    rows = own_west.shape[0]
    count = halo.shape[0] // 3
    lane = iota((TILE, LANES), 1)
    to_west[:rows, :] = own_west[...]
    to_east[:rows, :] = own_east[...]

    def beyond(here):
        north = jnp.where(even, one[here, :], two[here, :])
        south = jnp.where(even, two[here, :], one[here, :])
        return north, jnp.where(at_bottom, 0.0, south)

    def blank(slots, columns=width):
        return jnp.zeros((slots, columns), jnp.float32)

    plan, ends_at = shared_plan(count)
    each = width // LANES
    tiles, ends = [], []
    for sens in range(count):
        north, south = beyond(slice(STATE_ROWS * sens, STATE_ROWS * (sens + 1)))
        third_north = north[7:8] + 0.5 * north[5:6]
        third_south = south[7:8] - 0.5 * south[4:5]
        fold = jnp.where(at_top, north[6:7], 0.0)
        tiles.append(jnp.concatenate([north[:2], third_north, blank(2), third_south, south[:2]], axis=0))
        tiles.append(jnp.concatenate([north[2:4], blank(4), south[2:4]], axis=0))
        tiles.append(jnp.concatenate([north[4:6], blank(1), fold, blank(1), south[4:7]], axis=0))
        end_north, end_south = beyond(slice(ends_at + sens // each, ends_at + sens // each + 1))
        mine, turned = (slice(number * LANES, (number + 1) * LANES) for number in (sens % each, each - 1 - sens % each))
        end_north = jnp.where(at_top, end_north[:, turned], end_north[:, mine])
        west = [blank(2, LANES), jnp.where(at_top, end_north, 0.0), blank(5, LANES)]
        east = [blank(2, LANES), jnp.where(at_top, 0.0, end_north), blank(2, LANES), end_south[:, mine], blank(2, LANES)]
        ends.append((jnp.concatenate(west, axis=0), jnp.concatenate(east, axis=0)))
    for key, kind, turned, at, slots in plan:
        north, south = beyond(slice(at, at + slots))
        gap = [blank(DEEP - slots)] if slots < DEEP else []
        plain = jnp.concatenate([north] + gap + gap + [south], axis=0)
        values = [plain]
        if kind >= 2 and slots < DEEP:
            fold = ([north[:-1]] if slots > 1 else []) + gap + [north[-1:]] + gap + [south]
            if kind == 3:
                fold = [north[1:], blank(1), north[:1]] + gap + [south]
                values.append(jnp.where(at_top, jnp.concatenate(fold, axis=0), plain))
            else:
                values = [jnp.where(at_top, jnp.concatenate(fold, axis=0), plain)]
        tiles += values
    tiles.append(blank(TILE))
    for field, value in enumerate(tiles):
        if field < halo.shape[0]:
            halo[field] = value
        else:
            halo_static[field - halo.shape[0]] = value
    packed = [None, None]
    for key, start, columns, field in column_fields(count):
        pieces = lane_tiles(tiles[field])
        if field < 3 * count and field % 3 == 1:
            west, east = ends[field // 3]
            pieces = [pieces[0] + west, pieces[-1] + east]
        for way, piece, shift in ((0, pieces[0], start), (1, pieces[-1], (start + columns) % LANES)):
            if shift:
                piece = pltpu.roll(piece, shift, 1)
            packed[way] = piece if packed[way] is None else jnp.where(lane >= start, piece, packed[way])
    to_west[rows:, :] = packed[0]
    to_east[rows:, :] = packed[1]


def rows_of(tile):
    return slice(tile * TILE, (tile + 1) * TILE)


KEEP, DEPTH, DRAG, VEL = 0, 2, 4, 6
FIRST, LAND, RATIO = 0, 2, 3


def coefficients(field, halo, moving, fixed):
    cells = field(("depth", None), 0)
    cells = jnp.where(cells > 0.0, cells, 1.0)
    height, wide = cells.shape
    row = iota((height, wide), 0)
    stores = [(fixed, (LAND,), 0.5 * field(("land", None), 0))]
    for side, way in enumerate("uv"):
        kind = side + 1
        if side == 0:
            face = 0.5 * (cells + pltpu.roll(cells, wide - 1, 1))
        else:
            face = 0.5 * (cells + pltpu.roll(cells, height - 1, 0))
            if halo is not None:
                face = jnp.where(row == halo * TILE + 3, pltpu.roll(face, DEEP, 0), face)
        inverse = 1.0 / face
        ratio = -field(("drag", kind), kind) * inverse
        wet = [field(("wet_" + way, step), kind) for step in range(3)]
        stores += [(fixed, (RATIO + side,), ratio), (fixed, (FIRST + side,), 0.5 * wet[2])]
        for step in range(3):
            now = field(("traj_" + way, step), kind)
            square = now * now
            root = lax.rsqrt(square + speed_floor)
            speed = (square + speed_floor) * root
            keep = 2.0 + ratio * (speed + square * root)
            deep = face
            if step > 0:
                mask = 0.5 * wet[step - 1]
                keep, deep = keep * mask, deep * mask
            stores += [
                (moving, (KEEP + side, step), keep),
                (moving, (DEPTH + side, step), deep),
                (moving, (DRAG + side, step), -now * speed * inverse),
                (moving, (VEL + side, step), now),
            ]
    for ref, index, value in stores:
        ref[index] = value


def south_of(values, tile):
    row = iota(values[tile].shape, 0)
    return jnp.where(row == 0, pltpu.roll(values[tile - 1], 1, 0), pltpu.roll(values[tile], 1, 0))


def north_of(values, tile):
    row = iota(values[tile].shape, 0)
    after = values[(tile + 1) % len(values)]
    return jnp.where(row == TILE - 1, pltpu.roll(after, TILE - 1, 0), pltpu.roll(values[tile], TILE - 1, 0))


def march(states, moving, fixed, halo, at_top):
    count = len(states[0][0])
    wide = states[0][0][0].shape[1]
    row = iota((TILE, wide), 0)
    group = range(len(states))

    def east_of(value):
        return pltpu.roll(value, wide - 1, 1)

    def west_of(value):
        return pltpu.roll(value, 1, 1)

    def fold_row(value):
        return jnp.where(at_top & (row == TILE - 1), pltpu.roll(value, DEEP, 0), 0.0)

    high = [list(state[0]) for state in states]
    flow_u, flow_v = [[] for _ in group], [[] for _ in group]
    for tile in range(count):
        here = rows_of(tile)
        first_u, first_v = fixed[FIRST, here, :], fixed[FIRST + 1, here, :]
        for one in group:
            flow_u[one].append(first_u * states[one][1][tile])
            flow_v[one].append(first_v * states[one][2][tile])
    history = []
    for step in (2, 1, 0):
        sea, turns_u, turns_v, next_u, next_v = ([[] for _ in group] for _ in range(5))
        face = [list(flows) for flows in flow_v]
        if halo is not None:
            for one in group:
                face[one][halo - 1] = flow_v[one][halo - 1] - fold_row(flow_v[one][halo])
        for tile in range(count):
            land = fixed[LAND, rows_of(tile), :]
            for one in group:
                high[one][tile] = (
                    high[one][tile]
                    + (flow_u[one][tile] - west_of(flow_u[one][tile]))
                    + (face[one][tile] - south_of(face[one], tile))
                )
                sea[one].append(land * high[one][tile])
        for tile in range(count):
            here = rows_of(tile)
            keep_u, keep_v = moving[KEEP, step, here, :], moving[KEEP + 1, step, here, :]
            deep_u, deep_v = moving[DEPTH, step, here, :], moving[DEPTH + 1, step, here, :]
            for one in group:
                turn_u = east_of(sea[one][tile]) - sea[one][tile]
                turn_v = north_of(sea[one], tile) - sea[one][tile]
                if tile == halo:
                    turn_v = jnp.where(row == 3, -pltpu.roll(turns_v[one][tile - 1], DEEP, 0), turn_v)
                turns_u[one].append(turn_u)
                turns_v[one].append(turn_v)
                next_u[one].append(keep_u * flow_u[one][tile] + deep_u * turn_u)
                next_v[one].append(keep_v * flow_v[one][tile] + deep_v * turn_v)
        history.append((step, flow_u, flow_v, turns_u, turns_v))
        flow_u, flow_v = next_u, next_v

    face_u, face_v, drags = ([[] for _ in group] for _ in range(3))
    for tile in range(count):
        here = rows_of(tile)
        sums = [[0.0] * 4 for _ in group]
        for step, steps_u, steps_v, turns_u, turns_v in history:
            for number, (index, values) in enumerate(
                ((DRAG, steps_u), (DRAG + 1, steps_v), (VEL, turns_u), (VEL + 1, turns_v))
            ):
                factor = moving[index, step, here, :]
                for one in group:
                    sums[one][number] += factor * values[one][tile]
        ratio_u, ratio_v = fixed[RATIO, here, :], fixed[RATIO + 1, here, :]
        for one in group:
            face_u[one].append(ratio_u * sums[one][0] + sums[one][2])
            face_v[one].append(ratio_v * sums[one][1] + sums[one][3])
            drags[one].append(sums[one][0] + sums[one][1])
    outs = []
    for one in group:
        totals = []
        for tile in range(count):
            total = face_u[one][tile] + west_of(face_u[one][tile]) + face_v[one][tile] + south_of(face_v[one], tile)
            if halo is not None and tile == halo - 1:
                total = total + fold_row(face_v[one][halo])
            totals.append(0.5 * total)
        outs.append((high[one], flow_u[one], flow_v[one], totals, drags[one]))
    return outs


STRIP_KEYS = tuple(
    (name, step) for name in ("traj_u", "traj_v", "wet_u", "wet_v") for step in range(3)
) + (("depth", None), ("drag", None), ("land", None))


def spread(packed):
    lane = iota(packed.shape, 1)
    arrays = [packed]
    for shift in (4 * GROUP, 2 * GROUP, GROUP):
        upper = (lane & shift) != 0
        halves = []
        for value in arrays:
            other = pltpu.roll(value, shift, 1)
            halves += [jnp.where(upper, other, value), jnp.where(upper, value, other)]
        arrays = halves
    return arrays


def shared_strips(values):
    strips = []
    for first in range(0, len(values), LANES // GROUP):
        some = values[first : first + LANES // GROUP]
        sides = [spread(packed) for packed in state_strips(some)]
        strips += [jnp.concatenate([sides[0][number], sides[1][number]], axis=1) for number in range(len(some))]
    return strips


def state_strips(values):
    lane = iota(values[0][0].shape, 1)
    sides = []
    for end in (-1, 0):
        strip = None
        for sens, pieces in enumerate(values):
            piece = pltpu.roll(pieces[end], GROUP * sens + GROUP // 2, 1)
            strip = piece if strip is None else jnp.where(lane >= GROUP * sens, piece, strip)
        sides.append(strip)
    return sides


def interior(*refs):
    held = dict(zip(NAMES, refs[:10]))
    results = refs[10:15]
    strips, strips_static, to_west, to_east = refs[15:19]
    moving, fixed = refs[19:21]
    sens_count, rows, width = held["adj_h"].shape
    count = rows // TILE

    def field(key, kind):
        name, step = key
        return (held[name][...] if held[name].ndim == 2 else held[name][step]).astype(jnp.float32)

    coefficients(field, None, moving, fixed)
    for number, strip in enumerate(shared_strips([lane_tiles(field(key, 0)) for key in STRIP_KEYS])):
        strips_static[number] = strip
    pack_columns(held, to_west, to_east)

    def each(turn, carry):
        first = turn * PAIR
        states = [
            tuple([held[name][first + one, rows_of(tile), :] for tile in range(count)] for name in NAMES[:3])
            for one in range(PAIR)
        ]
        for one, values in enumerate(march(states, moving, fixed, None, False)):
            for ref, tiles in zip(results, values):
                for tile in range(count):
                    ref[first + one, rows_of(tile), :] = tiles[tile]
        return carry

    lax.fori_loop(0, sens_count // PAIR, each, 0)
    for kind in range(3):
        values = [lane_tiles(held[NAMES[kind]][sens]) for sens in range(sens_count)]
        strips[kind] = jnp.concatenate(state_strips(values), axis=1)


def row_edges(*refs):
    held = dict(zip(NAMES, refs[:10]))
    halo, halo_static = refs[10:12]
    results = refs[17:22]
    outs = refs[22:27]
    strips, strips_static = refs[27:29]
    moving, fixed, sems = refs[29:32]
    _, at_top, _ = place()
    sens_count, rows, width = held["adj_h"].shape
    row = iota((TILE, width), 0)
    top, bottom = rows // TILE - 1, 0
    inside = (slice(None), pl.ds(TILE, rows - 2 * TILE), pl.ds(LANES, width - 2 * LANES))
    copies = [
        pltpu.make_async_copy(results[number].at[inside], outs[number].at[inside], sems.at[number])
        for number in range(5)
    ]
    for copy in copies:
        copy.start()

    def shifted_halo(value, kind):
        if kind == 1:
            return jnp.where(at_top & (row < DEEP), pltpu.roll(value, width - 1, 1), value)
        return value

    def field(key, kind):
        name, step = key
        ref = held[name] if held[name].ndim == 2 else held[name].at[step]
        if key in TILES:
            between = shifted_halo(halo_static[TILES.index(key)], kind)
        else:
            between = jnp.ones((TILE, width), jnp.float32)
        parts = [ref[rows_of(top), :].astype(jnp.float32), between, ref[rows_of(bottom), :].astype(jnp.float32)]
        return jnp.concatenate(parts, axis=0)

    coefficients(field, 1, moving, fixed)

    def each(turn, carry):
        first = turn * PAIR
        states = []
        for one in range(PAIR):
            state = []
            for kind in range(3):
                ref = held[NAMES[kind]]
                between = shifted_halo(halo[3 * (first + one) + kind], kind)
                state.append([ref[first + one, rows_of(top), :], between, ref[first + one, rows_of(bottom), :]])
            states.append(tuple(state))
        for one, values in enumerate(march(states, moving, fixed, 1, at_top)):
            for ref, tiles in zip(results, values):
                ref[first + one, rows - DEEP :, :] = tiles[0][DEEP:]
                ref[first + one, :DEEP, :] = tiles[2][:DEEP]
        return carry

    lax.fori_loop(0, sens_count // PAIR, each, 0)
    state = [
        state_strips([lane_tiles(halo[3 * sens + kind]) for sens in range(sens_count)]) for kind in range(3)
    ]
    static = shared_strips([lane_tiles(halo_static[index]) for index in range(len(TILES))])
    for kind in range(3):
        strips[kind] = jnp.concatenate(state[kind], axis=1)
    for index in range(len(TILES)):
        strips_static[index] = static[index]
    for copy in copies:
        copy.wait()


def column_edges(*refs):
    results = refs[:5]
    strips, strips_static, halo_strips, halo_strips_static, from_west_ref, from_east_ref = refs[5:11]
    outs = refs[16:21]
    ends, moving, fixed, sems = refs[21:25]
    _, at_top, _ = place()
    sens_count, rows, width = results[0].shape
    count = rows // TILE + 1
    last = count - 1
    half = GROUP // 2
    height = rows + TILE
    lane = iota((height, LANES), 1)
    within = lane & (GROUP - 1)
    row = iota((height, 2 * LANES), 0)

    copies = []
    for number in range(5):
        for side, first in enumerate((0, rows - TILE)):
            middle = (slice(None), pl.ds(first, TILE), pl.ds(LANES, width - 2 * LANES))
            copies.append(
                pltpu.make_async_copy(results[number].at[middle], outs[number].at[middle], sems.at[2 + side, number])
            )
            copies[-1].start()
    from_west, from_east = from_west_ref[...], from_east_ref[...]
    easts = spread(pltpu.roll(from_east, LANES + half - 3 * DEEP, 1))
    wests = spread(pltpu.roll(from_west, LANES + DEEP - 3 * DEEP, 1))

    def joined(own, halo_own, east, west, kind):
        own = jnp.concatenate([own, halo_own], axis=0)
        east = jnp.where(within < half, own[:, :LANES], east)
        west = jnp.where(within >= half, own[:, LANES:], west)
        value = jnp.concatenate([east, west], axis=1)
        if kind == 1:
            turned = pltpu.roll(value, 2 * LANES - 1, 1)
            value = jnp.where(at_top & (row >= rows) & (row < rows + DEEP), turned, value)
        return value

    def field(key, kind):
        name, step = key
        own = strips_static[STRIP_KEYS.index((name, None) if name == "drag" else key)]
        if key not in TILES:
            east = west = jnp.ones((height, LANES), jnp.float32)
            return joined(own, jnp.ones((TILE, 2 * LANES), jnp.float32), east, west, kind)
        east = west = jnp.zeros((height, LANES), jnp.float32)
        if key in COLUMN_SLOTS:
            slot, offset, columns = COLUMN_SLOTS[key]
            east, west = easts[slot], wests[slot]
            if offset:
                east = pltpu.roll(east, LANES - offset, 1)
            if columns + offset < DEEP:
                west = pltpu.roll(west, DEEP - columns - offset, 1)
        return joined(own, halo_strips_static[TILES.index(key)], east, west, kind)

    coefficients(field, last, moving, fixed)
    state = []
    for kind in range(3):
        east = pltpu.roll(from_east[:, :LANES], (half - DEEP * kind) % LANES, 1)
        west = pltpu.roll(from_west[:, :LANES], (DEEP - DEEP * kind) % LANES, 1)
        value = joined(strips[kind], halo_strips[kind], east, west, kind)
        state.append([value[rows_of(tile), :] for tile in range(count)])
    (values,) = march([tuple(state)], moving, fixed, last, at_top)
    lane = iota((rows, LANES), 1)
    for number in range(5):
        strip = jnp.concatenate(values[number][:last], axis=0)
        for side, first in ((0, width - LANES), (1, 0)):
            inside = lane >= LANES - DEEP if side == 0 else lane < DEEP
            part = strip[:, side * LANES : (side + 1) * LANES]
            merged = []
            for sens in range(sens_count):
                shift = (LANES - half - GROUP * sens) % LANES
                piece = pltpu.roll(part, shift, 1) if shift else part
                merged.append(jnp.where(inside, piece, results[number][sens, :, first : first + LANES]))
            for sens in range(sens_count):
                ends[side, number, sens] = merged[sens]
            copies.append(
                pltpu.make_async_copy(
                    ends.at[side, number], outs[number].at[:, :, pl.ds(first, LANES)], sems.at[side, number]
                )
            )
            copies[-1].start()
    for copy in copies:
        copy.wait()


def on_device(traj_u, traj_v, adj_h, adj_u, adj_v, depth, drag, land, wet_u, wet_v):
    count, rows, width = adj_h.shape
    steps = traj_u.shape[0]
    args = (adj_h, adj_u, adj_v, traj_u, traj_v, wet_u, wet_v, depth, drag, land)
    in_hbm_args = tuple(pltpu.with_memory_space_constraint(arg, pltpu.HBM) for arg in args)

    in_vmem = pl.BlockSpec(memory_space=pltpu.VMEM)
    in_hbm = pl.BlockSpec(memory_space=pl.ANY)
    params = pltpu.CompilerParams(vmem_limit_bytes=VMEM_LIMIT)
    row_pack = jax.ShapeDtypeStruct((message_rows(count, width), width), jnp.float32)
    packed = pl.pallas_call(
        pack_far,
        in_specs=[in_hbm] * len(args),
        out_specs=in_vmem,
        out_shape=row_pack,
        scratch_shapes=[pltpu.VMEM(arg.shape[:-2] + (TILE, width), arg.dtype) for arg in args]
        + [pltpu.SemaphoreType.DMA((len(args),))],
        compiler_params=params,
        name="pack_far",
    )(*in_hbm_args)

    lons, lats, subs = (lax.axis_size(axis) for axis in GRID)
    total_rows = lats * subs

    def device(lon, row):
        return lon * total_rows + row

    route = [(device(lon, 0), device(lon ^ 1, 0)) for lon in range(lons)]
    for lon in range(lons):
        for row in range(1, total_rows - 1, 2):
            route += [(device(lon, row), device(lon, row + 1)), (device(lon, row + 1), device(lon, row))]
        route.append((device(lon, total_rows - 1), device(lons - 1 - lon, total_rows - 1)))
    two = lax.ppermute(packed, GRID, route)
    one = pl.pallas_call(
        pack_near,
        in_specs=[in_vmem] * len(args) + [in_hbm],
        out_specs=in_vmem,
        out_shape=jax.ShapeDtypeStruct((message_size(count, width), width), jnp.float32),
        compiler_params=params,
        name="pack_near",
    )(*args, packed)
    one = lax.ppermute(one, "sub", [(core, core ^ 1) for core in range(subs)])


    def shape(*dims):
        return jax.ShapeDtypeStruct(dims, jnp.float32)

    def scratch(tiles, wide):
        return [
            pltpu.VMEM((8, steps, tiles * TILE, wide), jnp.float32),
            pltpu.VMEM((5, tiles * TILE, wide), jnp.float32),
        ]

    state = shape(*adj_h.shape)
    first = pl.pallas_call(
        interior,
        in_specs=[in_vmem] * 10,
        out_specs=[in_vmem] * 9,
        out_shape=[state] * 5
        + [shape(3, rows, 2 * LANES), shape(len(STRIP_KEYS), rows, 2 * LANES)]
        + [shape(rows, LANES)] * 2,
        scratch_shapes=scratch(rows // TILE, width),
        compiler_params=params,
        name="interior",
    )(*args)
    results, strips, own_columns = first[:5], first[5:7], first[7:]

    full_pack = jax.ShapeDtypeStruct((rows + TILE, LANES), jnp.float32)
    halo, halo_static, to_west, to_east = pl.pallas_call(
        merge_rows,
        out_shape=[
            shape(3 * count, TILE, width),
            shape(len(TILES), TILE, width),
            full_pack,
            full_pack,
        ],
        compiler_params=params,
        name="merge_rows",
    )(one, two, *own_columns)
    from_west = lax.ppermute(to_east, "lon", [(lon, (lon + 1) % lons) for lon in range(lons)])
    from_east = lax.ppermute(to_west, "lon", [(lon, (lon - 1) % lons) for lon in range(lons)])

    second = pl.pallas_call(
        row_edges,
        in_specs=[in_vmem] * 17,
        out_specs=[in_vmem] * 5 + [in_hbm] * 5 + [in_vmem] * 2,
        out_shape=[state] * 10 + [shape(3, TILE, 2 * LANES), shape(len(TILES), TILE, 2 * LANES)],
        input_output_aliases={12 + number: number for number in range(5)},
        scratch_shapes=scratch(3, width) + [pltpu.SemaphoreType.DMA((5,))],
        compiler_params=params,
        name="row_edges",
    )(*args, halo, halo_static, *results)
    results, outs, halo_strips = second[:5], second[5:10], second[10:]

    return pl.pallas_call(
        column_edges,
        in_specs=[in_vmem] * 11 + [in_hbm] * 5,
        out_specs=[in_hbm] * 5,
        out_shape=[state] * 5,
        input_output_aliases={11 + number: number for number in range(5)},
        scratch_shapes=[pltpu.VMEM((2, 5, count, rows, LANES), jnp.float32)]
        + scratch(rows // TILE + 1, 2 * LANES)
        + [pltpu.SemaphoreType.DMA((4, 5))],
        compiler_params=params,
        name="column_edges",
    )(*results, *strips, *halo_strips, from_west, from_east, *outs)


def solution(mesh):
    state = P("case", ROWS, "lon")
    fixed = P(ROWS, "lon")
    return jax.shard_map(
        on_device,
        mesh=mesh,
        in_specs=(state,) * 5 + (fixed,) * 3 + (state,) * 2,
        out_specs=(state,) * 5,
        check_vma=False,
    )
```

```python
import functools

import jax
import jax.numpy as jnp
from jax import lax
from jax.experimental import pallas as pl
from jax.experimental.pallas import tpu as pltpu
from jax.sharding import PartitionSpec as P

time_step = 0.5
gravity = 1.0
speed_floor = 0.01

ROWS = ("lat", "sub")
GRID = ("lon", "lat", "sub")
TILE = 8
LANES = 128
DEEP = 4
GROUP = 16
PAIR = 8
VMEM_LIMIT = 48 * 1024 * 1024


def iota(shape, axis):
    return lax.broadcasted_iota(jnp.int32, shape, axis)


def place():
    row = lax.axis_index("lat") * lax.axis_size("sub") + lax.axis_index("sub")
    last = lax.axis_size("lat") * lax.axis_size("sub") - 1
    return row % 2 == 0, row == last, row == 0


STATE_ROWS = 8
SHARED = (
    (("traj_v", 2), 2, 3, True),
    (("traj_v", 1), 2, 2, True),
    (("traj_v", 0), 2, 1, True),
    (("traj_u", 2), 1, 2, True),
    (("traj_u", 1), 1, 1, True),
    (("wet_v", 1), 2, 3, False),
    (("wet_v", 0), 2, 2, False),
    (("wet_u", 1), 1, 2, False),
    (("wet_u", 0), 1, 1, False),
    (("depth", None), 0, 3, False),
    (("drag", None), 3, 3, False),
    (("land", None), 0, 3, False),
)
NAMES = ("adj_h", "adj_u", "adj_v", "traj_u", "traj_v", "wet_u", "wet_v", "depth", "drag", "land")
TILES = tuple(entry[0] for entry in SHARED[:10]) + (("drag", 1), ("drag", 2), ("land", None), ("traj_u", 0))


def load(refs, name, step):
    value = refs[name][...] if step is None or name == "drag" else refs[name][step]
    return value.astype(jnp.float32)


def message_size(count, width):
    return STATE_ROWS * count + sum(entry[2] for entry in SHARED) + -(-count // (width // LANES))


def message_rows(count, width):
    return -(-message_size(count, width) // TILE) * TILE


def shared_plan(count):
    plan, at = [], STATE_ROWS * count
    for key, kind, slots, turned in SHARED:
        plan.append((key, kind, turned, at, slots))
        at += slots
    return plan, at


def lane_tiles(value):
    return [value[:, at : at + LANES] for at in range(0, value.shape[1], LANES)]


def masked(refs, key):
    name, step = key
    value = load(refs, name, step)
    if name == "adj_u":
        value = value * load(refs, "wet_u", 2)
    if name == "adj_v":
        value = value * load(refs, "wet_v", 2)
    return value


def start_copies(arrays, held, sems, window, names=NAMES):
    copies = {}
    for number, name in enumerate(NAMES):
        array = arrays[name]
        if name in names:
            lead = (slice(None),) * (array.ndim - 2)
            source = array.at[lead + window(*array.shape[-2:])]
            copies[name] = pltpu.make_async_copy(source, held[name], sems.at[number])
            copies[name].start()
    return copies


def row_window(at_bottom_edge):
    def window(rows, width):
        first = pl.multiple_of(jnp.where(at_bottom_edge, 0, rows - TILE), TILE)
        return pl.ds(first, TILE), slice(None)

    return window


LOW, HIGH, FOLD = range(3)


def edge_rows(value, slots, mode, kind=0, turned=False):
    if mode == LOW:
        return [value[:slots]]
    if mode == HIGH:
        return [value[TILE - slots :]]
    if kind == 2:
        order = [TILE - 2 - slot for slot in range(slots - 1)] + [TILE - 1]
    else:
        order = [TILE - 1 - slot for slot in range(slots)]
    picked = [value[source : source + 1] for source in order]
    if turned:
        picked = [-row for row in picked[: slots - 1]] + picked[slots - 1 :] if kind == 2 else [-row for row in picked]
    return picked


def pack_edge(held, target, mode):
    count, _, width = held["adj_h"].shape
    lane = iota((TILE, width), 1)
    across = LANES - 1 - iota((TILE, LANES), 1)
    third = 2 if mode == LOW else TILE - 3

    def mirrored(value):
        if mode != FOLD:
            return value
        rows = []
        for first in range(0, value.shape[0], TILE):
            pieces = lane_tiles(value[first : first + TILE])[::-1]
            rows.append(jnp.concatenate([jnp.take_along_axis(piece, across, axis=1) for piece in pieces], axis=1))
        return jnp.concatenate(rows, axis=0)

    ends = []
    for sens in range(count):
        high, flow_u, flow_v = (masked(held, (name, sens)) for name in NAMES[:3])
        west = jnp.where(lane == 0, 0.0, pltpu.roll(flow_u, 1, 1))
        ahead = high + 0.5 * (flow_u - west + flow_v - pltpu.roll(flow_v, 1, 0))
        rows = edge_rows(high, 2, mode)
        rows += edge_rows(flow_u, 2, mode, 1, True)
        rows += edge_rows(flow_v, 3, mode, 2, True)
        rows.append(ahead[third : third + 1])
        here = slice(STATE_ROWS * sens, STATE_ROWS * (sens + 1))
        target[here, :] = mirrored(jnp.concatenate(rows, axis=0))
        end = flow_u[third : third + 1, width - LANES :]
        ends.append(-end if mode == FOLD else end)
    rows = []
    plan, _ = shared_plan(count)
    for key, kind, turned, at, slots in plan:
        rows += edge_rows(masked(held, key), slots, mode, kind, turned)
    each = width // LANES
    for first in range(0, count, each):
        some = ends[first : first + each]
        blank = [jnp.zeros((1, LANES), jnp.float32)] * (each - len(some))
        rows.append(jnp.concatenate(some + blank, axis=1))
    rows.append(jnp.zeros((message_rows(count, width) - message_size(count, width), width), jnp.float32))
    shared = mirrored(jnp.concatenate([row for row in rows if row.shape[0]], axis=0))
    size = target.shape[0] - STATE_ROWS * count
    target[STATE_ROWS * count :, :] = shared[:size]


def pack_far(*refs):
    arrays = dict(zip(NAMES, refs[:10]))
    target = refs[10]
    held = dict(zip(NAMES, refs[11:21]))
    even, at_top, _ = place()
    for copy in start_copies(arrays, held, refs[21], row_window(even)).values():
        copy.wait()

    @pl.when(even)
    def _():
        pack_edge(held, target, LOW)

    @pl.when(jnp.logical_not(even) & jnp.logical_not(at_top))
    def _():
        pack_edge(held, target, HIGH)

    @pl.when(at_top)
    def _():
        pack_edge(held, target, FOLD)


def pack_near(*refs):
    args = dict(zip(NAMES, refs[:10]))
    near = refs[11]
    even, _, _ = place()
    count, rows, width = args["adj_h"].shape
    low, high = (
        {name: ref.at[(slice(None),) * (ref.ndim - 2) + (pl.ds(first, TILE),)] for name, ref in args.items()}
        for first in (0, rows - TILE)
    )

    @pl.when(even)
    def _():
        pack_edge(high, near, HIGH)

    @pl.when(jnp.logical_not(even))
    def _():
        pack_edge(low, near, LOW)


COLUMN_SLOTS = {
    ("traj_u", 2): (0, 0, 3),
    ("traj_u", 0): (0, 3, 1),
    ("wet_u", 1): (1, 0, 3),
    ("depth", None): (2, 0, 3),
    ("drag", 1): (3, 0, 3),
    ("land", None): (4, 0, 3),
    ("traj_u", 1): (5, 0, 2),
    ("wet_u", 0): (5, 2, 2),
    ("traj_v", 2): (6, 0, 2),
    ("wet_v", 1): (6, 2, 2),
    ("drag", 2): (7, 0, 2),
    ("traj_v", 1): (7, 2, 1),
    ("wet_v", 0): (7, 3, 1),
}


def column_fields(count):
    fields = []
    for sens in range(count):
        for kind in range(3):
            fields.append(((NAMES[kind], sens), GROUP * sens + DEEP * kind, DEEP, 3 * sens + kind))
    for key, (slot, offset, columns) in COLUMN_SLOTS.items():
        fields.append((key, GROUP * slot + 3 * DEEP + offset, columns, 3 * count + TILES.index(key)))
    return sorted(fields, key=lambda entry: entry[1])


def pack_columns(held, to_west, to_east):
    count, rows, width = held["adj_h"].shape
    lane = iota((rows, LANES), 1)
    for target, first, east in ((to_west, 0, False), (to_east, width - LANES, True)):
        side_held = {name: ref.at[(slice(None),) * (ref.ndim - 1) + (pl.ds(first, LANES),)] for name, ref in held.items()}
        packed = None
        for key, start, columns, _ in column_fields(count):
            value = masked(side_held, key)
            shift = (start + columns) % LANES if east else start
            if shift:
                value = pltpu.roll(value, shift, 1)
            packed = value if packed is None else jnp.where(lane >= start, value, packed)
        target[...] = packed


def received(one, two):
    even, at_top, at_bottom = place()

    def beyond(here):
        north = jnp.where(even, one[here, :], two[here, :])
        south = jnp.where(even, two[here, :], one[here, :])
        return north, jnp.where(at_bottom, 0.0, south)

    return beyond


def blank(slots, columns):
    return jnp.zeros((slots, columns), jnp.float32)


def halo_tiles(one, two, count):
    _, at_top, _ = place()
    width = one.shape[1]
    beyond = received(one, two)
    plan, _ = shared_plan(count)
    tiles = []
    for sens in range(count):
        north, south = beyond(slice(STATE_ROWS * sens, STATE_ROWS * (sens + 1)))
        third_north = north[7:8] + 0.5 * north[5:6]
        third_south = south[7:8] - 0.5 * south[4:5]
        fold = jnp.where(at_top, north[6:7], 0.0)
        tiles.append(jnp.concatenate([north[:2], third_north, blank(2, width), third_south, south[:2]], axis=0))
        tiles.append(jnp.concatenate([north[2:4], blank(4, width), south[2:4]], axis=0))
        tiles.append(jnp.concatenate([north[4:6], blank(1, width), fold, blank(1, width), south[4:7]], axis=0))
    for key, kind, turned, at, slots in plan:
        north, south = beyond(slice(at, at + slots))
        gap = [blank(DEEP - slots, width)] if slots < DEEP else []
        plain = jnp.concatenate([north] + gap + gap + [south], axis=0)
        values = [plain]
        if kind >= 2 and slots < DEEP:
            fold = ([north[:-1]] if slots > 1 else []) + gap + [north[-1:]] + gap + [south]
            if kind == 3:
                fold = [north[1:], blank(1, width), north[:1]] + gap + [south]
                values.append(jnp.where(at_top, jnp.concatenate(fold, axis=0), plain))
            else:
                values = [jnp.where(at_top, jnp.concatenate(fold, axis=0), plain)]
        tiles += values
    tiles.append(blank(TILE, width))
    return tiles


def merge_columns(count, one, two, own_west, own_east, to_west, to_east):
    _, at_top, _ = place()
    width = one.shape[1]
    rows = own_west.shape[0]
    lane = iota((TILE, LANES), 1)
    to_west[:rows, :] = own_west[...]
    to_east[:rows, :] = own_east[...]
    tiles = halo_tiles(
        *(jnp.concatenate([ref[:, :LANES], ref[:, width - LANES :]], axis=1) for ref in (one, two)), count
    )
    beyond = received(one, two)
    each = width // LANES
    _, ends_at = shared_plan(count)
    ends = []
    for sens in range(count):
        end_north, end_south = beyond(slice(ends_at + sens // each, ends_at + sens // each + 1))
        mine, turned = (slice(number * LANES, (number + 1) * LANES) for number in (sens % each, each - 1 - sens % each))
        end_north = jnp.where(at_top, end_north[:, turned], end_north[:, mine])
        west = [blank(2, LANES), jnp.where(at_top, end_north, 0.0), blank(5, LANES)]
        east = [blank(2, LANES), jnp.where(at_top, 0.0, end_north), blank(2, LANES), end_south[:, mine], blank(2, LANES)]
        ends.append((jnp.concatenate(west, axis=0), jnp.concatenate(east, axis=0)))
    packed = [None, None]
    for key, start, columns, field in column_fields(count):
        pieces = lane_tiles(tiles[field])
        if field < 3 * count and field % 3 == 1:
            west, east = ends[field // 3]
            pieces = [pieces[0] + west, pieces[-1] + east]
        for way, piece, shift in ((0, pieces[0], start), (1, pieces[-1], (start + columns) % LANES)):
            if shift:
                piece = pltpu.roll(piece, shift, 1)
            packed[way] = piece if packed[way] is None else jnp.where(lane >= start, piece, packed[way])
    to_west[rows:, :] = packed[0]
    to_east[rows:, :] = packed[1]


def rows_of(tile):
    return slice(tile * TILE, (tile + 1) * TILE)


KEEP, DEPTH, DRAG, VEL = 0, 2, 4, 6
FIRST, LAND, RATIO = 0, 2, 3


def coefficients(field, halo, moving, fixed):
    cells = field(("depth", None), 0)
    cells = jnp.where(cells > 0.0, cells, 1.0)
    height, wide = cells.shape
    row = iota((height, wide), 0)
    stores = [(fixed, (LAND,), 0.5 * field(("land", None), 0))]
    for side, way in enumerate("uv"):
        kind = side + 1
        if side == 0:
            face = 0.5 * (cells + pltpu.roll(cells, wide - 1, 1))
        else:
            face = 0.5 * (cells + pltpu.roll(cells, height - 1, 0))
            if halo is not None:
                face = jnp.where(row == halo * TILE + 3, pltpu.roll(face, DEEP, 0), face)
        inverse = 1.0 / face
        ratio = -field(("drag", kind), kind) * inverse
        wet = [field(("wet_" + way, step), kind) for step in range(3)]
        stores += [(fixed, (RATIO + side,), ratio), (fixed, (FIRST + side,), 0.5 * wet[2])]
        for step in range(3):
            now = field(("traj_" + way, step), kind)
            square = now * now
            root = lax.rsqrt(square + speed_floor)
            speed = (square + speed_floor) * root
            keep = 2.0 + ratio * (speed + square * root)
            deep = face
            if step > 0:
                mask = 0.5 * wet[step - 1]
                keep, deep = keep * mask, deep * mask
            stores += [
                (moving, (KEEP + side, step), keep),
                (moving, (DEPTH + side, step), deep),
                (moving, (DRAG + side, step), -now * speed * inverse),
                (moving, (VEL + side, step), now),
            ]
    for ref, index, value in stores:
        ref[index] = value


def south_of(values, tile):
    row = iota(values[tile].shape, 0)
    return jnp.where(row == 0, pltpu.roll(values[tile - 1], 1, 0), pltpu.roll(values[tile], 1, 0))


def north_of(values, tile):
    row = iota(values[tile].shape, 0)
    after = values[(tile + 1) % len(values)]
    return jnp.where(row == TILE - 1, pltpu.roll(after, TILE - 1, 0), pltpu.roll(values[tile], TILE - 1, 0))


def march(states, moving, fixed, halo, at_top):
    count = len(states[0][0])
    wide = states[0][0][0].shape[1]
    row = iota((TILE, wide), 0)
    group = range(len(states))

    def east_of(value):
        return pltpu.roll(value, wide - 1, 1)

    def west_of(value):
        return pltpu.roll(value, 1, 1)

    def fold_row(value):
        return jnp.where(at_top & (row == TILE - 1), pltpu.roll(value, DEEP, 0), 0.0)

    high = [list(state[0]) for state in states]
    flow_u, flow_v = [[] for _ in group], [[] for _ in group]
    for tile in range(count):
        here = rows_of(tile)
        first_u, first_v = fixed[FIRST, here, :], fixed[FIRST + 1, here, :]
        for one in group:
            flow_u[one].append(first_u * states[one][1][tile])
            flow_v[one].append(first_v * states[one][2][tile])
    history = []
    for step in (2, 1, 0):
        sea, turns_u, turns_v, next_u, next_v = ([[] for _ in group] for _ in range(5))
        face = [list(flows) for flows in flow_v]
        if halo is not None:
            for one in group:
                face[one][halo - 1] = flow_v[one][halo - 1] - fold_row(flow_v[one][halo])
        for tile in range(count):
            land = fixed[LAND, rows_of(tile), :]
            for one in group:
                high[one][tile] = (
                    high[one][tile]
                    + (flow_u[one][tile] - west_of(flow_u[one][tile]))
                    + (face[one][tile] - south_of(face[one], tile))
                )
                sea[one].append(land * high[one][tile])
        for tile in range(count):
            here = rows_of(tile)
            keep_u, keep_v = moving[KEEP, step, here, :], moving[KEEP + 1, step, here, :]
            deep_u, deep_v = moving[DEPTH, step, here, :], moving[DEPTH + 1, step, here, :]
            for one in group:
                turn_u = east_of(sea[one][tile]) - sea[one][tile]
                turn_v = north_of(sea[one], tile) - sea[one][tile]
                if tile == halo:
                    turn_v = jnp.where(row == 3, -pltpu.roll(turns_v[one][tile - 1], DEEP, 0), turn_v)
                turns_u[one].append(turn_u)
                turns_v[one].append(turn_v)
                next_u[one].append(keep_u * flow_u[one][tile] + deep_u * turn_u)
                next_v[one].append(keep_v * flow_v[one][tile] + deep_v * turn_v)
        history.append((step, flow_u, flow_v, turns_u, turns_v))
        flow_u, flow_v = next_u, next_v

    face_u, face_v, drags = ([[] for _ in group] for _ in range(3))
    for tile in range(count):
        here = rows_of(tile)
        sums = [[0.0] * 4 for _ in group]
        for step, steps_u, steps_v, turns_u, turns_v in history:
            for number, (index, values) in enumerate(
                ((DRAG, steps_u), (DRAG + 1, steps_v), (VEL, turns_u), (VEL + 1, turns_v))
            ):
                factor = moving[index, step, here, :]
                for one in group:
                    sums[one][number] += factor * values[one][tile]
        ratio_u, ratio_v = fixed[RATIO, here, :], fixed[RATIO + 1, here, :]
        for one in group:
            face_u[one].append(ratio_u * sums[one][0] + sums[one][2])
            face_v[one].append(ratio_v * sums[one][1] + sums[one][3])
            drags[one].append(sums[one][0] + sums[one][1])
    outs = []
    for one in group:
        totals = []
        for tile in range(count):
            total = face_u[one][tile] + west_of(face_u[one][tile]) + face_v[one][tile] + south_of(face_v[one], tile)
            if halo is not None and tile == halo - 1:
                total = total + fold_row(face_v[one][halo])
            totals.append(0.5 * total)
        outs.append((high[one], flow_u[one], flow_v[one], totals, drags[one]))
    return outs


STRIP_KEYS = tuple(
    (name, step) for name in ("traj_u", "traj_v", "wet_u", "wet_v") for step in range(3)
) + (("depth", None), ("drag", None), ("land", None))


def spread(packed):
    lane = iota(packed.shape, 1)
    arrays = [packed]
    for shift in (4 * GROUP, 2 * GROUP, GROUP):
        upper = (lane & shift) != 0
        halves = []
        for value in arrays:
            other = pltpu.roll(value, shift, 1)
            halves += [jnp.where(upper, other, value), jnp.where(upper, value, other)]
        arrays = halves
    return arrays


def shared_strips(values):
    strips = []
    for first in range(0, len(values), LANES // GROUP):
        some = values[first : first + LANES // GROUP]
        sides = [spread(packed) for packed in state_strips(some)]
        strips += [jnp.concatenate([sides[0][number], sides[1][number]], axis=1) for number in range(len(some))]
    return strips


def state_strips(values):
    lane = iota(values[0][0].shape, 1)
    sides = []
    for end in (-1, 0):
        strip = None
        for sens, pieces in enumerate(values):
            piece = pltpu.roll(pieces[end], GROUP * sens + GROUP // 2, 1)
            strip = piece if strip is None else jnp.where(lane >= GROUP * sens, piece, strip)
        sides.append(strip)
    return sides


def interior(march_now, *refs):
    held = dict(zip(NAMES, refs[:10]))
    results = refs[10:15]
    strips, strips_static, to_west, to_east = refs[15:19]
    moving, fixed = refs[19:21]
    sens_count, rows, width = held["adj_h"].shape
    count = rows // TILE

    def field(key, kind):
        name, step = key
        return (held[name][...] if held[name].ndim == 2 else held[name][step]).astype(jnp.float32)

    if not march_now:
        for number, strip in enumerate(shared_strips([lane_tiles(field(key, 0)) for key in STRIP_KEYS])):
            strips_static[number] = strip
        pack_columns(held, to_west, to_east)
        for kind in range(3):
            values = [lane_tiles(held[NAMES[kind]][sens]) for sens in range(sens_count)]
            strips[kind] = jnp.concatenate(state_strips(values), axis=1)
        return
    coefficients(field, None, moving, fixed)

    def each(turn, carry):
        first = turn * PAIR
        states = [
            tuple([held[name][first + one, rows_of(tile), :] for tile in range(count)] for name in NAMES[:3])
            for one in range(PAIR)
        ]
        for one, values in enumerate(march(states, moving, fixed, None, False)):
            for ref, tiles in zip(results, values):
                for tile in range(count):
                    ref[first + one, rows_of(tile), :] = tiles[tile]
        return carry

    lax.fori_loop(0, sens_count // PAIR, each, 0)


def waits_for_top():
    row = lax.axis_index("lat") * lax.axis_size("sub") + lax.axis_index("sub")
    return (row == lax.axis_size("lat") * lax.axis_size("sub") - 2) & (lax.axis_index("lon") == 0)


def near_and_interior(*refs):
    pack_near(*refs[:12])

    @pl.when(waits_for_top())
    def _():
        interior(True, *refs[:10], *refs[12:])


def interior_after(*refs):
    interior(False, *refs[:10], *refs[19:])

    @pl.when(jnp.logical_not(waits_for_top()))
    def _():
        interior(True, *refs[:10], *refs[19:])


def row_edges(*refs):
    held = dict(zip(NAMES, refs[:10]))
    one, two = refs[10:12]
    results = refs[17:22]
    outs = refs[22:27]
    strips, strips_static = refs[27:29]
    halo, halo_static, moving, fixed, sems = refs[29:34]
    _, at_top, _ = place()
    sens_count, rows, width = held["adj_h"].shape
    row = iota((TILE, width), 0)
    top, bottom = rows // TILE - 1, 0
    inside = (slice(None), pl.ds(TILE, rows - 2 * TILE), pl.ds(LANES, width - 2 * LANES))
    copies = [
        pltpu.make_async_copy(results[number].at[inside], outs[number].at[inside], sems.at[number])
        for number in range(5)
    ]
    for copy in copies:
        copy.start()
    for number, value in enumerate(halo_tiles(one, two, sens_count)):
        if number < 3 * sens_count:
            halo[number] = value
        else:
            halo_static[number - 3 * sens_count] = value

    def shifted_halo(value, kind):
        if kind == 1:
            return jnp.where(at_top & (row < DEEP), pltpu.roll(value, width - 1, 1), value)
        return value

    def field(key, kind):
        name, step = key
        ref = held[name] if held[name].ndim == 2 else held[name].at[step]
        if key in TILES:
            between = shifted_halo(halo_static[TILES.index(key)], kind)
        else:
            between = jnp.ones((TILE, width), jnp.float32)
        parts = [ref[rows_of(top), :].astype(jnp.float32), between, ref[rows_of(bottom), :].astype(jnp.float32)]
        return jnp.concatenate(parts, axis=0)

    coefficients(field, 1, moving, fixed)

    def each(turn, carry):
        first = turn * PAIR
        states = []
        for one in range(PAIR):
            state = []
            for kind in range(3):
                ref = held[NAMES[kind]]
                between = shifted_halo(halo[3 * (first + one) + kind], kind)
                state.append([ref[first + one, rows_of(top), :], between, ref[first + one, rows_of(bottom), :]])
            states.append(tuple(state))
        for one, values in enumerate(march(states, moving, fixed, 1, at_top)):
            for ref, tiles in zip(results, values):
                ref[first + one, rows - DEEP :, :] = tiles[0][DEEP:]
                ref[first + one, :DEEP, :] = tiles[2][:DEEP]
        return carry

    lax.fori_loop(0, sens_count // PAIR, each, 0)
    state = [
        state_strips([lane_tiles(halo[3 * sens + kind]) for sens in range(sens_count)]) for kind in range(3)
    ]
    static = shared_strips([lane_tiles(halo_static[index]) for index in range(len(TILES))])
    for kind in range(3):
        strips[kind] = jnp.concatenate(state[kind], axis=1)
    for index in range(len(TILES)):
        strips_static[index] = static[index]
    for copy in copies:
        copy.wait()


def column_edges(*refs):
    results = refs[:5]
    strips, strips_static, halo_strips, halo_strips_static, from_west_ref, from_east_ref = refs[5:11]
    outs = refs[16:21]
    ends, moving, fixed, sems = refs[21:25]
    _, at_top, _ = place()
    sens_count, rows, width = results[0].shape
    count = rows // TILE + 1
    last = count - 1
    half = GROUP // 2
    height = rows + TILE
    lane = iota((height, LANES), 1)
    within = lane & (GROUP - 1)
    row = iota((height, 2 * LANES), 0)

    copies = []
    for number in range(5):
        for side, first in enumerate((0, rows - TILE)):
            middle = (slice(None), pl.ds(first, TILE), pl.ds(LANES, width - 2 * LANES))
            copies.append(
                pltpu.make_async_copy(results[number].at[middle], outs[number].at[middle], sems.at[2 + side, number])
            )
            copies[-1].start()
    from_west, from_east = from_west_ref[...], from_east_ref[...]
    easts = spread(pltpu.roll(from_east, LANES + half - 3 * DEEP, 1))
    wests = spread(pltpu.roll(from_west, LANES + DEEP - 3 * DEEP, 1))

    def joined(own, halo_own, east, west, kind):
        own = jnp.concatenate([own, halo_own], axis=0)
        east = jnp.where(within < half, own[:, :LANES], east)
        west = jnp.where(within >= half, own[:, LANES:], west)
        value = jnp.concatenate([east, west], axis=1)
        if kind == 1:
            turned = pltpu.roll(value, 2 * LANES - 1, 1)
            value = jnp.where(at_top & (row >= rows) & (row < rows + DEEP), turned, value)
        return value

    def field(key, kind):
        name, step = key
        own = strips_static[STRIP_KEYS.index((name, None) if name == "drag" else key)]
        if key not in TILES:
            east = west = jnp.ones((height, LANES), jnp.float32)
            return joined(own, jnp.ones((TILE, 2 * LANES), jnp.float32), east, west, kind)
        east = west = jnp.zeros((height, LANES), jnp.float32)
        if key in COLUMN_SLOTS:
            slot, offset, columns = COLUMN_SLOTS[key]
            east, west = easts[slot], wests[slot]
            if offset:
                east = pltpu.roll(east, LANES - offset, 1)
            if columns + offset < DEEP:
                west = pltpu.roll(west, DEEP - columns - offset, 1)
        return joined(own, halo_strips_static[TILES.index(key)], east, west, kind)

    coefficients(field, last, moving, fixed)
    state = []
    for kind in range(3):
        east = pltpu.roll(from_east[:, :LANES], (half - DEEP * kind) % LANES, 1)
        west = pltpu.roll(from_west[:, :LANES], (DEEP - DEEP * kind) % LANES, 1)
        value = joined(strips[kind], halo_strips[kind], east, west, kind)
        state.append([value[rows_of(tile), :] for tile in range(count)])
    (values,) = march([tuple(state)], moving, fixed, last, at_top)
    lane = iota((rows, LANES), 1)
    for number in range(5):
        strip = jnp.concatenate(values[number][:last], axis=0)
        for side, first in ((0, width - LANES), (1, 0)):
            inside = lane >= LANES - DEEP if side == 0 else lane < DEEP
            part = strip[:, side * LANES : (side + 1) * LANES]
            merged = []
            for sens in range(sens_count):
                shift = (LANES - half - GROUP * sens) % LANES
                piece = pltpu.roll(part, shift, 1) if shift else part
                merged.append(jnp.where(inside, piece, results[number][sens, :, first : first + LANES]))
            for sens in range(sens_count):
                ends[side, number, sens] = merged[sens]
            copies.append(
                pltpu.make_async_copy(
                    ends.at[side, number], outs[number].at[:, :, pl.ds(first, LANES)], sems.at[side, number]
                )
            )
            copies[-1].start()
    for copy in copies:
        copy.wait()


def on_device(traj_u, traj_v, adj_h, adj_u, adj_v, depth, drag, land, wet_u, wet_v):
    count, rows, width = adj_h.shape
    steps = traj_u.shape[0]
    args = (adj_h, adj_u, adj_v, traj_u, traj_v, wet_u, wet_v, depth, drag, land)
    in_hbm_args = tuple(pltpu.with_memory_space_constraint(arg, pltpu.HBM) for arg in args)

    in_vmem = pl.BlockSpec(memory_space=pltpu.VMEM)
    in_hbm = pl.BlockSpec(memory_space=pl.ANY)
    params = pltpu.CompilerParams(vmem_limit_bytes=VMEM_LIMIT)
    row_pack = jax.ShapeDtypeStruct((message_rows(count, width), width), jnp.float32)
    packed = pl.pallas_call(
        pack_far,
        in_specs=[in_hbm] * len(args),
        out_specs=in_vmem,
        out_shape=row_pack,
        scratch_shapes=[pltpu.VMEM(arg.shape[:-2] + (TILE, width), arg.dtype) for arg in args]
        + [pltpu.SemaphoreType.DMA((len(args),))],
        compiler_params=params,
        name="pack_far",
    )(*in_hbm_args)

    lons, lats, subs = (lax.axis_size(axis) for axis in GRID)
    total_rows = lats * subs

    def device(lon, row):
        return lon * total_rows + row

    route = [(device(lon, 0), device(lon ^ 1, 0)) for lon in range(lons)]
    for lon in range(lons):
        for row in range(1, total_rows - 1, 2):
            route += [(device(lon, row), device(lon, row + 1)), (device(lon, row + 1), device(lon, row))]
        route.append((device(lon, total_rows - 1), device(lons - 1 - lon, total_rows - 1)))
    two = lax.ppermute(packed, GRID, route)

    def shape(*dims):
        return jax.ShapeDtypeStruct(dims, jnp.float32)

    def scratch(tiles, wide):
        return [
            pltpu.VMEM((8, steps, tiles * TILE, wide), jnp.float32),
            pltpu.VMEM((5, tiles * TILE, wide), jnp.float32),
        ]

    state = shape(*adj_h.shape)
    inner_shapes = (
        [state] * 5
        + [shape(3, rows, 2 * LANES), shape(len(STRIP_KEYS), rows, 2 * LANES)]
        + [shape(rows, LANES)] * 2
    )
    one, *first = pl.pallas_call(
        near_and_interior,
        in_specs=[in_vmem] * 10 + [in_hbm],
        out_specs=[in_vmem] * 10,
        out_shape=[shape(message_size(count, width), width)] + inner_shapes,
        scratch_shapes=scratch(rows // TILE, width),
        compiler_params=params,
        name="near_and_interior",
    )(*args, packed)
    one = lax.ppermute(one, "sub", [(core, core ^ 1) for core in range(subs)])
    first = pl.pallas_call(
        interior_after,
        in_specs=[in_vmem] * 19,
        out_specs=[in_vmem] * 9,
        out_shape=inner_shapes,
        input_output_aliases={10 + number: number for number in range(9)},
        scratch_shapes=scratch(rows // TILE, width),
        compiler_params=params,
        name="interior_after",
    )(*args, *first)
    results, strips, own_columns = first[:5], first[5:7], first[7:]

    full_pack = jax.ShapeDtypeStruct((rows + TILE, LANES), jnp.float32)
    to_west, to_east = pl.pallas_call(
        functools.partial(merge_columns, count),
        out_shape=[full_pack] * 2,
        compiler_params=params,
        name="merge_columns",
    )(one, two, *own_columns)
    from_west = lax.ppermute(to_east, "lon", [(lon, (lon + 1) % lons) for lon in range(lons)])
    from_east = lax.ppermute(to_west, "lon", [(lon, (lon - 1) % lons) for lon in range(lons)])

    second = pl.pallas_call(
        row_edges,
        in_specs=[in_vmem] * 17,
        out_specs=[in_vmem] * 5 + [in_hbm] * 5 + [in_vmem] * 2,
        out_shape=[state] * 10 + [shape(3, TILE, 2 * LANES), shape(len(TILES), TILE, 2 * LANES)],
        input_output_aliases={12 + number: number for number in range(5)},
        scratch_shapes=[
            pltpu.VMEM((3 * count, TILE, width), jnp.float32),
            pltpu.VMEM((len(TILES), TILE, width), jnp.float32),
        ]
        + scratch(3, width)
        + [pltpu.SemaphoreType.DMA((5,))],
        compiler_params=params,
        name="row_edges",
    )(*args, one, two, *results)
    results, outs, halo_strips = second[:5], second[5:10], second[10:]

    return pl.pallas_call(
        column_edges,
        in_specs=[in_vmem] * 11 + [in_hbm] * 5,
        out_specs=[in_hbm] * 5,
        out_shape=[state] * 5,
        input_output_aliases={11 + number: number for number in range(5)},
        scratch_shapes=[pltpu.VMEM((2, 5, count, rows, LANES), jnp.float32)]
        + scratch(rows // TILE + 1, 2 * LANES)
        + [pltpu.SemaphoreType.DMA((4, 5))],
        compiler_params=params,
        name="column_edges",
    )(*results, *strips, *halo_strips, from_west, from_east, *outs)


def solution(mesh):
    state = P("case", ROWS, "lon")
    fixed = P(ROWS, "lon")
    return jax.shard_map(
        on_device,
        mesh=mesh,
        in_specs=(state,) * 5 + (fixed,) * 3 + (state,) * 2,
        out_specs=(state,) * 5,
        check_vma=False,
    )
```

```python
import functools

import jax
import jax.numpy as jnp
from jax import lax
from jax.experimental import pallas as pl
from jax.experimental.pallas import tpu as pltpu
from jax.sharding import PartitionSpec as P

time_step = 0.5
gravity = 1.0
speed_floor = 0.01

ROWS = ("lat", "sub")
GRID = ("lon", "lat", "sub")
TILE = 8
LANES = 128
DEEP = 4
GROUP = 16
PAIR = 8
VMEM_LIMIT = 48 * 1024 * 1024


def iota(shape, axis):
    return lax.broadcasted_iota(jnp.int32, shape, axis)


def place():
    row = lax.axis_index("lat") * lax.axis_size("sub") + lax.axis_index("sub")
    last = lax.axis_size("lat") * lax.axis_size("sub") - 1
    return row % 2 == 0, row == last, row == 0


STATE_ROWS = 8
SHARED = (
    (("traj_v", 2), 2, 3, True),
    (("traj_v", 1), 2, 2, True),
    (("traj_v", 0), 2, 1, True),
    (("traj_u", 2), 1, 2, True),
    (("traj_u", 1), 1, 1, True),
    (("wet_v", 1), 2, 3, False),
    (("wet_v", 0), 2, 2, False),
    (("wet_u", 1), 1, 2, False),
    (("wet_u", 0), 1, 1, False),
    (("depth", None), 0, 3, False),
    (("drag", None), 3, 3, False),
    (("land", None), 0, 3, False),
)
NAMES = ("adj_h", "adj_u", "adj_v", "traj_u", "traj_v", "wet_u", "wet_v", "depth", "drag", "land")
TILES = tuple(entry[0] for entry in SHARED[:10]) + (("drag", 1), ("drag", 2), ("land", None), ("traj_u", 0))


def load(refs, name, step):
    value = refs[name][...] if step is None or name == "drag" else refs[name][step]
    return value.astype(jnp.float32)


def message_size(count, width):
    return STATE_ROWS * count + sum(entry[2] for entry in SHARED) + -(-count // (width // LANES))


def message_rows(count, width):
    return -(-message_size(count, width) // TILE) * TILE


def shared_plan(count):
    plan, at = [], STATE_ROWS * count
    for key, kind, slots, turned in SHARED:
        plan.append((key, kind, turned, at, slots))
        at += slots
    return plan, at


def lane_tiles(value):
    return [value[:, at : at + LANES] for at in range(0, value.shape[1], LANES)]


def masked(refs, key):
    name, step = key
    value = load(refs, name, step)
    if name == "adj_u":
        value = value * load(refs, "wet_u", 2)
    if name == "adj_v":
        value = value * load(refs, "wet_v", 2)
    return value


def start_copies(arrays, held, sems, window, names=NAMES):
    copies = {}
    for number, name in enumerate(NAMES):
        array = arrays[name]
        if name in names:
            lead = (slice(None),) * (array.ndim - 2)
            source = array.at[lead + window(*array.shape[-2:])]
            copies[name] = pltpu.make_async_copy(source, held[name], sems.at[number])
            copies[name].start()
    return copies


def row_window(at_bottom_edge):
    def window(rows, width):
        first = pl.multiple_of(jnp.where(at_bottom_edge, 0, rows - TILE), TILE)
        return pl.ds(first, TILE), slice(None)

    return window


LOW, HIGH, FOLD = range(3)


def edge_rows(value, slots, mode, kind=0, turned=False):
    if mode == LOW:
        return [value[:slots]]
    if mode == HIGH:
        return [value[TILE - slots :]]
    if kind == 2:
        order = [TILE - 2 - slot for slot in range(slots - 1)] + [TILE - 1]
    else:
        order = [TILE - 1 - slot for slot in range(slots)]
    picked = [value[source : source + 1] for source in order]
    if turned:
        picked = [-row for row in picked[: slots - 1]] + picked[slots - 1 :] if kind == 2 else [-row for row in picked]
    return picked


def pack_edge(held, target, mode):
    count, _, width = held["adj_h"].shape
    lane = iota((TILE, width), 1)
    across = LANES - 1 - iota((TILE, LANES), 1)
    third = 2 if mode == LOW else TILE - 3

    def mirrored(value):
        if mode != FOLD:
            return value
        rows = []
        for first in range(0, value.shape[0], TILE):
            pieces = lane_tiles(value[first : first + TILE])[::-1]
            rows.append(jnp.concatenate([jnp.take_along_axis(piece, across, axis=1) for piece in pieces], axis=1))
        return jnp.concatenate(rows, axis=0)

    ends = []
    for sens in range(count):
        high, flow_u, flow_v = (masked(held, (name, sens)) for name in NAMES[:3])
        west = jnp.where(lane == 0, 0.0, pltpu.roll(flow_u, 1, 1))
        ahead = high + 0.5 * (flow_u - west + flow_v - pltpu.roll(flow_v, 1, 0))
        rows = edge_rows(high, 2, mode)
        rows += edge_rows(flow_u, 2, mode, 1, True)
        rows += edge_rows(flow_v, 3, mode, 2, True)
        rows.append(ahead[third : third + 1])
        here = slice(STATE_ROWS * sens, STATE_ROWS * (sens + 1))
        target[here, :] = mirrored(jnp.concatenate(rows, axis=0))
        end = flow_u[third : third + 1, width - LANES :]
        ends.append(-end if mode == FOLD else end)
    rows = []
    plan, _ = shared_plan(count)
    for key, kind, turned, at, slots in plan:
        rows += edge_rows(masked(held, key), slots, mode, kind, turned)
    each = width // LANES
    for first in range(0, count, each):
        some = ends[first : first + each]
        blank = [jnp.zeros((1, LANES), jnp.float32)] * (each - len(some))
        rows.append(jnp.concatenate(some + blank, axis=1))
    rows.append(jnp.zeros((message_rows(count, width) - message_size(count, width), width), jnp.float32))
    shared = mirrored(jnp.concatenate([row for row in rows if row.shape[0]], axis=0))
    size = target.shape[0] - STATE_ROWS * count
    target[STATE_ROWS * count :, :] = shared[:size]


def pack_far(*refs):
    arrays = dict(zip(NAMES, refs[:10]))
    target = refs[10]
    held = dict(zip(NAMES, refs[11:21]))
    even, at_top, _ = place()
    for copy in start_copies(arrays, held, refs[21], row_window(even)).values():
        copy.wait()

    @pl.when(even)
    def _():
        pack_edge(held, target, LOW)

    @pl.when(jnp.logical_not(even) & jnp.logical_not(at_top))
    def _():
        pack_edge(held, target, HIGH)

    @pl.when(at_top)
    def _():
        pack_edge(held, target, FOLD)


def pack_near(*refs):
    args = dict(zip(NAMES, refs[:10]))
    near = refs[11]
    even, _, _ = place()
    count, rows, width = args["adj_h"].shape
    low, high = (
        {name: ref.at[(slice(None),) * (ref.ndim - 2) + (pl.ds(first, TILE),)] for name, ref in args.items()}
        for first in (0, rows - TILE)
    )

    @pl.when(even)
    def _():
        pack_edge(high, near, HIGH)

    @pl.when(jnp.logical_not(even))
    def _():
        pack_edge(low, near, LOW)


COLUMN_SLOTS = {
    ("traj_u", 2): (0, 0, 3),
    ("traj_u", 0): (0, 3, 1),
    ("wet_u", 1): (1, 0, 3),
    ("depth", None): (2, 0, 3),
    ("drag", 1): (3, 0, 3),
    ("land", None): (4, 0, 3),
    ("traj_u", 1): (5, 0, 2),
    ("wet_u", 0): (5, 2, 2),
    ("traj_v", 2): (6, 0, 2),
    ("wet_v", 1): (6, 2, 2),
    ("drag", 2): (7, 0, 2),
    ("traj_v", 1): (7, 2, 1),
    ("wet_v", 0): (7, 3, 1),
}


def column_fields(count):
    fields = []
    for sens in range(count):
        for kind in range(3):
            fields.append(((NAMES[kind], sens), GROUP * sens + DEEP * kind, DEEP, 3 * sens + kind))
    for key, (slot, offset, columns) in COLUMN_SLOTS.items():
        fields.append((key, GROUP * slot + 3 * DEEP + offset, columns, 3 * count + TILES.index(key)))
    return sorted(fields, key=lambda entry: entry[1])


def pack_columns(held, to_west, to_east):
    count, rows, width = held["adj_h"].shape
    lane = iota((rows, LANES), 1)
    for target, first, east in ((to_west, 0, False), (to_east, width - LANES, True)):
        side_held = {name: ref.at[(slice(None),) * (ref.ndim - 1) + (pl.ds(first, LANES),)] for name, ref in held.items()}
        packed = None
        for key, start, columns, _ in column_fields(count):
            value = masked(side_held, key)
            shift = (start + columns) % LANES if east else start
            if shift:
                value = pltpu.roll(value, shift, 1)
            packed = value if packed is None else jnp.where(lane >= start, value, packed)
        target[...] = packed


def received(one, two):
    even, at_top, at_bottom = place()

    def beyond(here):
        north = jnp.where(even, one[here, :], two[here, :])
        south = jnp.where(even, two[here, :], one[here, :])
        return north, jnp.where(at_bottom, 0.0, south)

    return beyond


def blank(slots, columns):
    return jnp.zeros((slots, columns), jnp.float32)


def halo_tiles(one, two, count):
    _, at_top, _ = place()
    width = one.shape[1]
    beyond = received(one, two)
    plan, _ = shared_plan(count)
    tiles = []
    for sens in range(count):
        north, south = beyond(slice(STATE_ROWS * sens, STATE_ROWS * (sens + 1)))
        third_north = north[7:8] + 0.5 * north[5:6]
        third_south = south[7:8] - 0.5 * south[4:5]
        fold = jnp.where(at_top, north[6:7], 0.0)
        tiles.append(jnp.concatenate([north[:2], third_north, blank(2, width), third_south, south[:2]], axis=0))
        tiles.append(jnp.concatenate([north[2:4], blank(4, width), south[2:4]], axis=0))
        tiles.append(jnp.concatenate([north[4:6], blank(1, width), fold, blank(1, width), south[4:7]], axis=0))
    for key, kind, turned, at, slots in plan:
        north, south = beyond(slice(at, at + slots))
        gap = [blank(DEEP - slots, width)] if slots < DEEP else []
        plain = jnp.concatenate([north] + gap + gap + [south], axis=0)
        values = [plain]
        if kind >= 2 and slots < DEEP:
            fold = ([north[:-1]] if slots > 1 else []) + gap + [north[-1:]] + gap + [south]
            if kind == 3:
                fold = [north[1:], blank(1, width), north[:1]] + gap + [south]
                values.append(jnp.where(at_top, jnp.concatenate(fold, axis=0), plain))
            else:
                values = [jnp.where(at_top, jnp.concatenate(fold, axis=0), plain)]
        tiles += values
    tiles.append(blank(TILE, width))
    return tiles


def merge_columns(count, one, two, own_west, own_east, to_west, to_east):
    _, at_top, _ = place()
    width = one.shape[1]
    rows = own_west.shape[0]
    lane = iota((TILE, LANES), 1)
    to_west[:rows, :] = own_west[...]
    to_east[:rows, :] = own_east[...]
    tiles = halo_tiles(
        *(jnp.concatenate([ref[:, :LANES], ref[:, width - LANES :]], axis=1) for ref in (one, two)), count
    )
    beyond = received(one, two)
    each = width // LANES
    _, ends_at = shared_plan(count)
    ends = []
    for sens in range(count):
        end_north, end_south = beyond(slice(ends_at + sens // each, ends_at + sens // each + 1))
        mine, turned = (slice(number * LANES, (number + 1) * LANES) for number in (sens % each, each - 1 - sens % each))
        end_north = jnp.where(at_top, end_north[:, turned], end_north[:, mine])
        west = [blank(2, LANES), jnp.where(at_top, end_north, 0.0), blank(5, LANES)]
        east = [blank(2, LANES), jnp.where(at_top, 0.0, end_north), blank(2, LANES), end_south[:, mine], blank(2, LANES)]
        ends.append((jnp.concatenate(west, axis=0), jnp.concatenate(east, axis=0)))
    packed = [None, None]
    for key, start, columns, field in column_fields(count):
        pieces = lane_tiles(tiles[field])
        if field < 3 * count and field % 3 == 1:
            west, east = ends[field // 3]
            pieces = [pieces[0] + west, pieces[-1] + east]
        for way, piece, shift in ((0, pieces[0], start), (1, pieces[-1], (start + columns) % LANES)):
            if shift:
                piece = pltpu.roll(piece, shift, 1)
            packed[way] = piece if packed[way] is None else jnp.where(lane >= start, piece, packed[way])
    to_west[rows:, :] = packed[0]
    to_east[rows:, :] = packed[1]


def rows_of(tile):
    return slice(tile * TILE, (tile + 1) * TILE)


KEEP, DEPTH, DRAG, VEL = 0, 2, 4, 6
FIRST, LAND, RATIO = 0, 2, 3


def coefficients(field, halo, moving, fixed):
    cells = field(("depth", None), 0)
    cells = jnp.where(cells > 0.0, cells, 1.0)
    height, wide = cells.shape
    row = iota((height, wide), 0)
    stores = [(fixed, (LAND,), 0.5 * field(("land", None), 0))]
    for side, way in enumerate("uv"):
        kind = side + 1
        if side == 0:
            face = 0.5 * (cells + pltpu.roll(cells, wide - 1, 1))
        else:
            face = 0.5 * (cells + pltpu.roll(cells, height - 1, 0))
            if halo is not None:
                face = jnp.where(row == halo * TILE + 3, pltpu.roll(face, DEEP, 0), face)
        inverse = 1.0 / face
        ratio = -field(("drag", kind), kind) * inverse
        wet = [field(("wet_" + way, step), kind) for step in range(3)]
        stores += [(fixed, (RATIO + side,), ratio), (fixed, (FIRST + side,), 0.5 * wet[2])]
        for step in range(3):
            now = field(("traj_" + way, step), kind)
            square = now * now
            root = lax.rsqrt(square + speed_floor)
            speed = (square + speed_floor) * root
            keep = 2.0 + ratio * (speed + square * root)
            deep = face
            if step > 0:
                mask = 0.5 * wet[step - 1]
                keep, deep = keep * mask, deep * mask
            stores += [
                (moving, (KEEP + side, step), keep),
                (moving, (DEPTH + side, step), deep),
                (moving, (DRAG + side, step), -now * speed * inverse),
                (moving, (VEL + side, step), now),
            ]
    for ref, index, value in stores:
        ref[index] = value


def south_of(values, tile):
    row = iota(values[tile].shape, 0)
    return jnp.where(row == 0, pltpu.roll(values[tile - 1], 1, 0), pltpu.roll(values[tile], 1, 0))


def north_of(values, tile):
    row = iota(values[tile].shape, 0)
    after = values[(tile + 1) % len(values)]
    return jnp.where(row == TILE - 1, pltpu.roll(after, TILE - 1, 0), pltpu.roll(values[tile], TILE - 1, 0))


def march(states, moving, fixed, halo, at_top):
    count = len(states[0][0])
    wide = states[0][0][0].shape[1]
    row = iota((TILE, wide), 0)
    group = range(len(states))

    def east_of(value):
        return pltpu.roll(value, wide - 1, 1)

    def west_of(value):
        return pltpu.roll(value, 1, 1)

    def fold_row(value):
        return jnp.where(at_top & (row == TILE - 1), pltpu.roll(value, DEEP, 0), 0.0)

    high = [list(state[0]) for state in states]
    flow_u, flow_v = [[] for _ in group], [[] for _ in group]
    for tile in range(count):
        here = rows_of(tile)
        first_u, first_v = fixed[FIRST, here, :], fixed[FIRST + 1, here, :]
        for one in group:
            flow_u[one].append(first_u * states[one][1][tile])
            flow_v[one].append(first_v * states[one][2][tile])
    history = []
    for step in (2, 1, 0):
        sea, turns_u, turns_v, next_u, next_v = ([[] for _ in group] for _ in range(5))
        face = [list(flows) for flows in flow_v]
        if halo is not None:
            for one in group:
                face[one][halo - 1] = flow_v[one][halo - 1] - fold_row(flow_v[one][halo])
        for tile in range(count):
            land = fixed[LAND, rows_of(tile), :]
            for one in group:
                high[one][tile] = (
                    high[one][tile]
                    + (flow_u[one][tile] - west_of(flow_u[one][tile]))
                    + (face[one][tile] - south_of(face[one], tile))
                )
                sea[one].append(land * high[one][tile])
        for tile in range(count):
            here = rows_of(tile)
            keep_u, keep_v = moving[KEEP, step, here, :], moving[KEEP + 1, step, here, :]
            deep_u, deep_v = moving[DEPTH, step, here, :], moving[DEPTH + 1, step, here, :]
            for one in group:
                turn_u = east_of(sea[one][tile]) - sea[one][tile]
                turn_v = north_of(sea[one], tile) - sea[one][tile]
                if tile == halo:
                    turn_v = jnp.where(row == 3, -pltpu.roll(turns_v[one][tile - 1], DEEP, 0), turn_v)
                turns_u[one].append(turn_u)
                turns_v[one].append(turn_v)
                next_u[one].append(keep_u * flow_u[one][tile] + deep_u * turn_u)
                next_v[one].append(keep_v * flow_v[one][tile] + deep_v * turn_v)
        history.append((step, flow_u, flow_v, turns_u, turns_v))
        flow_u, flow_v = next_u, next_v

    face_u, face_v, drags = ([[] for _ in group] for _ in range(3))
    for tile in range(count):
        here = rows_of(tile)
        sums = [[0.0] * 4 for _ in group]
        for step, steps_u, steps_v, turns_u, turns_v in history:
            for number, (index, values) in enumerate(
                ((DRAG, steps_u), (DRAG + 1, steps_v), (VEL, turns_u), (VEL + 1, turns_v))
            ):
                factor = moving[index, step, here, :]
                for one in group:
                    sums[one][number] += factor * values[one][tile]
        ratio_u, ratio_v = fixed[RATIO, here, :], fixed[RATIO + 1, here, :]
        for one in group:
            face_u[one].append(ratio_u * sums[one][0] + sums[one][2])
            face_v[one].append(ratio_v * sums[one][1] + sums[one][3])
            drags[one].append(sums[one][0] + sums[one][1])
    outs = []
    for one in group:
        totals = []
        for tile in range(count):
            total = face_u[one][tile] + west_of(face_u[one][tile]) + face_v[one][tile] + south_of(face_v[one], tile)
            if halo is not None and tile == halo - 1:
                total = total + fold_row(face_v[one][halo])
            totals.append(0.5 * total)
        outs.append((high[one], flow_u[one], flow_v[one], totals, drags[one]))
    return outs


STRIP_KEYS = tuple(
    (name, step) for name in ("traj_u", "traj_v", "wet_u", "wet_v") for step in range(3)
) + (("depth", None), ("drag", None), ("land", None))


def spread(packed):
    lane = iota(packed.shape, 1)
    arrays = [packed]
    for shift in (4 * GROUP, 2 * GROUP, GROUP):
        upper = (lane & shift) != 0
        halves = []
        for value in arrays:
            other = pltpu.roll(value, shift, 1)
            halves += [jnp.where(upper, other, value), jnp.where(upper, value, other)]
        arrays = halves
    return arrays


def shared_strips(values):
    strips = []
    for first in range(0, len(values), LANES // GROUP):
        some = values[first : first + LANES // GROUP]
        sides = [spread(packed) for packed in state_strips(some)]
        strips += [jnp.concatenate([sides[0][number], sides[1][number]], axis=1) for number in range(len(some))]
    return strips


def state_strips(values):
    lane = iota(values[0][0].shape, 1)
    sides = []
    for end in (-1, 0):
        strip = None
        for sens, pieces in enumerate(values):
            piece = pltpu.roll(pieces[end], GROUP * sens + GROUP // 2, 1)
            strip = piece if strip is None else jnp.where(lane >= GROUP * sens, piece, strip)
        sides.append(strip)
    return sides


def interior(march_now, *refs):
    held = dict(zip(NAMES, refs[:10]))
    results = refs[10:15]
    strips, strips_static, to_west, to_east = refs[15:19]
    moving, fixed = refs[19:21]
    sens_count, rows, width = held["adj_h"].shape
    count = rows // TILE

    def field(key, kind):
        name, step = key
        return (held[name][...] if held[name].ndim == 2 else held[name][step]).astype(jnp.float32)

    if not march_now:
        for number, strip in enumerate(shared_strips([lane_tiles(field(key, 0)) for key in STRIP_KEYS])):
            strips_static[number] = strip
        pack_columns(held, to_west, to_east)
        for kind in range(3):
            values = [lane_tiles(held[NAMES[kind]][sens]) for sens in range(sens_count)]
            strips[kind] = jnp.concatenate(state_strips(values), axis=1)
        return
    coefficients(field, None, moving, fixed)

    def each(turn, carry):
        first = turn * PAIR
        states = [
            tuple([held[name][first + one, rows_of(tile), :] for tile in range(count)] for name in NAMES[:3])
            for one in range(PAIR)
        ]
        for one, values in enumerate(march(states, moving, fixed, None, False)):
            for ref, tiles in zip(results, values):
                for tile in range(count):
                    ref[first + one, rows_of(tile), :] = tiles[tile]
        return carry

    lax.fori_loop(0, sens_count // PAIR, each, 0)


def waits_for_top():
    row = lax.axis_index("lat") * lax.axis_size("sub") + lax.axis_index("sub")
    return (row == lax.axis_size("lat") * lax.axis_size("sub") - 2) & (lax.axis_index("lon") == 0)


def near_and_interior(*refs):
    pack_near(*refs[:12])

    @pl.when(waits_for_top())
    def _():
        interior(True, *refs[:10], *refs[12:])


def interior_after(*refs):
    interior(False, *refs[:10], *refs[19:])

    @pl.when(jnp.logical_not(waits_for_top()))
    def _():
        interior(True, *refs[:10], *refs[19:])


def row_edges(*refs):
    held = dict(zip(NAMES, refs[:10]))
    one, two = refs[10:12]
    results = refs[17:22]
    outs = refs[22:27]
    strips, strips_static = refs[27:29]
    halo, halo_static, moving, fixed, sems = refs[29:34]
    _, at_top, _ = place()
    sens_count, rows, width = held["adj_h"].shape
    row = iota((TILE, width), 0)
    top, bottom = rows // TILE - 1, 0
    inside = (slice(None), pl.ds(TILE, rows - 2 * TILE), pl.ds(LANES, width - 2 * LANES))
    copies = [
        pltpu.make_async_copy(results[number].at[inside], outs[number].at[inside], sems.at[number])
        for number in range(5)
    ]
    for copy in copies:
        copy.start()
    for number, value in enumerate(halo_tiles(one, two, sens_count)):
        if number < 3 * sens_count:
            halo[number] = value
        else:
            halo_static[number - 3 * sens_count] = value

    def shifted_halo(value, kind):
        if kind == 1:
            return jnp.where(at_top & (row < DEEP), pltpu.roll(value, width - 1, 1), value)
        return value

    def field(key, kind):
        name, step = key
        ref = held[name] if held[name].ndim == 2 else held[name].at[step]
        if key in TILES:
            between = shifted_halo(halo_static[TILES.index(key)], kind)
        else:
            between = jnp.ones((TILE, width), jnp.float32)
        parts = [ref[rows_of(top), :].astype(jnp.float32), between, ref[rows_of(bottom), :].astype(jnp.float32)]
        return jnp.concatenate(parts, axis=0)

    coefficients(field, 1, moving, fixed)

    def each(turn, carry):
        first = turn * PAIR
        states = []
        for one in range(PAIR):
            state = []
            for kind in range(3):
                ref = held[NAMES[kind]]
                between = shifted_halo(halo[3 * (first + one) + kind], kind)
                state.append([ref[first + one, rows_of(top), :], between, ref[first + one, rows_of(bottom), :]])
            states.append(tuple(state))
        for one, values in enumerate(march(states, moving, fixed, 1, at_top)):
            for ref, tiles in zip(results, values):
                ref[first + one, rows - DEEP :, :] = tiles[0][DEEP:]
                ref[first + one, :DEEP, :] = tiles[2][:DEEP]
        return carry

    lax.fori_loop(0, sens_count // PAIR, each, 0)
    state = [
        state_strips([lane_tiles(halo[3 * sens + kind]) for sens in range(sens_count)]) for kind in range(3)
    ]
    static = shared_strips([lane_tiles(halo_static[index]) for index in range(len(TILES))])
    for kind in range(3):
        strips[kind] = jnp.concatenate(state[kind], axis=1)
    for index in range(len(TILES)):
        strips_static[index] = static[index]
    for copy in copies:
        copy.wait()


def column_edges(*refs):
    results = refs[:5]
    strips, strips_static, halo_strips, halo_strips_static, from_west_ref, from_east_ref = refs[5:11]
    outs = refs[16:21]
    ends, moving, fixed, sems = refs[21:25]
    _, at_top, _ = place()
    sens_count, rows, width = results[0].shape
    count = rows // TILE + 1
    last = count - 1
    half = GROUP // 2
    height = rows + TILE
    lane = iota((height, LANES), 1)
    within = lane & (GROUP - 1)
    row = iota((height, 2 * LANES), 0)

    copies = []
    for number in range(5):
        for side, first in enumerate((0, rows - TILE)):
            middle = (slice(None), pl.ds(first, TILE), pl.ds(LANES, width - 2 * LANES))
            copies.append(
                pltpu.make_async_copy(results[number].at[middle], outs[number].at[middle], sems.at[2 + side, number])
            )
            copies[-1].start()
    from_west, from_east = from_west_ref[...], from_east_ref[...]
    easts = spread(pltpu.roll(from_east, LANES + half - 3 * DEEP, 1))
    wests = spread(pltpu.roll(from_west, LANES + DEEP - 3 * DEEP, 1))

    def joined(own, halo_own, east, west, kind):
        own = jnp.concatenate([own, halo_own], axis=0)
        east = jnp.where(within < half, own[:, :LANES], east)
        west = jnp.where(within >= half, own[:, LANES:], west)
        value = jnp.concatenate([east, west], axis=1)
        if kind == 1:
            turned = pltpu.roll(value, 2 * LANES - 1, 1)
            value = jnp.where(at_top & (row >= rows) & (row < rows + DEEP), turned, value)
        return value

    def field(key, kind):
        name, step = key
        own = strips_static[STRIP_KEYS.index((name, None) if name == "drag" else key)]
        if key not in TILES:
            east = west = jnp.ones((height, LANES), jnp.float32)
            return joined(own, jnp.ones((TILE, 2 * LANES), jnp.float32), east, west, kind)
        east = west = jnp.zeros((height, LANES), jnp.float32)
        if key in COLUMN_SLOTS:
            slot, offset, columns = COLUMN_SLOTS[key]
            east, west = easts[slot], wests[slot]
            if offset:
                east = pltpu.roll(east, LANES - offset, 1)
            if columns + offset < DEEP:
                west = pltpu.roll(west, DEEP - columns - offset, 1)
        return joined(own, halo_strips_static[TILES.index(key)], east, west, kind)

    coefficients(field, last, moving, fixed)
    state = []
    for kind in range(3):
        east = pltpu.roll(from_east[:, :LANES], (half - DEEP * kind) % LANES, 1)
        west = pltpu.roll(from_west[:, :LANES], (DEEP - DEEP * kind) % LANES, 1)
        value = joined(strips[kind], halo_strips[kind], east, west, kind)
        state.append([value[rows_of(tile), :] for tile in range(count)])
    (values,) = march([tuple(state)], moving, fixed, last, at_top)
    lane = iota((rows, LANES), 1)
    for number in range(5):
        strip = jnp.concatenate(values[number][:last], axis=0)
        for side, first in ((0, width - LANES), (1, 0)):
            inside = lane >= LANES - DEEP if side == 0 else lane < DEEP
            part = strip[:, side * LANES : (side + 1) * LANES]
            merged = []
            for sens in range(sens_count):
                shift = (LANES - half - GROUP * sens) % LANES
                piece = pltpu.roll(part, shift, 1) if shift else part
                merged.append(jnp.where(inside, piece, results[number][sens, :, first : first + LANES]))
            for sens in range(sens_count):
                ends[side, number, sens] = merged[sens]
            copies.append(
                pltpu.make_async_copy(
                    ends.at[side, number], outs[number].at[:, :, pl.ds(first, LANES)], sems.at[side, number]
                )
            )
            copies[-1].start()
    for copy in copies:
        copy.wait()


def on_device(traj_u, traj_v, adj_h, adj_u, adj_v, depth, drag, land, wet_u, wet_v):
    count, rows, width = adj_h.shape
    steps = traj_u.shape[0]
    args = (adj_h, adj_u, adj_v, traj_u, traj_v, wet_u, wet_v, depth, drag, land)
    in_hbm_args = tuple(pltpu.with_memory_space_constraint(arg, pltpu.HBM) for arg in args)

    in_vmem = pl.BlockSpec(memory_space=pltpu.VMEM)
    in_hbm = pl.BlockSpec(memory_space=pl.ANY)
    params = pltpu.CompilerParams(vmem_limit_bytes=VMEM_LIMIT)
    row_pack = jax.ShapeDtypeStruct((message_rows(count, width), width), jnp.float32)
    packed = pl.pallas_call(
        pack_far,
        in_specs=[in_hbm] * len(args),
        out_specs=in_vmem,
        out_shape=row_pack,
        scratch_shapes=[pltpu.VMEM(arg.shape[:-2] + (TILE, width), arg.dtype) for arg in args]
        + [pltpu.SemaphoreType.DMA((len(args),))],
        compiler_params=params,
        name="pack_far",
    )(*in_hbm_args)

    lons, lats, subs = (lax.axis_size(axis) for axis in GRID)
    total_rows = lats * subs

    def device(lon, row):
        return lon * total_rows + row

    cases = lax.axis_size("case")
    each = lons * total_rows
    route = []
    for case in range(cases):
        here = case * each
        for lon in range(lons):
            route.append((here + device(lon, 0), (case + 1) % cases * each + device(lon, 0)))
            for row in range(1, total_rows - 1, 2):
                low, high = here + device(lon, row), here + device(lon, row + 1)
                route += [(low, high), (high, low)]
            route.append((here + device(lon, total_rows - 1), here + device(lons - 1 - lon, total_rows - 1)))
    two = lax.ppermute(packed, ("case",) + GRID, route)

    def shape(*dims):
        return jax.ShapeDtypeStruct(dims, jnp.float32)

    def scratch(tiles, wide):
        return [
            pltpu.VMEM((8, steps, tiles * TILE, wide), jnp.float32),
            pltpu.VMEM((5, tiles * TILE, wide), jnp.float32),
        ]

    state = shape(*adj_h.shape)
    inner_shapes = (
        [state] * 5
        + [shape(3, rows, 2 * LANES), shape(len(STRIP_KEYS), rows, 2 * LANES)]
        + [shape(rows, LANES)] * 2
    )
    one, *first = pl.pallas_call(
        near_and_interior,
        in_specs=[in_vmem] * 10 + [in_hbm],
        out_specs=[in_vmem] * 10,
        out_shape=[shape(message_size(count, width), width)] + inner_shapes,
        scratch_shapes=scratch(rows // TILE, width),
        compiler_params=params,
        name="near_and_interior",
    )(*args, packed)
    one = lax.ppermute(one, "sub", [(core, core ^ 1) for core in range(subs)])
    first = pl.pallas_call(
        interior_after,
        in_specs=[in_vmem] * 19,
        out_specs=[in_vmem] * 9,
        out_shape=inner_shapes,
        input_output_aliases={10 + number: number for number in range(9)},
        scratch_shapes=scratch(rows // TILE, width),
        compiler_params=params,
        name="interior_after",
    )(*args, *first)
    results, strips, own_columns = first[:5], first[5:7], first[7:]

    full_pack = jax.ShapeDtypeStruct((rows + TILE, LANES), jnp.float32)
    to_west, to_east = pl.pallas_call(
        functools.partial(merge_columns, count),
        out_shape=[full_pack] * 2,
        compiler_params=params,
        name="merge_columns",
    )(one, two, *own_columns)
    from_west = lax.ppermute(to_east, "lon", [(lon, (lon + 1) % lons) for lon in range(lons)])
    from_east = lax.ppermute(to_west, "lon", [(lon, (lon - 1) % lons) for lon in range(lons)])

    second = pl.pallas_call(
        row_edges,
        in_specs=[in_vmem] * 17,
        out_specs=[in_vmem] * 5 + [in_hbm] * 5 + [in_vmem] * 2,
        out_shape=[state] * 10 + [shape(3, TILE, 2 * LANES), shape(len(TILES), TILE, 2 * LANES)],
        input_output_aliases={12 + number: number for number in range(5)},
        scratch_shapes=[
            pltpu.VMEM((3 * count, TILE, width), jnp.float32),
            pltpu.VMEM((len(TILES), TILE, width), jnp.float32),
        ]
        + scratch(3, width)
        + [pltpu.SemaphoreType.DMA((5,))],
        compiler_params=params,
        name="row_edges",
    )(*args, one, two, *results)
    results, outs, halo_strips = second[:5], second[5:10], second[10:]

    return pl.pallas_call(
        column_edges,
        in_specs=[in_vmem] * 11 + [in_hbm] * 5,
        out_specs=[in_hbm] * 5,
        out_shape=[state] * 5,
        input_output_aliases={11 + number: number for number in range(5)},
        scratch_shapes=[pltpu.VMEM((2, 5, count, rows, LANES), jnp.float32)]
        + scratch(rows // TILE + 1, 2 * LANES)
        + [pltpu.SemaphoreType.DMA((4, 5))],
        compiler_params=params,
        name="column_edges",
    )(*results, *strips, *halo_strips, from_west, from_east, *outs)


def solution(mesh):
    state = P("case", ROWS, "lon")
    fixed = P(ROWS, "lon")
    return jax.shard_map(
        on_device,
        mesh=mesh,
        in_specs=(state,) * 5 + (fixed,) * 3 + (state,) * 2,
        out_specs=(state,) * 5,
        check_vma=False,
    )
```

```python
import functools

import jax
import jax.numpy as jnp
from jax import lax
from jax.experimental import pallas as pl
from jax.experimental.pallas import tpu as pltpu
from jax.sharding import PartitionSpec as P

time_step = 0.5
gravity = 1.0
speed_floor = 0.01

ROWS = ("lat", "sub")
GRID = ("lon", "lat", "sub")
TILE = 8
LANES = 128
DEEP = 4
GROUP = 16
PAIR = 8
VMEM_LIMIT = 48 * 1024 * 1024


def iota(shape, axis):
    return lax.broadcasted_iota(jnp.int32, shape, axis)


def place():
    row = lax.axis_index("lat") * lax.axis_size("sub") + lax.axis_index("sub")
    last = lax.axis_size("lat") * lax.axis_size("sub") - 1
    return row % 2 == 0, row == last, row == 0


STATE_ROWS = 8
SHARED = (
    (("traj_v", 2), 2, 3, True),
    (("traj_v", 1), 2, 2, True),
    (("traj_v", 0), 2, 1, True),
    (("traj_u", 2), 1, 2, True),
    (("traj_u", 1), 1, 1, True),
    (("wet_v", 1), 2, 3, False),
    (("wet_v", 0), 2, 2, False),
    (("wet_u", 1), 1, 2, False),
    (("wet_u", 0), 1, 1, False),
    (("depth", None), 0, 3, False),
    (("drag", None), 3, 3, False),
    (("land", None), 0, 3, False),
)
NAMES = ("adj_h", "adj_u", "adj_v", "traj_u", "traj_v", "wet_u", "wet_v", "depth", "drag", "land")
TILES = tuple(entry[0] for entry in SHARED[:10]) + (("drag", 1), ("drag", 2), ("land", None), ("traj_u", 0))


def load(refs, name, step):
    value = refs[name][...] if step is None or name == "drag" else refs[name][step]
    return value.astype(jnp.float32)


def message_size(count, width):
    return STATE_ROWS * count + sum(entry[2] for entry in SHARED) + -(-count // (width // LANES))


def message_rows(count, width):
    return -(-message_size(count, width) // TILE) * TILE


def shared_plan(count):
    plan, at = [], STATE_ROWS * count
    for key, kind, slots, turned in SHARED:
        plan.append((key, kind, turned, at, slots))
        at += slots
    return plan, at


def lane_tiles(value):
    return [value[:, at : at + LANES] for at in range(0, value.shape[1], LANES)]


def masked(refs, key):
    name, step = key
    value = load(refs, name, step)
    if name == "adj_u":
        value = value * load(refs, "wet_u", 2)
    if name == "adj_v":
        value = value * load(refs, "wet_v", 2)
    return value


def start_copies(arrays, held, sems, window, names=NAMES):
    copies = {}
    for number, name in enumerate(NAMES):
        array = arrays[name]
        if name in names:
            lead = (slice(None),) * (array.ndim - 2)
            source = array.at[lead + window(*array.shape[-2:])]
            copies[name] = pltpu.make_async_copy(source, held[name], sems.at[number])
            copies[name].start()
    return copies


def row_window(at_bottom_edge):
    def window(rows, width):
        first = pl.multiple_of(jnp.where(at_bottom_edge, 0, rows - TILE), TILE)
        return pl.ds(first, TILE), slice(None)

    return window


LOW, HIGH, FOLD = range(3)


def edge_rows(value, slots, mode, kind=0, turned=False):
    if mode == LOW:
        return [value[:slots]]
    if mode == HIGH:
        return [value[TILE - slots :]]
    if kind == 2:
        order = [TILE - 2 - slot for slot in range(slots - 1)] + [TILE - 1]
    else:
        order = [TILE - 1 - slot for slot in range(slots)]
    picked = [value[source : source + 1] for source in order]
    if turned:
        picked = [-row for row in picked[: slots - 1]] + picked[slots - 1 :] if kind == 2 else [-row for row in picked]
    return picked


def pack_edge(held, target, mode):
    count, _, width = held["adj_h"].shape
    lane = iota((TILE, width), 1)
    across = LANES - 1 - iota((TILE, LANES), 1)
    third = 2 if mode == LOW else TILE - 3

    def mirrored(value):
        if mode != FOLD:
            return value
        rows = []
        for first in range(0, value.shape[0], TILE):
            pieces = lane_tiles(value[first : first + TILE])[::-1]
            rows.append(jnp.concatenate([jnp.take_along_axis(piece, across, axis=1) for piece in pieces], axis=1))
        return jnp.concatenate(rows, axis=0)

    ends = []
    for sens in range(count):
        high, flow_u, flow_v = (masked(held, (name, sens)) for name in NAMES[:3])
        west = jnp.where(lane == 0, 0.0, pltpu.roll(flow_u, 1, 1))
        ahead = high + 0.5 * (flow_u - west + flow_v - pltpu.roll(flow_v, 1, 0))
        rows = edge_rows(high, 2, mode)
        rows += edge_rows(flow_u, 2, mode, 1, True)
        rows += edge_rows(flow_v, 3, mode, 2, True)
        rows.append(ahead[third : third + 1])
        here = slice(STATE_ROWS * sens, STATE_ROWS * (sens + 1))
        target[here, :] = mirrored(jnp.concatenate(rows, axis=0))
        end = flow_u[third : third + 1, width - LANES :]
        ends.append(-end if mode == FOLD else end)
    rows = []
    plan, _ = shared_plan(count)
    for key, kind, turned, at, slots in plan:
        rows += edge_rows(masked(held, key), slots, mode, kind, turned)
    each = width // LANES
    for first in range(0, count, each):
        some = ends[first : first + each]
        blank = [jnp.zeros((1, LANES), jnp.float32)] * (each - len(some))
        rows.append(jnp.concatenate(some + blank, axis=1))
    rows.append(jnp.zeros((message_rows(count, width) - message_size(count, width), width), jnp.float32))
    shared = mirrored(jnp.concatenate([row for row in rows if row.shape[0]], axis=0))
    size = target.shape[0] - STATE_ROWS * count
    target[STATE_ROWS * count :, :] = shared[:size]


def pack_far(*refs):
    arrays = dict(zip(NAMES, refs[:10]))
    target = refs[10]
    held = dict(zip(NAMES, refs[11:21]))
    even, at_top, _ = place()
    for copy in start_copies(arrays, held, refs[21], row_window(even)).values():
        copy.wait()

    @pl.when(even)
    def _():
        pack_edge(held, target, LOW)

    @pl.when(jnp.logical_not(even) & jnp.logical_not(at_top))
    def _():
        pack_edge(held, target, HIGH)

    @pl.when(at_top)
    def _():
        pack_edge(held, target, FOLD)


def pack_near(*refs):
    args = dict(zip(NAMES, refs[:10]))
    near = refs[11]
    even, _, _ = place()
    count, rows, width = args["adj_h"].shape
    low, high = (
        {name: ref.at[(slice(None),) * (ref.ndim - 2) + (pl.ds(first, TILE),)] for name, ref in args.items()}
        for first in (0, rows - TILE)
    )

    @pl.when(even)
    def _():
        pack_edge(high, near, HIGH)

    @pl.when(jnp.logical_not(even))
    def _():
        pack_edge(low, near, LOW)


COLUMN_SLOTS = {
    ("traj_u", 2): (0, 0, 3),
    ("traj_u", 0): (0, 3, 1),
    ("wet_u", 1): (1, 0, 3),
    ("depth", None): (2, 0, 3),
    ("drag", 1): (3, 0, 3),
    ("land", None): (4, 0, 3),
    ("traj_u", 1): (5, 0, 2),
    ("wet_u", 0): (5, 2, 2),
    ("traj_v", 2): (6, 0, 2),
    ("wet_v", 1): (6, 2, 2),
    ("drag", 2): (7, 0, 2),
    ("traj_v", 1): (7, 2, 1),
    ("wet_v", 0): (7, 3, 1),
}


def column_fields(count):
    fields = []
    for sens in range(count):
        for kind in range(3):
            fields.append(((NAMES[kind], sens), GROUP * sens + DEEP * kind, DEEP, 3 * sens + kind))
    for key, (slot, offset, columns) in COLUMN_SLOTS.items():
        fields.append((key, GROUP * slot + 3 * DEEP + offset, columns, 3 * count + TILES.index(key)))
    return sorted(fields, key=lambda entry: entry[1])


def pack_columns(held, to_west, to_east):
    count, rows, width = held["adj_h"].shape
    lane = iota((rows, LANES), 1)
    for target, first, east in ((to_west, 0, False), (to_east, width - LANES, True)):
        side_held = {name: ref.at[(slice(None),) * (ref.ndim - 1) + (pl.ds(first, LANES),)] for name, ref in held.items()}
        packed = None
        for key, start, columns, _ in column_fields(count):
            value = masked(side_held, key)
            shift = (start + columns) % LANES if east else start
            if shift:
                value = pltpu.roll(value, shift, 1)
            packed = value if packed is None else jnp.where(lane >= start, value, packed)
        target[...] = packed


def received(one, two):
    even, at_top, at_bottom = place()

    def beyond(here):
        north = jnp.where(even, one[here, :], two[here, :])
        south = jnp.where(even, two[here, :], one[here, :])
        return north, jnp.where(at_bottom, 0.0, south)

    return beyond


def blank(slots, columns):
    return jnp.zeros((slots, columns), jnp.float32)


def halo_tiles(one, two, count):
    _, at_top, _ = place()
    width = one.shape[1]
    beyond = received(one, two)
    plan, _ = shared_plan(count)
    tiles = []
    for sens in range(count):
        north, south = beyond(slice(STATE_ROWS * sens, STATE_ROWS * (sens + 1)))
        third_north = north[7:8] + 0.5 * north[5:6]
        third_south = south[7:8] - 0.5 * south[4:5]
        fold = jnp.where(at_top, north[6:7], 0.0)
        tiles.append(jnp.concatenate([north[:2], third_north, blank(2, width), third_south, south[:2]], axis=0))
        tiles.append(jnp.concatenate([north[2:4], blank(4, width), south[2:4]], axis=0))
        tiles.append(jnp.concatenate([north[4:6], blank(1, width), fold, blank(1, width), south[4:7]], axis=0))
    for key, kind, turned, at, slots in plan:
        north, south = beyond(slice(at, at + slots))
        gap = [blank(DEEP - slots, width)] if slots < DEEP else []
        plain = jnp.concatenate([north] + gap + gap + [south], axis=0)
        values = [plain]
        if kind >= 2 and slots < DEEP:
            fold = ([north[:-1]] if slots > 1 else []) + gap + [north[-1:]] + gap + [south]
            if kind == 3:
                fold = [north[1:], blank(1, width), north[:1]] + gap + [south]
                values.append(jnp.where(at_top, jnp.concatenate(fold, axis=0), plain))
            else:
                values = [jnp.where(at_top, jnp.concatenate(fold, axis=0), plain)]
        tiles += values
    tiles.append(blank(TILE, width))
    return tiles


def merge_columns(count, one, two, own_west, own_east, to_west, to_east):
    _, at_top, _ = place()
    width = one.shape[1]
    rows = own_west.shape[0]
    lane = iota((TILE, LANES), 1)
    to_west[:rows, :] = own_west[...]
    to_east[:rows, :] = own_east[...]
    tiles = halo_tiles(
        *(jnp.concatenate([ref[:, :LANES], ref[:, width - LANES :]], axis=1) for ref in (one, two)), count
    )
    beyond = received(one, two)
    each = width // LANES
    _, ends_at = shared_plan(count)
    ends = []
    for sens in range(count):
        end_north, end_south = beyond(slice(ends_at + sens // each, ends_at + sens // each + 1))
        mine, turned = (slice(number * LANES, (number + 1) * LANES) for number in (sens % each, each - 1 - sens % each))
        end_north = jnp.where(at_top, end_north[:, turned], end_north[:, mine])
        west = [blank(2, LANES), jnp.where(at_top, end_north, 0.0), blank(5, LANES)]
        east = [blank(2, LANES), jnp.where(at_top, 0.0, end_north), blank(2, LANES), end_south[:, mine], blank(2, LANES)]
        ends.append((jnp.concatenate(west, axis=0), jnp.concatenate(east, axis=0)))
    packed = [None, None]
    for key, start, columns, field in column_fields(count):
        pieces = lane_tiles(tiles[field])
        if field < 3 * count and field % 3 == 1:
            west, east = ends[field // 3]
            pieces = [pieces[0] + west, pieces[-1] + east]
        for way, piece, shift in ((0, pieces[0], start), (1, pieces[-1], (start + columns) % LANES)):
            if shift:
                piece = pltpu.roll(piece, shift, 1)
            packed[way] = piece if packed[way] is None else jnp.where(lane >= start, piece, packed[way])
    to_west[rows:, :] = packed[0]
    to_east[rows:, :] = packed[1]


def rows_of(tile):
    return slice(tile * TILE, (tile + 1) * TILE)


KEEP, DEPTH, DRAG, VEL = 0, 2, 4, 6
FIRST, LAND, RATIO = 0, 2, 3


def coefficients(field, halo, moving, fixed):
    cells = field(("depth", None), 0)
    cells = jnp.where(cells > 0.0, cells, 1.0)
    height, wide = cells.shape
    row = iota((height, wide), 0)
    stores = [(fixed, (LAND,), 0.5 * field(("land", None), 0))]
    for side, way in enumerate("uv"):
        kind = side + 1
        if side == 0:
            face = 0.5 * (cells + pltpu.roll(cells, wide - 1, 1))
        else:
            face = 0.5 * (cells + pltpu.roll(cells, height - 1, 0))
            if halo is not None:
                face = jnp.where(row == halo * TILE + 3, pltpu.roll(face, DEEP, 0), face)
        inverse = 1.0 / face
        ratio = -field(("drag", kind), kind) * inverse
        wet = [field(("wet_" + way, step), kind) for step in range(3)]
        stores += [(fixed, (RATIO + side,), ratio), (fixed, (FIRST + side,), 0.5 * wet[2])]
        for step in range(3):
            now = field(("traj_" + way, step), kind)
            square = now * now
            root = lax.rsqrt(square + speed_floor)
            speed = (square + speed_floor) * root
            keep = 2.0 + ratio * (speed + square * root)
            deep = face
            if step > 0:
                mask = 0.5 * wet[step - 1]
                keep, deep = keep * mask, deep * mask
            stores += [
                (moving, (KEEP + side, step), keep),
                (moving, (DEPTH + side, step), deep),
                (moving, (DRAG + side, step), -now * speed * inverse),
                (moving, (VEL + side, step), now),
            ]
    for ref, index, value in stores:
        ref[index] = value


def south_of(values, tile):
    row = iota(values[tile].shape, 0)
    return jnp.where(row == 0, pltpu.roll(values[tile - 1], 1, 0), pltpu.roll(values[tile], 1, 0))


def north_of(values, tile):
    row = iota(values[tile].shape, 0)
    after = values[(tile + 1) % len(values)]
    return jnp.where(row == TILE - 1, pltpu.roll(after, TILE - 1, 0), pltpu.roll(values[tile], TILE - 1, 0))


def march(states, moving, fixed, halo, at_top):
    count = len(states[0][0])
    wide = states[0][0][0].shape[1]
    row = iota((TILE, wide), 0)
    group = range(len(states))

    def east_of(value):
        return pltpu.roll(value, wide - 1, 1)

    def west_of(value):
        return pltpu.roll(value, 1, 1)

    def fold_row(value):
        return jnp.where(at_top & (row == TILE - 1), pltpu.roll(value, DEEP, 0), 0.0)

    high = [list(state[0]) for state in states]
    flow_u, flow_v = [[] for _ in group], [[] for _ in group]
    for tile in range(count):
        here = rows_of(tile)
        first_u, first_v = fixed[FIRST, here, :], fixed[FIRST + 1, here, :]
        for one in group:
            flow_u[one].append(first_u * states[one][1][tile])
            flow_v[one].append(first_v * states[one][2][tile])
    history = []
    for step in (2, 1, 0):
        sea, turns_u, turns_v, next_u, next_v = ([[] for _ in group] for _ in range(5))
        face = [list(flows) for flows in flow_v]
        if halo is not None:
            for one in group:
                face[one][halo - 1] = flow_v[one][halo - 1] - fold_row(flow_v[one][halo])
        for tile in range(count):
            land = fixed[LAND, rows_of(tile), :]
            for one in group:
                high[one][tile] = (
                    high[one][tile]
                    + (flow_u[one][tile] - west_of(flow_u[one][tile]))
                    + (face[one][tile] - south_of(face[one], tile))
                )
                sea[one].append(land * high[one][tile])
        for tile in range(count):
            here = rows_of(tile)
            keep_u, keep_v = moving[KEEP, step, here, :], moving[KEEP + 1, step, here, :]
            deep_u, deep_v = moving[DEPTH, step, here, :], moving[DEPTH + 1, step, here, :]
            for one in group:
                turn_u = east_of(sea[one][tile]) - sea[one][tile]
                turn_v = north_of(sea[one], tile) - sea[one][tile]
                if tile == halo:
                    turn_v = jnp.where(row == 3, -pltpu.roll(turns_v[one][tile - 1], DEEP, 0), turn_v)
                turns_u[one].append(turn_u)
                turns_v[one].append(turn_v)
                next_u[one].append(keep_u * flow_u[one][tile] + deep_u * turn_u)
                next_v[one].append(keep_v * flow_v[one][tile] + deep_v * turn_v)
        history.append((step, flow_u, flow_v, turns_u, turns_v))
        flow_u, flow_v = next_u, next_v

    face_u, face_v, drags = ([[] for _ in group] for _ in range(3))
    for tile in range(count):
        here = rows_of(tile)
        sums = [[0.0] * 4 for _ in group]
        for step, steps_u, steps_v, turns_u, turns_v in history:
            for number, (index, values) in enumerate(
                ((DRAG, steps_u), (DRAG + 1, steps_v), (VEL, turns_u), (VEL + 1, turns_v))
            ):
                factor = moving[index, step, here, :]
                for one in group:
                    sums[one][number] += factor * values[one][tile]
        ratio_u, ratio_v = fixed[RATIO, here, :], fixed[RATIO + 1, here, :]
        for one in group:
            face_u[one].append(ratio_u * sums[one][0] + sums[one][2])
            face_v[one].append(ratio_v * sums[one][1] + sums[one][3])
            drags[one].append(sums[one][0] + sums[one][1])
    outs = []
    for one in group:
        totals = []
        for tile in range(count):
            total = face_u[one][tile] + west_of(face_u[one][tile]) + face_v[one][tile] + south_of(face_v[one], tile)
            if halo is not None and tile == halo - 1:
                total = total + fold_row(face_v[one][halo])
            totals.append(0.5 * total)
        outs.append((high[one], flow_u[one], flow_v[one], totals, drags[one]))
    return outs


STRIP_KEYS = tuple(
    (name, step) for name in ("traj_u", "traj_v", "wet_u", "wet_v") for step in range(3)
) + (("depth", None), ("drag", None), ("land", None))


def spread(packed):
    lane = iota(packed.shape, 1)
    arrays = [packed]
    for shift in (4 * GROUP, 2 * GROUP, GROUP):
        upper = (lane & shift) != 0
        halves = []
        for value in arrays:
            other = pltpu.roll(value, shift, 1)
            halves += [jnp.where(upper, other, value), jnp.where(upper, value, other)]
        arrays = halves
    return arrays


def shared_strips(values):
    strips = []
    for first in range(0, len(values), LANES // GROUP):
        some = values[first : first + LANES // GROUP]
        sides = [spread(packed) for packed in state_strips(some)]
        strips += [jnp.concatenate([sides[0][number], sides[1][number]], axis=1) for number in range(len(some))]
    return strips


def state_strips(values):
    lane = iota(values[0][0].shape, 1)
    sides = []
    for end in (-1, 0):
        strip = None
        for sens, pieces in enumerate(values):
            piece = pltpu.roll(pieces[end], GROUP * sens + GROUP // 2, 1)
            strip = piece if strip is None else jnp.where(lane >= GROUP * sens, piece, strip)
        sides.append(strip)
    return sides


def interior(march_now, *refs):
    held = dict(zip(NAMES, refs[:10]))
    results = refs[10:15]
    strips, strips_static, to_west, to_east = refs[15:19]
    moving, fixed = refs[19:21]
    sens_count, rows, width = held["adj_h"].shape
    count = rows // TILE

    def field(key, kind):
        name, step = key
        return (held[name][...] if held[name].ndim == 2 else held[name][step]).astype(jnp.float32)

    if not march_now:
        for number, strip in enumerate(shared_strips([lane_tiles(field(key, 0)) for key in STRIP_KEYS])):
            strips_static[number] = strip
        pack_columns(held, to_west, to_east)
        for kind in range(3):
            values = [lane_tiles(held[NAMES[kind]][sens]) for sens in range(sens_count)]
            strips[kind] = jnp.concatenate(state_strips(values), axis=1)
        return
    coefficients(field, None, moving, fixed)

    def each(turn, carry):
        first = turn * PAIR
        states = [
            tuple([held[name][first + one, rows_of(tile), :] for tile in range(count)] for name in NAMES[:3])
            for one in range(PAIR)
        ]
        for one, values in enumerate(march(states, moving, fixed, None, False)):
            for ref, tiles in zip(results, values):
                for tile in range(count):
                    ref[first + one, rows_of(tile), :] = tiles[tile]
        return carry

    lax.fori_loop(0, sens_count // PAIR, each, 0)


def waits_for_top():
    row = lax.axis_index("lat") * lax.axis_size("sub") + lax.axis_index("sub")
    return (row == lax.axis_size("lat") * lax.axis_size("sub") - 2) & (lax.axis_index("lon") == 0)


def near_and_interior(*refs):
    pack_near(*refs[:12])

    @pl.when(waits_for_top())
    def _():
        interior(True, *refs[:10], *refs[12:])


def interior_after(*refs):
    interior(False, *refs[:10], *refs[19:])

    @pl.when(jnp.logical_not(waits_for_top()))
    def _():
        interior(True, *refs[:10], *refs[19:])


def row_edges(*refs):
    held = dict(zip(NAMES, refs[:10]))
    one, two = refs[10:12]
    results = refs[17:22]
    outs = refs[22:27]
    strips, strips_static = refs[27:29]
    halo, halo_static, moving, fixed, sems = refs[29:34]
    _, at_top, _ = place()
    sens_count, rows, width = held["adj_h"].shape
    row = iota((TILE, width), 0)
    top, bottom = rows // TILE - 1, 0
    inside = (slice(None), pl.ds(TILE, rows - 2 * TILE), pl.ds(LANES, width - 2 * LANES))
    copies = [
        pltpu.make_async_copy(results[number].at[inside], outs[number].at[inside], sems.at[number])
        for number in range(5)
    ]
    for copy in copies:
        copy.start()
    for number, value in enumerate(halo_tiles(one, two, sens_count)):
        if number < 3 * sens_count:
            halo[number] = value
        else:
            halo_static[number - 3 * sens_count] = value

    def shifted_halo(value, kind):
        if kind == 1:
            return jnp.where(at_top & (row < DEEP), pltpu.roll(value, width - 1, 1), value)
        return value

    def field(key, kind):
        name, step = key
        ref = held[name] if held[name].ndim == 2 else held[name].at[step]
        if key in TILES:
            between = shifted_halo(halo_static[TILES.index(key)], kind)
        else:
            between = jnp.ones((TILE, width), jnp.float32)
        parts = [ref[rows_of(top), :].astype(jnp.float32), between, ref[rows_of(bottom), :].astype(jnp.float32)]
        return jnp.concatenate(parts, axis=0)

    coefficients(field, 1, moving, fixed)

    def each(turn, carry):
        first = turn * PAIR
        states = []
        for one in range(PAIR):
            state = []
            for kind in range(3):
                ref = held[NAMES[kind]]
                between = shifted_halo(halo[3 * (first + one) + kind], kind)
                state.append([ref[first + one, rows_of(top), :], between, ref[first + one, rows_of(bottom), :]])
            states.append(tuple(state))
        for one, values in enumerate(march(states, moving, fixed, 1, at_top)):
            for ref, tiles in zip(results, values):
                ref[first + one, rows - DEEP :, :] = tiles[0][DEEP:]
                ref[first + one, :DEEP, :] = tiles[2][:DEEP]
        return carry

    lax.fori_loop(0, sens_count // PAIR, each, 0)
    state = [
        state_strips([lane_tiles(halo[3 * sens + kind]) for sens in range(sens_count)]) for kind in range(3)
    ]
    static = shared_strips([lane_tiles(halo_static[index]) for index in range(len(TILES))])
    for kind in range(3):
        strips[kind] = jnp.concatenate(state[kind], axis=1)
    for index in range(len(TILES)):
        strips_static[index] = static[index]
    for copy in copies:
        copy.wait()


def column_edges(*refs):
    results = refs[:5]
    strips, strips_static, halo_strips, halo_strips_static, from_west_ref, from_east_ref = refs[5:11]
    outs = refs[16:21]
    ends, moving, fixed, sems = refs[21:25]
    _, at_top, _ = place()
    sens_count, rows, width = results[0].shape
    count = rows // TILE + 1
    last = count - 1
    half = GROUP // 2
    height = rows + TILE
    lane = iota((height, LANES), 1)
    within = lane & (GROUP - 1)
    row = iota((height, 2 * LANES), 0)

    copies = []
    for number in range(5):
        for side, first in enumerate((0, rows - TILE)):
            middle = (slice(None), pl.ds(first, TILE), pl.ds(LANES, width - 2 * LANES))
            copies.append(
                pltpu.make_async_copy(results[number].at[middle], outs[number].at[middle], sems.at[2 + side, number])
            )
            copies[-1].start()
    from_west, from_east = from_west_ref[...], from_east_ref[...]
    easts = spread(pltpu.roll(from_east, LANES + half - 3 * DEEP, 1))
    wests = spread(pltpu.roll(from_west, LANES + DEEP - 3 * DEEP, 1))

    def joined(own, halo_own, east, west, kind):
        own = jnp.concatenate([own, halo_own], axis=0)
        east = jnp.where(within < half, own[:, :LANES], east)
        west = jnp.where(within >= half, own[:, LANES:], west)
        value = jnp.concatenate([east, west], axis=1)
        if kind == 1:
            turned = pltpu.roll(value, 2 * LANES - 1, 1)
            value = jnp.where(at_top & (row >= rows) & (row < rows + DEEP), turned, value)
        return value

    def field(key, kind):
        name, step = key
        own = strips_static[STRIP_KEYS.index((name, None) if name == "drag" else key)]
        if key not in TILES:
            east = west = jnp.ones((height, LANES), jnp.float32)
            return joined(own, jnp.ones((TILE, 2 * LANES), jnp.float32), east, west, kind)
        east = west = jnp.zeros((height, LANES), jnp.float32)
        if key in COLUMN_SLOTS:
            slot, offset, columns = COLUMN_SLOTS[key]
            east, west = easts[slot], wests[slot]
            if offset:
                east = pltpu.roll(east, LANES - offset, 1)
            if columns + offset < DEEP:
                west = pltpu.roll(west, DEEP - columns - offset, 1)
        return joined(own, halo_strips_static[TILES.index(key)], east, west, kind)

    coefficients(field, last, moving, fixed)
    state = []
    for kind in range(3):
        east = pltpu.roll(from_east[:, :LANES], (half - DEEP * kind) % LANES, 1)
        west = pltpu.roll(from_west[:, :LANES], (DEEP - DEEP * kind) % LANES, 1)
        value = joined(strips[kind], halo_strips[kind], east, west, kind)
        state.append([value[rows_of(tile), :] for tile in range(count)])
    (values,) = march([tuple(state)], moving, fixed, last, at_top)
    lane = iota((rows, LANES), 1)
    for number in range(5):
        strip = jnp.concatenate(values[number][:last], axis=0)
        for side, first in ((0, width - LANES), (1, 0)):
            inside = lane >= LANES - DEEP if side == 0 else lane < DEEP
            part = strip[:, side * LANES : (side + 1) * LANES]
            merged = []
            for sens in range(sens_count):
                shift = (LANES - half - GROUP * sens) % LANES
                piece = pltpu.roll(part, shift, 1) if shift else part
                merged.append(jnp.where(inside, piece, results[number][sens, :, first : first + LANES]))
            for sens in range(sens_count):
                ends[side, number, sens] = merged[sens]
            copies.append(
                pltpu.make_async_copy(
                    ends.at[side, number], outs[number].at[:, :, pl.ds(first, LANES)], sems.at[side, number]
                )
            )
            copies[-1].start(priority=side)
    for copy in copies:
        copy.wait()


def on_device(traj_u, traj_v, adj_h, adj_u, adj_v, depth, drag, land, wet_u, wet_v):
    count, rows, width = adj_h.shape
    steps = traj_u.shape[0]
    args = (adj_h, adj_u, adj_v, traj_u, traj_v, wet_u, wet_v, depth, drag, land)
    in_hbm_args = tuple(pltpu.with_memory_space_constraint(arg, pltpu.HBM) for arg in args)

    in_vmem = pl.BlockSpec(memory_space=pltpu.VMEM)
    in_hbm = pl.BlockSpec(memory_space=pl.ANY)
    params = pltpu.CompilerParams(vmem_limit_bytes=VMEM_LIMIT)
    row_pack = jax.ShapeDtypeStruct((message_rows(count, width), width), jnp.float32)
    packed = pl.pallas_call(
        pack_far,
        in_specs=[in_hbm] * len(args),
        out_specs=in_vmem,
        out_shape=row_pack,
        scratch_shapes=[pltpu.VMEM(arg.shape[:-2] + (TILE, width), arg.dtype) for arg in args]
        + [pltpu.SemaphoreType.DMA((len(args),))],
        compiler_params=params,
        name="pack_far",
    )(*in_hbm_args)

    lons, lats, subs = (lax.axis_size(axis) for axis in GRID)
    total_rows = lats * subs

    def device(lon, row):
        return lon * total_rows + row

    cases = lax.axis_size("case")
    each = lons * total_rows
    route = []
    for case in range(cases):
        here = case * each
        for lon in range(lons):
            route.append((here + device(lon, 0), (case + 1) % cases * each + device(lon, 0)))
            for row in range(1, total_rows - 1, 2):
                low, high = here + device(lon, row), here + device(lon, row + 1)
                route += [(low, high), (high, low)]
            route.append((here + device(lon, total_rows - 1), here + device(lons - 1 - lon, total_rows - 1)))
    two = lax.ppermute(packed, ("case",) + GRID, route)

    def shape(*dims):
        return jax.ShapeDtypeStruct(dims, jnp.float32)

    def scratch(tiles, wide):
        return [
            pltpu.VMEM((8, steps, tiles * TILE, wide), jnp.float32),
            pltpu.VMEM((5, tiles * TILE, wide), jnp.float32),
        ]

    state = shape(*adj_h.shape)
    inner_shapes = (
        [state] * 5
        + [shape(3, rows, 2 * LANES), shape(len(STRIP_KEYS), rows, 2 * LANES)]
        + [shape(rows, LANES)] * 2
    )
    one, *first = pl.pallas_call(
        near_and_interior,
        in_specs=[in_vmem] * 10 + [in_hbm],
        out_specs=[in_vmem] * 10,
        out_shape=[shape(message_size(count, width), width)] + inner_shapes,
        scratch_shapes=scratch(rows // TILE, width),
        compiler_params=params,
        name="near_and_interior",
    )(*args, packed)
    one = lax.ppermute(one, "sub", [(core, core ^ 1) for core in range(subs)])
    first = pl.pallas_call(
        interior_after,
        in_specs=[in_vmem] * 19,
        out_specs=[in_vmem] * 9,
        out_shape=inner_shapes,
        input_output_aliases={10 + number: number for number in range(9)},
        scratch_shapes=scratch(rows // TILE, width),
        compiler_params=params,
        name="interior_after",
    )(*args, *first)
    results, strips, own_columns = first[:5], first[5:7], first[7:]

    full_pack = jax.ShapeDtypeStruct((rows + TILE, LANES), jnp.float32)
    to_west, to_east = pl.pallas_call(
        functools.partial(merge_columns, count),
        out_shape=[full_pack] * 2,
        compiler_params=params,
        name="merge_columns",
    )(one, two, *own_columns)
    from_west = lax.ppermute(to_east, "lon", [(lon, (lon + 1) % lons) for lon in range(lons)])
    from_east = lax.ppermute(to_west, "lon", [(lon, (lon - 1) % lons) for lon in range(lons)])

    second = pl.pallas_call(
        row_edges,
        in_specs=[in_vmem] * 17,
        out_specs=[in_vmem] * 5 + [in_hbm] * 5 + [in_vmem] * 2,
        out_shape=[state] * 10 + [shape(3, TILE, 2 * LANES), shape(len(TILES), TILE, 2 * LANES)],
        input_output_aliases={12 + number: number for number in range(5)},
        scratch_shapes=[
            pltpu.VMEM((3 * count, TILE, width), jnp.float32),
            pltpu.VMEM((len(TILES), TILE, width), jnp.float32),
        ]
        + scratch(3, width)
        + [pltpu.SemaphoreType.DMA((5,))],
        compiler_params=params,
        name="row_edges",
    )(*args, one, two, *results)
    results, outs, halo_strips = second[:5], second[5:10], second[10:]

    return pl.pallas_call(
        column_edges,
        in_specs=[in_vmem] * 11 + [in_hbm] * 5,
        out_specs=[in_hbm] * 5,
        out_shape=[state] * 5,
        input_output_aliases={11 + number: number for number in range(5)},
        scratch_shapes=[pltpu.VMEM((2, 5, count, rows, LANES), jnp.float32)]
        + scratch(rows // TILE + 1, 2 * LANES)
        + [pltpu.SemaphoreType.DMA((4, 5))],
        compiler_params=params,
        name="column_edges",
    )(*results, *strips, *halo_strips, from_west, from_east, *outs)


def solution(mesh):
    state = P("case", ROWS, "lon")
    fixed = P(ROWS, "lon")
    return jax.shard_map(
        on_device,
        mesh=mesh,
        in_specs=(state,) * 5 + (fixed,) * 3 + (state,) * 2,
        out_specs=(state,) * 5,
        check_vma=False,
    )
```
